32 devices in a mesh: groups: 1, cells: 8 (over z, y), ctx: 4 (over x, core), dp: 1.
Axes of the slice: x: 2, y: 2, z: 4, core: 2. Of those that a mesh axis runs over, the one named last changes fastest.
Arguments:
- cell_feats: bfloat16 [1, 32768, 128], P(('groups', 'dp'), ('cells', 'ctx')), may hold values from -8 to 8
- cell_types: int32 [1, 256], P(('groups', 'dp'), ('cells', 'ctx')), may hold values from 0 to 3
- cell_routes: int32 [1, 32768, 2], P(('groups', 'dp'), ('cells', 'ctx')), may hold values from -1 to 127, as said below
- positions: float32 [1, 3, 4096], P(('groups', 'dp'), None, ('cells', 'ctx')), may hold values from -1 to 1
- targets: float32 [1, 4, 4096], P(('groups', 'dp'), None, ('cells', 'ctx')), may hold values from -6 to 6
- type_weight: bfloat16 [4, 128, 768], replicated, may hold values from -0.5 to 0.5
- query_weight: bfloat16 [768, 768], replicated, may hold values from -0.21875 to 0.21875
- key_weight: bfloat16 [768, 768], replicated, may hold values from -0.21875 to 0.21875
- out_weight: bfloat16 [768, 4], replicated, may hold values from -0.21875 to 0.21875
- anchor_gain: float32 [768], replicated, may hold values from 0.5 to 2
- query_gain: float32 [768], replicated, may hold values from 0.5 to 2
- key_gain: float32 [768], replicated, may hold values from 0.5 to 2
Outputs:
- prediction: float32 [1, 4, 4096], P(('groups', 'dp'), None, ('cells', 'ctx'))
- grad_query: float32 [768, 768], P(('groups', 'cells'), ('ctx', 'dp'))
The draws below stay inside these ranges and needn't reach their ends.
Inputs may be any that keep to these rules, and one draw needn't show every extreme that they name: `cell_routes`: A car's cells form 8 x 4 aligned tiles of 1024 rows; tile j lies in slab j // 4 and column j % 4, and supernode s belongs to tile s // 4. An entry is -1, a supernode of its own cell's tile, or a supernode of a tile in the same column and another slab. At most 32 entries of one tile name supernodes of one other tile; in every car the tiles of some slab receive exactly 32 such entries from every other tile of their column.
All inputs are finite; a program needn't handle non-finite values.
Results may differ from the reference program's by a relative error of at most 0.013.
Values may be sent and summed in bfloat16 or wider, within the bound.
A program may use at most 64 MiB of HBM per device.

```python
import math
import jax
import jax.numpy as jnp
from jax import lax

D = 768
HEAD_DIM = 64
FEAT = 128
TYPES = 4
OUTS = 4
BLOCK = 128
RAD = 2
CAP = 32
CELL_DEV = 1024
SN_DEV = 4
Q_DEV = 128
CARS = 1
CELLS = 32768
BLOCKS = 256
SUPER = 128
QUERIES = 4096
FREQ = 128
N_CELLS = 8
N_CTX = 4


def draw_cell_feats(key, part):
    shape = (CARS, CELLS, FEAT)
    values = jax.random.normal(jax.random.fold_in(key, 1), shape, jnp.float32)
    return jnp.clip(values, -8.0, 8.0).astype(jnp.bfloat16)


def draw_cell_routes(key, part):
    block_total = N_CELLS * N_CTX
    entry_count = CELL_DEV * RAD

    def one_block(vehicle, block_id):
        block_key = jax.random.fold_in(jax.random.fold_in(key, 101), vehicle * block_total + block_id)
        slab_id = block_id // N_CTX
        column_id = block_id % N_CTX
        full_slab = jax.random.randint(jax.random.fold_in(jax.random.fold_in(key, 202), vehicle), (), 0, N_CELLS)
        peer_ids = jnp.arange(N_CELLS, dtype=jnp.int32)
        load_counts = jax.random.randint(jax.random.fold_in(block_key, 1), (N_CELLS,), CAP // 3, CAP + 1)
        load_counts = jnp.where(peer_ids == full_slab, CAP, load_counts)
        load_counts = jnp.where(peer_ids == slab_id, 0, load_counts)
        bound_ids = jnp.cumsum(load_counts)
        order_ids = jnp.arange(entry_count, dtype=jnp.int32)
        target_slab = jnp.sum((order_ids[:, None] >= bound_ids[None, :]).astype(jnp.int32), axis=1)
        is_remote = order_ids < bound_ids[-1]
        mixing = jax.random.permutation(jax.random.fold_in(block_key, 2), entry_count)
        target_slab = target_slab[mixing]
        is_remote = is_remote[mixing]
        slot_draw = jax.random.randint(jax.random.fold_in(block_key, 3), (entry_count,), 0, SN_DEV)
        empty_mask = jax.random.randint(jax.random.fold_in(block_key, 4), (entry_count,), 0, 4) == 0
        remote_id = (target_slab * N_CTX + column_id) * SN_DEV + slot_draw
        local_id = jnp.where(empty_mask, -1, block_id * SN_DEV + slot_draw)
        return jnp.where(is_remote, remote_id, local_id).reshape(CELL_DEV, RAD)

    def one_vehicle(vehicle):

        def by_block(block_id):
            return one_block(vehicle, block_id)
        return jax.vmap(by_block)(jnp.arange(block_total, dtype=jnp.int32))
    table = jax.vmap(one_vehicle)(jnp.arange(CARS, dtype=jnp.int32))
    return table.reshape(CARS, block_total * CELL_DEV, RAD).astype(jnp.int32)


def set_ends(result, stream_key, smallest, largest):
    dims = result.shape
    index_at = [jax.random.randint(jax.random.fold_in(stream_key, axis), (), 0, dims[axis]) for axis in range(len(dims))]
    result = result.at[tuple(index_at)].set(smallest)
    longest = dims.index(max(dims))
    index_at[longest] = (index_at[longest] + 1) % dims[longest]
    return result.at[tuple(index_at)].set(largest)


def shard_levels(rng, shape, shards, least, top_value):
    def one(position, parts):
        steps = jax.random.uniform(jax.random.fold_in(jax.random.fold_in(rng, 6), position), (parts,), jnp.float32, least / len(shards), top_value / len(shards))
        return jnp.repeat(jnp.exp(steps), shape[position] // parts).reshape((-1,) + (1,) * (len(shape) - position - 1))

    loudness = one(*shards[0])
    for cut in shards[1:]:
        loudness = loudness * one(*cut)
    return loudness


def scatter_about(own_key, shape, scale, reach, cuts=(), kind=jnp.bfloat16):
    loudness = shard_levels(own_key, shape, cuts, -0.22, 0.18) if cuts else 1.0
    values = jax.random.normal(own_key, shape, jnp.float32) * scale * loudness
    return jnp.minimum(jnp.maximum(values, -reach), reach).astype(kind)


def setup_inputs(seed: int = 0, part: int = 0) -> dict:
    streams_of = jax.random.split(jax.random.key(seed), 13)
    part_splits = jax.random.split(jax.random.fold_in(streams_of[12], part), 13)
    return {
        "cell_feats": draw_cell_feats(jax.random.fold_in(jax.random.fold_in(streams_of[12], part), 71), part),
        "cell_types": set_ends(jax.random.randint(part_splits[1], (CARS, BLOCKS), 0, TYPES), jax.random.fold_in(part_splits[1], 1), 0, TYPES - 1).astype(jnp.int32),
        "cell_routes": draw_cell_routes(jax.random.fold_in(jax.random.fold_in(streams_of[12], part), 71), part),
        "positions": jnp.clip(jax.random.uniform(part_splits[3], (CARS, 3, QUERIES), jnp.float32, -1.0, 1.0) * shard_levels(part_splits[3], (CARS, 3, QUERIES), ((2, 32),), -0.4, 0.0), -1.0, 1.0),
        "targets": scatter_about(part_splits[4], (CARS, OUTS, QUERIES), 1.0, 6.0, ((2, 32),), jnp.float32),
        "type_weight": scatter_about(streams_of[5], (TYPES, FEAT, D), FEAT ** -0.5, 0.5),
        "query_weight": scatter_about(streams_of[6], (D, D), D ** -0.5, 0.21875),
        "key_weight": scatter_about(streams_of[7], (D, D), D ** -0.5, 0.21875),
        "out_weight": scatter_about(streams_of[8], (D, OUTS), D ** -0.5, 0.21875),
        "anchor_gain": jnp.clip(jnp.exp(jax.random.uniform(streams_of[9], (D,), jnp.float32, math.log(0.5), math.log(2.0))), 0.5, 2.0),
        "query_gain": jnp.clip(jnp.exp(jax.random.uniform(streams_of[10], (D,), jnp.float32, math.log(0.5), math.log(2.0))), 0.5, 2.0),
        "key_gain": jnp.clip(jnp.exp(jax.random.uniform(streams_of[11], (D,), jnp.float32, math.log(0.5), math.log(2.0))), 0.5, 2.0),
    }


EPS = 1e-06

def to_bf16(values):
    return lax.optimization_barrier(values.astype(jnp.bfloat16))

def head_norm(values):
    shaped = values.reshape(values.shape[:-1] + (values.shape[-1] // HEAD_DIM, HEAD_DIM))
    inverse = lax.rsqrt(lax.optimization_barrier(jnp.mean(shaped * shaped, axis=-1, keepdims=True)) + EPS)
    return (shaped * inverse).reshape(values.shape)

def embed_positions(coords):
    freq_ids = jnp.arange(FREQ, dtype=jnp.float32)
    rate_table = math.pi * jnp.exp2(freq_ids * (6.0 / FREQ))
    angles = jnp.transpose(coords)[:, :, None] * rate_table[None, None, :]
    sin_cos = jnp.stack([jnp.sin(angles), jnp.cos(angles)], axis=2)
    return sin_cos.reshape(coords.shape[1], 6 * FREQ).astype(jnp.bfloat16)

def pool_vehicle(cell_rows, type_ids, routes, type_weight):
    block_count = CELLS // CELL_DEV
    per_block = CELL_DEV // BLOCK
    cell_rows = cell_rows.reshape(block_count, per_block, BLOCK, FEAT)
    type_ids = type_ids.reshape(block_count, per_block)
    routes = routes.reshape(block_count, CELL_DEV, RAD)

    def pool_step(running, packed):
        block_rows, block_types, block_routes = packed
        chosen = jnp.take(type_weight, block_types, axis=0).astype(jnp.float32)
        pre_act = jnp.einsum('bnf,bfd->bnd', block_rows.astype(jnp.float32), chosen)
        embedded = to_bf16(jnp.tanh(pre_act)).astype(jnp.float32).reshape(CELL_DEV, D)
        for list_slot in range(RAD):
            seg_ids = block_routes[:, list_slot]
            seg_ids = jnp.where(seg_ids < 0, SUPER, seg_ids).astype(jnp.int32)
            running = running + jax.ops.segment_sum(embedded, seg_ids, num_segments=SUPER + 1)
        return (running, None)
    running, ignored = lax.scan(pool_step, jnp.zeros((SUPER + 1, D), jnp.float32), (cell_rows, type_ids, routes))
    return running[:SUPER]

def attend_vehicle(running, coords, goals, anchors, keys, query_weight, out_weight, query_gain):
    head_count = D // HEAD_DIM
    score_scale = HEAD_DIM ** (-0.5)
    block_count = QUERIES // Q_DEV
    coords = coords.reshape(3, block_count, Q_DEV).transpose(1, 0, 2)
    goals = goals.reshape(OUTS, block_count, Q_DEV).transpose(1, 0, 2)
    key_heads = keys.astype(jnp.float32).reshape(SUPER, head_count, HEAD_DIM)
    value_heads = anchors.astype(jnp.float32).reshape(SUPER, head_count, HEAD_DIM)
    out_wide = out_weight.astype(jnp.float32)

    def query_step(carried, packed):
        block_coords, block_goals = packed
        embed = embed_positions(block_coords)
        query_lin = jnp.dot(embed, query_weight, preferred_element_type=jnp.float32)
        query_hat = to_bf16(head_norm(query_lin) * query_gain)
        query_heads = query_hat.astype(jnp.float32).reshape(Q_DEV, head_count, HEAD_DIM)
        scores = jnp.einsum('qhd,khd->hqk', query_heads, key_heads) * score_scale
        exponent = jnp.exp(scores)
        probs_f32 = exponent / lax.optimization_barrier(jnp.sum(exponent, axis=-1, keepdims=True))
        weights = to_bf16(probs_f32).astype(jnp.float32)
        attended = to_bf16(jnp.einsum('hqk,khd->qhd', weights, value_heads).reshape(Q_DEV, D))
        predicted = lax.dot_general(out_weight, attended, (((0,), (1,)), ((), ())), preferred_element_type=jnp.float32)
        residue = predicted - block_goals
        grad_attended = to_bf16(lax.dot_general(residue, out_wide, (((0,), (1,)), ((), ())), precision=lax.Precision.HIGHEST))
        grad_heads = grad_attended.astype(jnp.float32).reshape(Q_DEV, head_count, HEAD_DIM)
        grad_weights = jnp.einsum('qhd,khd->hqk', grad_heads, value_heads)
        grad_scores = probs_f32 * (grad_weights - lax.optimization_barrier(jnp.sum(probs_f32 * grad_weights, axis=-1, keepdims=True)))
        grad_scores = to_bf16(grad_scores).astype(jnp.float32)
        grad_qhat = (jnp.einsum('hqk,khd->qhd', grad_scores, key_heads) * score_scale).reshape(Q_DEV, D)
        weighted = (grad_qhat * query_gain).reshape(Q_DEV, head_count, HEAD_DIM)
        shaped = query_lin.reshape(Q_DEV, head_count, HEAD_DIM)
        inverse = lax.rsqrt(lax.optimization_barrier(jnp.mean(shaped * shaped, axis=-1, keepdims=True)) + EPS)
        unit_rows = shaped * inverse
        grad_qlin = to_bf16(((weighted - unit_rows * lax.optimization_barrier(jnp.mean(weighted * unit_rows, axis=-1, keepdims=True))) * inverse).reshape(Q_DEV, D))
        carried = carried + lax.dot_general(embed, grad_qlin, (((0,), (0,)), ((), ())), preferred_element_type=jnp.float32)
        return (carried, predicted)
    running, predicted = lax.scan(query_step, running, (coords, goals))
    return (running, predicted.transpose(1, 0, 2).reshape(OUTS, QUERIES))

def reference(cell_feats, cell_types, cell_routes, positions, targets, type_weight, query_weight, key_weight, out_weight, anchor_gain, query_gain, key_gain):
    running = jnp.zeros((D, D), jnp.float32)
    outputs = []
    for vehicle in range(CARS):
        pooled = pool_vehicle(cell_feats[vehicle], cell_types[vehicle], cell_routes[vehicle], type_weight)
        inverse = lax.rsqrt(lax.optimization_barrier(jnp.mean(pooled * pooled, axis=-1, keepdims=True)) + EPS)
        anchors = to_bf16(pooled * inverse * anchor_gain)
        keys = to_bf16(head_norm(jnp.dot(anchors, key_weight, preferred_element_type=jnp.float32)) * key_gain)
        running, predicted = attend_vehicle(running, positions[vehicle], targets[vehicle], anchors, keys, query_weight, out_weight, query_gain)
        outputs.append(predicted)
    return (jnp.stack(outputs), running)
```

```python
import functools
import math

import jax
import jax.numpy as jnp
from jax import lax
from jax.experimental import pallas as pl
from jax.experimental.pallas import tpu as pltpu
from jax.sharding import PartitionSpec as P

D = 768
HEAD_DIM = 64
SN_DEV = 4
FREQ = 128


EPS = 1e-06


def head_norm(values):
    shaped = values.reshape(values.shape[:-1] + (values.shape[-1] // HEAD_DIM, HEAD_DIM))
    inverse = lax.rsqrt(jnp.mean(shaped * shaped, axis=-1, keepdims=True) + EPS)
    return (shaped * inverse).reshape(values.shape)


def embed_positions(coords):
    freq_ids = jnp.arange(FREQ, dtype=jnp.float32)
    rate_table = math.pi * jnp.exp2(freq_ids * (6.0 / FREQ))
    angles = jnp.transpose(coords)[:, :, None] * rate_table[None, None, :]
    sin_cos = jnp.stack([jnp.sin(angles), jnp.cos(angles)], axis=2)
    return sin_cos.reshape(coords.shape[1], 6 * FREQ).astype(jnp.bfloat16)


def cell_embed(cell_rows, type_ids, type_weight):
    row_count = cell_rows.shape[0]
    per_block = row_count // type_ids.shape[0]
    shaped = cell_rows.reshape(type_ids.shape[0], per_block, cell_rows.shape[1])
    chosen = type_weight[0][None]
    for type_id in range(1, type_weight.shape[0]):
        chosen = jnp.where((type_ids == type_id)[:, None, None], type_weight[type_id][None], chosen)
    pre_act = jnp.einsum("bnf,bfd->bnd", shaped, chosen, preferred_element_type=jnp.float32)
    return jnp.tanh(pre_act).astype(jnp.bfloat16).reshape(row_count, -1)


def make_keys(anchors, key_weight, key_gain):
    key_lin = jnp.dot(anchors, key_weight, preferred_element_type=jnp.float32)
    return (head_norm(key_lin) * key_gain).astype(jnp.bfloat16)


def general_device(
    cell_feats,
    cell_types,
    cell_routes,
    positions,
    targets,
    type_weight,
    query_weight,
    key_weight,
    out_weight,
    anchor_gain,
    query_gain,
    key_gain,
):
    slab_count = lax.axis_size("cells")
    column_count = lax.axis_size("ctx")
    cell_rows = cell_feats[0]
    type_ids = cell_types[0]
    routes = cell_routes[0]
    embedded = cell_embed(cell_rows, type_ids, type_weight)
    slots = jnp.arange(slab_count * SN_DEV, dtype=jnp.int32)
    owned = (slots // SN_DEV * column_count + lax.axis_index("ctx")) * SN_DEV + slots % SN_DEV
    table = jnp.sum((routes[None, :, :] == owned[:, None, None]).astype(jnp.int32), axis=2)
    partial = jnp.dot(table.astype(jnp.bfloat16), embedded, preferred_element_type=jnp.float32)
    pooled = lax.psum_scatter(partial, "cells", scatter_dimension=0, tiled=True)
    inverse = lax.rsqrt(jnp.mean(pooled * pooled, axis=-1, keepdims=True) + EPS)
    anchors = (pooled * inverse * anchor_gain).astype(jnp.bfloat16)
    own_keys = make_keys(anchors, key_weight, key_gain)
    all_keys, all_anchors = (
        lax.all_gather(own_keys, ("cells", "ctx"), axis=0, tiled=True),
        lax.all_gather(anchors, ("cells", "ctx"), axis=0, tiled=True),
    )
    embed = embed_positions(positions[0])
    query_lin = jnp.dot(embed, query_weight, preferred_element_type=jnp.float32)
    query_hat = (head_norm(query_lin) * query_gain).astype(jnp.bfloat16)
    query_count = embed.shape[0]
    head_count = D // HEAD_DIM
    group_size = 4
    score_scale = HEAD_DIM ** (-0.5)
    query_heads = query_hat.reshape(query_count, head_count, HEAD_DIM)
    key_heads = all_keys.reshape(-1, head_count, HEAD_DIM)
    value_heads = all_anchors.reshape(-1, head_count, HEAD_DIM)
    probs_saved = []
    outputs = []
    for first_head in range(0, head_count, group_size):
        last_head = first_head + group_size
        scores = (
            jnp.einsum(
                "qhd,khd->hqk",
                query_heads[:, first_head:last_head],
                key_heads[:, first_head:last_head],
                preferred_element_type=jnp.float32,
            )
            * score_scale
        )
        exponent = jnp.exp(scores)
        probs_f32 = exponent / jnp.sum(exponent, axis=-1, keepdims=True)
        probs_saved.append(probs_f32)
        outputs.append(
            jnp.einsum(
                "hqk,khd->qhd",
                probs_f32.astype(jnp.bfloat16),
                value_heads[:, first_head:last_head],
                preferred_element_type=jnp.float32,
            )
        )
    attended = jnp.concatenate(outputs, axis=1).reshape(query_count, D).astype(jnp.bfloat16)
    predicted = lax.dot_general(
        out_weight, attended, (((0,), (1,)), ((), ())), preferred_element_type=jnp.float32
    )
    residue = predicted - targets[0]
    grad_attended = lax.dot_general(
        residue,
        out_weight.astype(jnp.float32),
        (((0,), (1,)), ((), ())),
        precision=lax.Precision.HIGHEST,
    ).astype(jnp.bfloat16)
    grad_heads = grad_attended.reshape(query_count, head_count, HEAD_DIM)
    pieces = []
    for group_index, first_head in enumerate(range(0, head_count, group_size)):
        last_head = first_head + group_size
        probs_f32 = probs_saved[group_index]
        grad_weights = jnp.einsum(
            "qhd,khd->hqk",
            grad_heads[:, first_head:last_head],
            value_heads[:, first_head:last_head],
            preferred_element_type=jnp.float32,
        )
        grad_scores = probs_f32 * (
            grad_weights - jnp.sum(probs_f32 * grad_weights, axis=-1, keepdims=True)
        )
        pieces.append(
            jnp.einsum(
                "hqk,khd->qhd",
                grad_scores.astype(jnp.bfloat16),
                key_heads[:, first_head:last_head],
                preferred_element_type=jnp.float32,
            )
            * score_scale
        )
    grad_qhat = jnp.concatenate(pieces, axis=1).reshape(query_count, D)
    weighted = (grad_qhat * query_gain).reshape(query_count, head_count, HEAD_DIM)
    shaped = query_lin.reshape(query_count, head_count, HEAD_DIM)
    norm_inverse = lax.rsqrt(jnp.mean(shaped * shaped, axis=-1, keepdims=True) + EPS)
    unit_rows = shaped * norm_inverse
    grad_qlin = (
        (
            (weighted - unit_rows * jnp.mean(weighted * unit_rows, axis=-1, keepdims=True))
            * norm_inverse
        )
        .reshape(query_count, D)
        .astype(jnp.bfloat16)
    )
    summed = lax.psum_scatter(
        lax.dot_general(
            embed, grad_qlin, (((0,), (0,)), ((), ())), preferred_element_type=jnp.float32
        ),
        "cells",
        scatter_dimension=0,
        tiled=True,
    )
    grad_query = lax.psum_scatter(summed, ("ctx", "dp"), scatter_dimension=1, tiled=True)
    return (predicted[None], grad_query)


BF = jnp.bfloat16
F32 = jnp.float32
MESH = pl.DeviceIdType.MESH
SIN_TERMS = [math.pi ** n * (-1) ** (n // 2) / math.factorial(n) for n in (1, 3, 5, 7, 9, 11, 13)]
COS_TERMS = [math.pi ** n * (-1) ** (n // 2) / math.factorial(n) for n in (0, 2, 4, 6, 8, 10, 12)]


def mm(a, b):
    return jnp.dot(a, b, preferred_element_type=F32)


def series(terms, square):
    total = jnp.full_like(square, terms[-1])
    for term in terms[-2::-1]:
        total = total * square + term
    return total


def rate_table():
    ids = lax.broadcasted_iota(jnp.int32, (FREQ, FREQ), 0)
    rates = jnp.ones((FREQ, FREQ), F32)
    for bit in range(FREQ.bit_length() - 1):
        rates = rates * jnp.where((ids & (1 << bit)) != 0, 2.0 ** (6.0 * (1 << bit) / FREQ), 1.0).astype(F32)
    return rates


def fused_kernel(
    nc,
    nx,
    feats_h,
    types_h,
    routes_h,
    pos_h,
    tgt_h,
    type_w_h,
    query_w,
    key_w,
    out_wt_h,
    anchor_g_h,
    query_g_h,
    key_g_h,
    pred_out,
    grad_out,
    feats,
    types,
    routes,
    pos,
    tgt,
    type_w,
    out_wt,
    anchor_g,
    query_g,
    key_g,
    kwin,
    qwin,
    qwin_t,
    gain_t,
    emb,
    part,
    part_in,
    anc,
    kv,
    pos_all,
    tgt_all,
    pred_part,
    pred_all,
    emb_t,
    qlin,
    probs,
    glin,
    y_send,
    y_in,
    z_send,
    z_in,
    local_sem,
    a_send,
    a_recv,
    p_send,
    p_recv,
    t_send,
    t_recv,
    b_send,
    b_recv,
    k_send,
    k_recv,
    o_send,
    o_recv,
    g_send,
    g_recv,
):
    c = lax.axis_index("cells")
    x = lax.axis_index("ctx")
    width = D // nx
    pair = 2 * width
    heads = width // HEAD_DIM
    half = D // 2
    odd = lax.rem(x, 2) == 1
    start = pl.multiple_of((x // 2) * pair, 128)
    q_dev = pos.shape[-1]

    def cells_peer(k):
        return {"cells": lax.rem(c + k, nc)}

    def ctx_peer(k):
        return {"ctx": lax.rem(x + k, nx)}

    barrier = pltpu.get_barrier_semaphore()
    for k in range(1, nc):
        pl.semaphore_signal(barrier, inc=1, device_id=cells_peer(k), device_id_type=MESH)
    for k in range(1, nx):
        pl.semaphore_signal(barrier, inc=1, device_id=ctx_peer(k), device_id_type=MESH)
    loads = [
        pltpu.make_async_copy(src, dst, local_sem.at[i])
        for i, (src, dst) in enumerate(
            (
                (types_h, types),
                (type_w_h, type_w),
                (feats_h, feats),
                (routes_h, routes),
                (pos_h, pos),
                (tgt_h, tgt),
                (query_w.at[:, pl.ds(start, pair)], qwin),
                (key_w.at[:, pl.ds(start, pair)], kwin),
                (out_wt_h, out_wt),
                (anchor_g_h, anchor_g.at[0]),
                (query_g_h, query_g.at[0]),
                (key_g_h, key_g.at[0]),
            )
        )
    ]
    for load in loads:
        load.start()

    def own(values):
        return jnp.where(odd, values[:, width:], values[:, :width])

    sent = []

    def send(src, dst, send_sem, recv_sem, peer):
        copy = pltpu.make_async_remote_copy(
            src_ref=src, dst_ref=dst, send_sem=send_sem, recv_sem=recv_sem, device_id=peer, device_id_type=MESH
        )
        copy.start()
        sent.append(copy)
        return copy

    for load in loads[:3]:
        load.wait()
    block = feats.shape[0] // types.shape[1]
    for b in range(types.shape[1]):
        pre = mm(feats[b * block : (b + 1) * block, :], type_w[types[0, b]])
        emb[b * block : (b + 1) * block, :] = jnp.tanh(pre).astype(BF)
    for load in loads[3:]:
        load.wait()
    row = lax.broadcasted_iota(jnp.int32, (nc * 8, feats.shape[0]), 0)
    label = ((row // 8) * nx + x) * SN_DEV + lax.rem(row, 4)
    table = (
        jnp.where(routes[0:1, :] == label, 1.0, 0.0) + jnp.where(routes[1:2, :] == label, 1.0, 0.0)
    ).astype(BF)
    low = mm(table, emb[:, :half])
    high = mm(table, emb[:, half:])
    mixed = jnp.where(lax.rem(lax.broadcasted_iota(jnp.int32, low.shape, 0), 8) < 4, low, high)
    for s in range(nc):
        part[s] = mixed[8 * s : 8 * s + 8, :]

    qwin_t[...] = qwin[...].T
    gain_t[...] = jnp.broadcast_to(query_g[:, pl.ds(start, pair)], (128, pair)).T
    out_rows = own(out_wt[:, pl.ds(start, pair)].astype(F32))
    out_cols = jnp.concatenate([out_rows, out_rows, out_rows, jnp.zeros_like(out_rows)], axis=0).T.astype(BF)
    key_gain = own(key_g[:, pl.ds(start, pair)])

    rates = rate_table()

    def embed_block(i):
        cols = pl.ds(pl.multiple_of(i * q_dev, 128), q_dev)
        for d in range(3):
            turns = rates * pos_all[i, d]
            whole = jnp.floor(turns + 0.5)
            rest = turns - whole
            parity = whole * 0.5
            sign = 1.0 - 4.0 * (parity - jnp.floor(parity))
            square = rest * rest
            spot = (2 * d) * FREQ
            emb_t[spot : spot + FREQ, cols] = (series(SIN_TERMS, square) * rest * sign).astype(BF)
            emb_t[spot + FREQ : spot + 2 * FREQ, cols] = (series(COS_TERMS, square) * sign).astype(BF)

    pos_all[x] = pos[...]
    tgt_all[x] = tgt[...]
    embed_block(x)

    pl.semaphore_wait(barrier, nc + nx - 2)
    a_copies = []
    for k in range(1, nc):
        a_copies.append(
            send(part.at[lax.rem(c + k, nc)], part_in.at[k], a_send.at[k], a_recv.at[k], cells_peer(k))
        )
    p_copies = []
    t_copies = []
    for k in range(1, nx):
        p_copies.append(send(pos, pos_all.at[x], p_send.at[k], p_recv.at[k], ctx_peer(k)))
        t_copies.append(send(tgt, tgt_all.at[x], t_send.at[k], t_recv.at[k], ctx_peer(k)))

    for k in range(1, nx):
        p_copies[k - 1].wait_recv()
        embed_block(lax.rem(x + nx - k, nx))

    for copy in a_copies:
        copy.wait_recv()
    pooled = part[c]
    for k in range(1, nc):
        pooled = pooled + part_in[k]
    square = pooled * pooled
    square = square + pltpu.roll(square, 4, 0)
    inverse = lax.rsqrt(jnp.sum(square, axis=1, keepdims=True) * (1.0 / D) + EPS)
    lower = lax.broadcasted_iota(jnp.int32, pooled.shape, 0) < 4
    gain = jnp.where(lower, anchor_g[:, :half], anchor_g[:, half:])
    anc[0] = (pooled * inverse * gain).astype(BF).astype(F32)
    b_copies = []
    for k in range(1, nx):
        b_copies.append(send(anc.at[0], anc.at[k], b_send.at[k], b_recv.at[k], ctx_peer(k)))

    mine = pl.ds(pl.multiple_of(lax.rem(x, 2) * width, 64), width)
    qlin[...] = mm(qwin_t[mine, :], emb_t[...])
    gains = gain_t[mine, :][:, 0:1]
    inverses = []
    hats = []
    for h in range(heads):
        rows = slice(h * HEAD_DIM, (h + 1) * HEAD_DIM)
        piece = qlin[rows, :]
        inverses.append(lax.rsqrt(jnp.mean(piece * piece, axis=0, keepdims=True) + EPS))
        hats.append((piece * inverses[h] * gains[rows, :]).astype(BF))

    for copy in b_copies:
        copy.wait_recv()
    rows_low = jnp.concatenate([anc[k, 0:4, :] for k in range(nx)], axis=0)
    rows_high = jnp.concatenate([anc[k, 4:8, :] for k in range(nx)], axis=0)
    key_lin = own(mm(rows_low.astype(BF), kwin[:half, :]) + mm(rows_high.astype(BF), kwin[half:, :]))
    values = own(jnp.where(x < nx // 2, rows_low, rows_high))
    pieces = []
    for h in range(heads):
        piece = key_lin[:, h * HEAD_DIM : (h + 1) * HEAD_DIM]
        pieces.append(piece * lax.rsqrt(jnp.mean(piece * piece, axis=1, keepdims=True) + EPS))
    keys = jnp.concatenate(pieces, axis=1) * key_gain
    kv[0] = jnp.concatenate([keys, values], axis=1).astype(BF)
    k_copies = []
    for k in range(1, nc):
        k_copies.append(send(kv.at[0], kv.at[k], k_send.at[k], k_recv.at[k], cells_peer(k)))

    for copy in k_copies:
        copy.wait_recv()
    both = jnp.concatenate([kv[k] for k in range(nc)], axis=0)
    both_t = both.T
    scale = HEAD_DIM ** (-0.5)
    count = both.shape[0]
    outs = []
    for h in range(heads):
        cols = slice(h * HEAD_DIM, (h + 1) * HEAD_DIM)
        exponent = jnp.exp(mm(both[:, cols], hats[h]) * scale)
        share = exponent * (1.0 / jnp.sum(exponent, axis=0, keepdims=True))
        probs[h] = share
        outs.append(mm(both_t[width + h * HEAD_DIM : width + (h + 1) * HEAD_DIM, :], share.astype(BF)).astype(BF))
    attended = jnp.concatenate(outs, axis=0)
    pred_part[0] = mm(out_rows.astype(BF), attended)
    o_copies = []
    for k in range(1, nx):
        o_copies.append(send(pred_part.at[0], pred_part.at[k], o_send.at[k], o_recv.at[k], ctx_peer(k)))
    for copy in t_copies:
        copy.wait_recv()
    goals = jnp.concatenate([tgt_all[i] for i in range(nx)], axis=1)
    for copy in o_copies:
        copy.wait_recv()
    predicted = pred_part[0]
    for k in range(1, nx):
        predicted = predicted + pred_part[k]
    pred_all[...] = predicted
    residue = predicted - goals
    first = residue.astype(BF).astype(F32)
    second = (residue - first).astype(BF).astype(F32)
    third = residue - first - second
    split = jnp.concatenate([first, second, third, jnp.zeros_like(third)], axis=0).astype(BF)
    grad_att = mm(out_cols, split).astype(BF)
    for h in range(heads):
        rows = slice(h * HEAD_DIM, (h + 1) * HEAD_DIM)
        share = probs[h]
        grad_w = mm(both[:, width + h * HEAD_DIM : width + (h + 1) * HEAD_DIM], grad_att[rows, :])
        inner = jnp.sum(share * grad_w, axis=0, keepdims=True)
        grad_s = (share * (grad_w - inner)).astype(BF)
        grad_q = mm(both_t[rows, :], grad_s) * scale
        weighted = grad_q * gains[rows, :]
        unit = qlin[rows, :] * inverses[h]
        shared = jnp.mean(weighted * unit, axis=0, keepdims=True)
        glin[rows, :] = ((weighted - unit * shared) * inverses[h]).astype(BF)

    glin_t = glin[...].T
    deep = D // nc
    pairs = nc // 2
    side = lax.rem(c, 2)
    place = c // 2
    order = sorted(range(1, pairs), key=lambda k: (abs(2 * k - pairs), k)) + [0]

    def terms(slab):
        rows = pl.ds(pl.multiple_of(slab * deep, 16), deep)
        full = mm(emb_t[rows, :], glin_t)
        rest = jnp.concatenate([full[: deep // 2, 128:], full[deep // 2 :, 128:]], axis=1)
        return jnp.concatenate([full[:, :128], rest], axis=0)

    far = pairs // 2
    straight = order[1:-1]

    def slab_at(k, flip):
        return lax.rem(place + k, pairs) * 2 + (1 - side if flip else side)

    def to_mate(k):
        y_send[k] = terms(slab_at(k, True)).astype(BF)
        return send(y_send.at[k], y_in.at[k], g_send.at[k], g_recv.at[k], {"cells": c + 1 - 2 * side})

    def along(k, src, dst, base, flip):
        return send(src.at[k], dst.at[k], g_send.at[base + k], g_recv.at[base + k], {"cells": slab_at(k, flip)})

    far_copy = to_mate(far)
    z_copies = []
    for k in straight:
        y_send[k] = terms(slab_at(k, True)).astype(BF)
        z_copies.append((along(k, y_send, y_in, pairs, True), y_in, k))
        z_send[k] = terms(slab_at(k, False)).astype(BF)
        z_copies.append((along(k, z_send, z_in, 2 * pairs, False), z_in, k))
    near_copy = to_mate(0)
    own_far = terms(slab_at(far, False))
    far_copy.wait_recv()
    z_send[far] = (own_far + y_in[far].astype(F32)).astype(BF)
    z_copies.append((along(far, z_send, z_in, 2 * pairs, False), z_in, far))
    total = terms(c)
    near_copy.wait_recv()
    total = total + y_in[0].astype(F32)
    pred_out[...] = pred_all[:, pl.ds(pl.multiple_of(x * q_dev, 128), q_dev)]
    for copy, landed, k in z_copies:
        copy.wait_recv()
        total = total + landed[k].astype(F32)
    grad_out[:, :128] = total[:deep]
    grad_out[: deep // 2, 128:] = total[deep:, : width - 128]
    grad_out[deep // 2 :, 128:] = total[deep:, width - 128 :]
    for copy in sent:
        copy.wait_send()


def finish(pred_in, grad_in, pred_o, grad_o):
    pred_o[...] = pred_in[...]
    grad_o[...] = grad_in[...]

def fused_device(
    nc,
    nx,
    cell_feats,
    cell_types,
    cell_routes,
    positions,
    targets,
    type_weight,
    query_weight,
    key_weight,
    out_weight,
    anchor_gain,
    query_gain,
    key_gain,
):
    width = D // nx
    cells = cell_feats.shape[1]
    q_dev = positions.shape[2]
    queries = nx * q_dev
    outs = targets.shape[1]
    deep = D // nc
    count = nc * nx * SN_DEV
    vmem = pl.BlockSpec(memory_space=pltpu.VMEM)
    dma = pltpu.SemaphoreType.DMA
    predicted, grad = pl.pallas_call(
        functools.partial(fused_kernel, nc, nx),
        out_shape=(
            pltpu.VMEM((outs, q_dev), F32),
            pltpu.VMEM((deep, width), F32),
        ),
        in_specs=[pl.BlockSpec(memory_space=pltpu.HBM)] * 12,
        out_specs=(vmem, vmem),
        scratch_shapes=[
            pltpu.VMEM((cells, cell_feats.shape[2]), BF),
            pltpu.SMEM(cell_types.shape, jnp.int32),
            pltpu.VMEM((cell_routes.shape[2], cells), jnp.int32),
            pltpu.VMEM((3, 1, q_dev), F32),
            pltpu.VMEM((outs, q_dev), F32),
            pltpu.VMEM(type_weight.shape, BF),
            pltpu.VMEM((outs, D), BF),
            pltpu.VMEM((1, D), F32),
            pltpu.VMEM((1, D), F32),
            pltpu.VMEM((1, D), F32),
            pltpu.VMEM((D, 2 * width), BF),
            pltpu.VMEM((D, 2 * width), BF),
            pltpu.VMEM((2 * width, D), BF),
            pltpu.VMEM((2 * width, 128), F32),
            pltpu.VMEM((cells, D), BF),
            pltpu.VMEM((nc, 8, D // 2), F32),
            pltpu.VMEM((nc, 8, D // 2), F32),
            pltpu.VMEM((nx, 8, D // 2), F32),
            pltpu.VMEM((nc, nx * SN_DEV, 2 * width), BF),
            pltpu.VMEM((nx, 3, 1, q_dev), F32),
            pltpu.VMEM((nx, outs, q_dev), F32),
            pltpu.VMEM((nx, outs, queries), F32),
            pltpu.VMEM((outs, queries), F32),
            pltpu.VMEM((D, queries), BF),
            pltpu.VMEM((width, queries), F32),
            pltpu.VMEM((width // HEAD_DIM, count, queries), F32),
            pltpu.VMEM((width, queries), BF),
            pltpu.VMEM((nc // 2, 3 * deep // 2, 128), BF),
            pltpu.VMEM((nc // 2, 3 * deep // 2, 128), BF),
            pltpu.VMEM((nc // 2, 3 * deep // 2, 128), BF),
            pltpu.VMEM((nc // 2, 3 * deep // 2, 128), BF),
            dma((12,)),
            dma((nc,)),
            dma((nc,)),
            dma((nx,)),
            dma((nx,)),
            dma((nx,)),
            dma((nx,)),
            dma((nx,)),
            dma((nx,)),
            dma((nc,)),
            dma((nc,)),
            dma((nx,)),
            dma((nx,)),
            dma((2 * nc,)),
            dma((2 * nc,)),
        ],
        compiler_params=pltpu.CompilerParams(
            collective_id=0, has_side_effects=True, vmem_limit_bytes=64 * 1024 * 1024 - 256 * 1024
        ),
    )(
        cell_feats[0],
        cell_types,
        cell_routes[0].T,
        positions[0].reshape(3, 1, q_dev),
        targets[0],
        type_weight,
        query_weight,
        key_weight,
        out_weight.T,
        anchor_gain,
        query_gain,
        key_gain,
    )
    predicted, grad = pl.pallas_call(
        finish,
        out_shape=(jax.ShapeDtypeStruct((outs, q_dev), F32), jax.ShapeDtypeStruct((deep, width), F32)),
        in_specs=[vmem, vmem],
        out_specs=(vmem, vmem),
        compiler_params=pltpu.CompilerParams(vmem_limit_bytes=1024 * 1024),
    )(predicted, grad)
    return (predicted[None], grad)


def solution(mesh):
    in_specs = (
        P(("groups", "dp"), ("cells", "ctx"), None),
        P(("groups", "dp"), ("cells", "ctx")),
        P(("groups", "dp"), ("cells", "ctx"), None),
        P(("groups", "dp"), None, ("cells", "ctx")),
        P(("groups", "dp"), None, ("cells", "ctx")),
        P(),
        P(),
        P(),
        P(),
        P(),
        P(),
        P(),
    )
    out_specs = (P(("groups", "dp"), None, ("cells", "ctx")), P(("groups", "cells"), ("ctx", "dp")))
    sizes = mesh.shape
    fits = sizes["groups"] == 1 and sizes["dp"] == 1 and sizes["ctx"] == 4 and D % (32 * sizes["cells"]) == 0 and sizes["cells"] % 2 == 0
    body = functools.partial(fused_device, sizes["cells"], sizes["ctx"]) if fits else general_device
    return jax.shard_map(
        body, mesh=mesh, in_specs=in_specs, out_specs=out_specs, check_vma=False
    )
```

```python
import functools
import math

import jax
import jax.numpy as jnp
from jax import lax
from jax.experimental import pallas as pl
from jax.experimental.pallas import tpu as pltpu
from jax.sharding import PartitionSpec as P

D = 768
HEAD_DIM = 64
SN_DEV = 4
FREQ = 128


EPS = 1e-06


def head_norm(values):
    shaped = values.reshape(values.shape[:-1] + (values.shape[-1] // HEAD_DIM, HEAD_DIM))
    inverse = lax.rsqrt(jnp.mean(shaped * shaped, axis=-1, keepdims=True) + EPS)
    return (shaped * inverse).reshape(values.shape)


def embed_positions(coords):
    freq_ids = jnp.arange(FREQ, dtype=jnp.float32)
    rate_table = math.pi * jnp.exp2(freq_ids * (6.0 / FREQ))
    angles = jnp.transpose(coords)[:, :, None] * rate_table[None, None, :]
    sin_cos = jnp.stack([jnp.sin(angles), jnp.cos(angles)], axis=2)
    return sin_cos.reshape(coords.shape[1], 6 * FREQ).astype(jnp.bfloat16)


def cell_embed(cell_rows, type_ids, type_weight):
    row_count = cell_rows.shape[0]
    per_block = row_count // type_ids.shape[0]
    shaped = cell_rows.reshape(type_ids.shape[0], per_block, cell_rows.shape[1])
    chosen = type_weight[0][None]
    for type_id in range(1, type_weight.shape[0]):
        chosen = jnp.where((type_ids == type_id)[:, None, None], type_weight[type_id][None], chosen)
    pre_act = jnp.einsum("bnf,bfd->bnd", shaped, chosen, preferred_element_type=jnp.float32)
    return jnp.tanh(pre_act).astype(jnp.bfloat16).reshape(row_count, -1)


def make_keys(anchors, key_weight, key_gain):
    key_lin = jnp.dot(anchors, key_weight, preferred_element_type=jnp.float32)
    return (head_norm(key_lin) * key_gain).astype(jnp.bfloat16)


def general_device(
    cell_feats,
    cell_types,
    cell_routes,
    positions,
    targets,
    type_weight,
    query_weight,
    key_weight,
    out_weight,
    anchor_gain,
    query_gain,
    key_gain,
):
    slab_count = lax.axis_size("cells")
    column_count = lax.axis_size("ctx")
    cell_rows = cell_feats[0]
    type_ids = cell_types[0]
    routes = cell_routes[0]
    embedded = cell_embed(cell_rows, type_ids, type_weight)
    slots = jnp.arange(slab_count * SN_DEV, dtype=jnp.int32)
    owned = (slots // SN_DEV * column_count + lax.axis_index("ctx")) * SN_DEV + slots % SN_DEV
    table = jnp.sum((routes[None, :, :] == owned[:, None, None]).astype(jnp.int32), axis=2)
    partial = jnp.dot(table.astype(jnp.bfloat16), embedded, preferred_element_type=jnp.float32)
    pooled = lax.psum_scatter(partial, "cells", scatter_dimension=0, tiled=True)
    inverse = lax.rsqrt(jnp.mean(pooled * pooled, axis=-1, keepdims=True) + EPS)
    anchors = (pooled * inverse * anchor_gain).astype(jnp.bfloat16)
    own_keys = make_keys(anchors, key_weight, key_gain)
    all_keys, all_anchors = (
        lax.all_gather(own_keys, ("cells", "ctx"), axis=0, tiled=True),
        lax.all_gather(anchors, ("cells", "ctx"), axis=0, tiled=True),
    )
    embed = embed_positions(positions[0])
    query_lin = jnp.dot(embed, query_weight, preferred_element_type=jnp.float32)
    query_hat = (head_norm(query_lin) * query_gain).astype(jnp.bfloat16)
    query_count = embed.shape[0]
    head_count = D // HEAD_DIM
    group_size = 4
    score_scale = HEAD_DIM ** (-0.5)
    query_heads = query_hat.reshape(query_count, head_count, HEAD_DIM)
    key_heads = all_keys.reshape(-1, head_count, HEAD_DIM)
    value_heads = all_anchors.reshape(-1, head_count, HEAD_DIM)
    probs_saved = []
    outputs = []
    for first_head in range(0, head_count, group_size):
        last_head = first_head + group_size
        scores = (
            jnp.einsum(
                "qhd,khd->hqk",
                query_heads[:, first_head:last_head],
                key_heads[:, first_head:last_head],
                preferred_element_type=jnp.float32,
            )
            * score_scale
        )
        exponent = jnp.exp(scores)
        probs_f32 = exponent / jnp.sum(exponent, axis=-1, keepdims=True)
        probs_saved.append(probs_f32)
        outputs.append(
            jnp.einsum(
                "hqk,khd->qhd",
                probs_f32.astype(jnp.bfloat16),
                value_heads[:, first_head:last_head],
                preferred_element_type=jnp.float32,
            )
        )
    attended = jnp.concatenate(outputs, axis=1).reshape(query_count, D).astype(jnp.bfloat16)
    predicted = lax.dot_general(
        out_weight, attended, (((0,), (1,)), ((), ())), preferred_element_type=jnp.float32
    )
    residue = predicted - targets[0]
    grad_attended = lax.dot_general(
        residue,
        out_weight.astype(jnp.float32),
        (((0,), (1,)), ((), ())),
        precision=lax.Precision.HIGHEST,
    ).astype(jnp.bfloat16)
    grad_heads = grad_attended.reshape(query_count, head_count, HEAD_DIM)
    pieces = []
    for group_index, first_head in enumerate(range(0, head_count, group_size)):
        last_head = first_head + group_size
        probs_f32 = probs_saved[group_index]
        grad_weights = jnp.einsum(
            "qhd,khd->hqk",
            grad_heads[:, first_head:last_head],
            value_heads[:, first_head:last_head],
            preferred_element_type=jnp.float32,
        )
        grad_scores = probs_f32 * (
            grad_weights - jnp.sum(probs_f32 * grad_weights, axis=-1, keepdims=True)
        )
        pieces.append(
            jnp.einsum(
                "hqk,khd->qhd",
                grad_scores.astype(jnp.bfloat16),
                key_heads[:, first_head:last_head],
                preferred_element_type=jnp.float32,
            )
            * score_scale
        )
    grad_qhat = jnp.concatenate(pieces, axis=1).reshape(query_count, D)
    weighted = (grad_qhat * query_gain).reshape(query_count, head_count, HEAD_DIM)
    shaped = query_lin.reshape(query_count, head_count, HEAD_DIM)
    norm_inverse = lax.rsqrt(jnp.mean(shaped * shaped, axis=-1, keepdims=True) + EPS)
    unit_rows = shaped * norm_inverse
    grad_qlin = (
        (
            (weighted - unit_rows * jnp.mean(weighted * unit_rows, axis=-1, keepdims=True))
            * norm_inverse
        )
        .reshape(query_count, D)
        .astype(jnp.bfloat16)
    )
    summed = lax.psum_scatter(
        lax.dot_general(
            embed, grad_qlin, (((0,), (0,)), ((), ())), preferred_element_type=jnp.float32
        ),
        "cells",
        scatter_dimension=0,
        tiled=True,
    )
    grad_query = lax.psum_scatter(summed, ("ctx", "dp"), scatter_dimension=1, tiled=True)
    return (predicted[None], grad_query)


BF = jnp.bfloat16
F32 = jnp.float32
MESH = pl.DeviceIdType.MESH
SIN_TERMS = [math.pi ** n * (-1) ** (n // 2) / math.factorial(n) for n in (1, 3, 5, 7, 9, 11, 13)]
COS_TERMS = [math.pi ** n * (-1) ** (n // 2) / math.factorial(n) for n in (0, 2, 4, 6, 8, 10, 12)]


def mm(a, b):
    return jnp.dot(a, b, preferred_element_type=F32)


def series(terms, square):
    total = jnp.full_like(square, terms[-1])
    for term in terms[-2::-1]:
        total = total * square + term
    return total


def rate_table():
    ids = lax.broadcasted_iota(jnp.int32, (FREQ, FREQ), 0)
    rates = jnp.ones((FREQ, FREQ), F32)
    for bit in range(FREQ.bit_length() - 1):
        rates = rates * jnp.where((ids & (1 << bit)) != 0, 2.0 ** (6.0 * (1 << bit) / FREQ), 1.0).astype(F32)
    return rates


def fused_kernel(
    feats_h,
    types_h,
    routes_h,
    pos_h,
    tgt_h,
    type_w_h,
    query_w,
    key_w_h,
    out_wt_h,
    anchor_g_h,
    query_g_h,
    key_g_h,
    pred_out,
    grad_out,
    feats,
    types,
    routes,
    pos,
    tgt,
    type_w,
    out_wt,
    anchor_g,
    query_g,
    key_g,
    key_w,
    qwin,
    qwin_t,
    gain_t,
    emb,
    part,
    part_b,
    part_in,
    w_out,
    kv_out,
    kv_in,
    pos_all,
    tgt_all,
    pred_part,
    emb_t,
    qlin,
    hats,
    probs,
    glin,
    y_send,
    y_in,
    z_send,
    z_in,
    total,
    local_sem,
    a_send,
    a_recv,
    p_send,
    p_recv,
    t_send,
    t_recv,
    k_send,
    k_recv,
    o_send,
    o_recv,
    g_send,
    g_recv,
):
    c = lax.axis_index("cells")
    x = lax.axis_index("ctx")
    z, y = c // 2, lax.rem(c, 2)
    xx, k = x // 2, lax.rem(x, 2)
    width = D // 4
    pair = 2 * width
    heads = width // HEAD_DIM
    odd = y == 1
    start = pl.multiple_of(xx * pair, 128)
    q_dev = pos.shape[-1]
    place = y * 2 + xx

    def flip(value, on):
        return 1 - value if on else value

    def far_z(m):
        return flip(z // 2, m // 2) * 2 + flip(lax.rem(z, 2), m % 2)

    def device(m, dy, dx, dk):
        return {"cells": far_z(m) * 2 + flip(y, dy), "ctx": flip(xx, dx) * 2 + flip(k, dk)}

    others = [(m, dy, dx, dk) for m in (3, 2, 1, 0) for dy in (1, 0) for dx in (1, 0) for dk in (1, 0)][:-1]

    loads = [
        pltpu.make_async_copy(src, dst, local_sem.at[i])
        for i, (src, dst) in enumerate(
            (
                (types_h, types),
                (type_w_h, type_w),
                (feats_h, feats),
                (routes_h, routes),
                (pos_h, pos),
                (tgt_h, tgt),
                (out_wt_h, out_wt),
                (anchor_g_h, anchor_g.at[0]),
                (query_g_h, query_g.at[0]),
                (key_g_h, key_g.at[0]),
                (query_w.at[:, pl.ds(start, pair)], qwin),
                (key_w_h, key_w),
            )
        )
    ]
    for load in loads[:4]:
        load.start()
    barrier = pltpu.get_barrier_semaphore()
    for spot in others:
        pl.semaphore_signal(barrier, inc=1, device_id=device(*spot), device_id_type=MESH)
    for load in loads[4:]:
        load.start()

    def own(values):
        return jnp.where(odd, values[:, width:], values[:, :width])

    def copy_to(src, dst, send_sem, recv_sem, peer):
        return pltpu.make_async_remote_copy(
            src_ref=src, dst_ref=dst, send_sem=send_sem, recv_sem=recv_sem, device_id=peer, device_id_type=MESH
        )

    for load in loads[:3]:
        load.wait()
    block = feats.shape[0] // types.shape[1]
    for b in range(types.shape[1]):
        pre = mm(feats[b * block : (b + 1) * block, :], type_w[types[0, b]])
        emb[b * block : (b + 1) * block, :] = jnp.tanh(pre).astype(BF)
    for load in loads[3:6]:
        load.wait()
    row = lax.broadcasted_iota(jnp.int32, (4 * 8, feats.shape[0]), 0)
    slab = ((row // 16) * 2 + lax.rem(row, 8) // 4) * 2 + lax.rem(row // 8, 2)
    label = (slab * 4 + x) * SN_DEV + lax.rem(row, 4)
    table = (
        jnp.where(routes[0:1, :] == label, 1.0, 0.0) + jnp.where(routes[1:2, :] == label, 1.0, 0.0)
    ).astype(BF)
    sums = mm(table, emb[...])
    for o in range(4):
        part[o] = sums[8 * o : 8 * o + 8, :]
        part_b[o] = sums[8 * o : 8 * o + 8, :].astype(BF)
    pos_all[place] = pos[...]
    tgt_all[place] = tgt[...]

    half = z // 2
    is_owner = (c >= 2) & (c < 6)
    mine = 2 + half * 2 + y

    def pool_copy(i):
        dh, dy = ((1, 1), (1, 0), (0, 1), (0, 0))[i]
        o = flip(half, dh) * 2 + flip(y, dy)
        return copy_to(
            part_b.at[o],
            part_in.at[lax.rem(c - (2 + o) + 8, 8)],
            a_send.at[i],
            a_recv.at[0],
            {"cells": 2 + o, "ctx": x},
        )

    pl.semaphore_wait(barrier, len(others))
    for i in range(3):
        pool_copy(i).start()

    @pl.when(jnp.logical_not(is_owner))
    def _():
        pool_copy(3).start()

    p_copies = []
    t_copies = []
    quad = ((1, 1), (1, 0), (0, 1))
    for i, (dy, dx) in enumerate(quad):
        p_copies.append(copy_to(pos, pos_all.at[place], p_send.at[i], p_recv.at[i], device(0, dy, dx, 0)))
        p_copies[i].start()
    for i, (dy, dx) in enumerate(quad):
        t_copies.append(copy_to(tgt, tgt_all.at[place], t_send.at[i], t_recv.at[i], device(0, dy, dx, 0)))
        t_copies[i].start()

    for load in loads[6:]:
        load.wait()
    rates = rate_table()

    def embed_block(i):
        cols = pl.ds(pl.multiple_of(i * q_dev, 128), q_dev)
        for d in range(3):
            turns = rates * pos_all[i, d]
            whole = jnp.floor(turns + 0.5)
            rest = turns - whole
            parity = whole * 0.5
            sign = 1.0 - 4.0 * (parity - jnp.floor(parity))
            square = rest * rest
            spot = (2 * d) * FREQ
            emb_t[spot : spot + FREQ, cols] = (series(SIN_TERMS, square) * rest * sign).astype(BF)
            emb_t[spot + FREQ : spot + 2 * FREQ, cols] = (series(COS_TERMS, square) * sign).astype(BF)

    embed_block(place)

    out_f = out_wt[...].astype(F32)
    out_t = jnp.concatenate([out_f, jnp.zeros_like(out_f)], axis=0).T.astype(BF)
    lane8 = lax.broadcasted_iota(jnp.int32, (8, 256), 1)
    pick = jnp.where(lax.rem(lane8, 4) == lax.broadcasted_iota(jnp.int32, (8, 256), 0), 1.0, 0.0).astype(BF)
    lane_d = lax.broadcasted_iota(jnp.int32, (D, 256), 1)
    inside = lax.rem(lane_d, 16) // 4
    head_of = (lane_d // 64) * heads + inside
    keep = (lax.broadcasted_iota(jnp.int32, (D, 256), 0) // HEAD_DIM == head_of) & (inside < heads)
    keep = keep & (lax.rem(lane_d, 64) < 48)
    w_out[...] = jnp.where(keep, mm(out_t, pick), 0.0).astype(BF)

    qwin_t[...] = qwin[...].T
    gain_t[...] = jnp.broadcast_to(query_g[:, pl.ds(start, pair)], (128, pair)).T

    for i, (dy, dx) in enumerate(quad):
        p_copies[i].wait_recv()
        embed_block(flip(y, dy) * 2 + flip(xx, dx))

    rows_mine = pl.ds(pl.multiple_of(y * width, 64), width)
    qlin[...] = mm(qwin_t[rows_mine, :], emb_t[...])
    gains = gain_t[rows_mine, :][:, 0:1]

    def norm_of(h):
        piece = qlin[h * HEAD_DIM : (h + 1) * HEAD_DIM, :]
        return lax.rsqrt(jnp.mean(piece * piece, axis=0, keepdims=True) + EPS)

    for h in range(heads):
        rows = slice(h * HEAD_DIM, (h + 1) * HEAD_DIM)
        hats[rows, :] = (qlin[rows, :] * norm_of(h) * gains[rows, :]).astype(BF)
    hats[width:, :] = jnp.zeros((256 - width, hats.shape[1]), BF)

    def key_copy(i):
        m, dy, dx, dk = others[i]
        group = flip(xx, dx) * 2 + flip(y, dy)
        return copy_to(
            kv_out.at[group],
            kv_in.at[(c - 2) * 4 + x],
            k_send.at[i],
            k_recv.at[0],
            device(m, dy, dx, dk),
        )

    @pl.when(is_owner)
    def _():
        arrived = part_in.at[pl.ds(1, 7)]
        copy_to(arrived, arrived, a_send.at[0], a_recv.at[0], {"cells": c, "ctx": x}).wait_recv()
        pooled = part[c - 2]
        for s in range(1, 8):
            pooled = pooled + part_in[s].astype(F32)
        inverse = lax.rsqrt(jnp.mean(pooled * pooled, axis=1, keepdims=True) + EPS)
        anchors = (pooled * inverse * anchor_g[...]).astype(BF)
        key_lin = mm(anchors, key_w[...])
        out_lin = mm(anchors, w_out[...])
        low = lax.broadcasted_iota(jnp.int32, (8, 128), 1) < HEAD_DIM
        pieces = []
        for j in range(D // 128):
            piece = key_lin[:, 128 * j : 128 * j + 128]
            square = piece * piece
            first = jnp.sum(jnp.where(low, square, 0.0), axis=1, keepdims=True)
            second = jnp.sum(jnp.where(low, 0.0, square), axis=1, keepdims=True)
            pieces.append(piece * lax.rsqrt(jnp.where(low, first, second) * (1.0 / HEAD_DIM) + EPS))
        keys = jnp.concatenate(pieces, axis=1) * key_g[...]
        coarse = out_lin.astype(BF).astype(F32)
        mixed = jnp.where(lax.rem(lane8, 64) // 16 == 1, out_lin - coarse, coarse)
        for g in range(4):
            kv_out[g] = jnp.concatenate(
                [keys[:, width * g : width * g + width], mixed[:, 64 * g : 64 * g + 64]], axis=1
            ).astype(BF)
        for i in range(len(others)):
            key_copy(i).start()
        kv_in[(c - 2) * 4 + x] = kv_out[xx * 2 + y]

    def keys_arrive(count):
        landed = kv_in.at[pl.ds(0, count)]
        copy_to(landed, landed, k_send.at[0], k_recv.at[0], {"cells": c, "ctx": x}).wait_recv()

    @pl.when(is_owner)
    def _():
        keys_arrive(15)

    @pl.when(jnp.logical_not(is_owner))
    def _():
        keys_arrive(16)

    both_f = jnp.concatenate([kv_in[s].astype(F32) for s in range(16)], axis=0)
    both = both_f.astype(BF)
    both_t = both.T
    scale = HEAD_DIM ** (-0.5)
    lane = lax.broadcasted_iota(jnp.int32, (both.shape[0], 128), 1)
    tile0, tile1 = both_f[:, :128], both_f[:, 128:]
    lefts = [
        jnp.where(lane < HEAD_DIM, tile0, 0.0).astype(BF),
        jnp.where(lane >= HEAD_DIM, tile0, 0.0).astype(BF),
        jnp.where(lane < HEAD_DIM, tile1, 0.0).astype(BF),
    ]
    queries = qlin.shape[1]
    out_row = lax.broadcasted_iota(jnp.int32, (16, queries), 0) // 4
    by_head = jnp.zeros((16, queries), F32)
    for h in range(heads):
        exponent = jnp.exp(mm(lefts[h], hats[(h // 2) * 128 : (h // 2) * 128 + 128, :]) * scale)
        share = exponent * (1.0 / jnp.sum(exponent, axis=0, keepdims=True))
        probs[h] = share
        outs = mm(both_t[width : width + 32, :], share.astype(BF))
        by_head = jnp.where(out_row == h, outs[:16] + outs[16:], by_head)
    pred_part[0] = by_head[0:4] + by_head[4:8] + by_head[8:12]
    o_copies = []
    for i, (dy, dx) in enumerate(quad):
        o_copies.append(
            copy_to(pred_part.at[0], pred_part.at[1 + i], o_send.at[i], o_recv.at[i], device(0, dy, dx, 0))
        )
        o_copies[i].start()

    for i in range(3):
        pool_copy(i).wait_send()

    @pl.when(jnp.logical_not(is_owner))
    def _():
        pool_copy(3).wait_send()

    @pl.when(is_owner)
    def _():
        for i in range(len(others)):
            key_copy(i).wait_send()

    for copy in p_copies + t_copies:
        copy.wait_send()
    for copy in t_copies:
        copy.wait_recv()
    goals = jnp.concatenate([tgt_all[i] for i in range(4)], axis=1)
    backs = [
        jnp.where((lane >= 64) & (lax.rem(lane, 16) // 4 == h), tile1, 0.0).astype(BF) for h in range(heads)
    ]
    for copy in o_copies:
        copy.wait_recv()
    predicted = pred_part[0] + pred_part[1] + pred_part[2] + pred_part[3]
    residue = predicted - goals
    coarse = residue.astype(BF).astype(F32)
    rest = residue - coarse
    none = jnp.zeros((64, queries), F32)
    split = jnp.concatenate([none] + [coarse] * 8 + [rest] * 8, axis=0).astype(BF)
    weighed = by_head * jnp.concatenate([residue] * 4, axis=0)
    for h in range(heads):
        rows = slice(h * HEAD_DIM, (h + 1) * HEAD_DIM)
        inner = jnp.sum(weighed[4 * h : 4 * h + 4], axis=0, keepdims=True)
        grad_s = (probs[h] * (mm(backs[h], split) - inner)).astype(BF)
        grad_q = mm(both_t[rows, :], grad_s) * scale
        weighted = grad_q * gains[rows, :]
        inverse = norm_of(h)
        unit = qlin[rows, :] * inverse
        shared = jnp.mean(weighted * unit, axis=0, keepdims=True)
        glin[rows, :] = ((weighted - unit * shared) * inverse).astype(BF)

    glin_t = glin[...].T
    deep = D // 8

    def terms(slab):
        rows = pl.ds(pl.multiple_of(slab * deep, 16), deep)
        full = mm(emb_t[rows, :], glin_t)
        rest = jnp.concatenate([full[: deep // 2, 128:], full[deep // 2 :, 128:]], axis=1)
        return jnp.concatenate([full[:, :128], rest], axis=0)

    mates = {}
    for m in (3, 2, 1, 0):
        y_send[m] = terms(far_z(m) * 2 + 1 - k).astype(BF)
        mates[m] = copy_to(y_send.at[m], y_in.at[m], g_send.at[m], g_recv.at[m], device(0, 0, 0, 1))
        mates[m].start()

    def along(m):
        peer = {"cells": far_z(m) * 2 + k, "ctx": xx * 2 + y}
        return copy_to(z_send.at[m], z_in.at[m], g_send.at[4 + m], g_recv.at[4 + m], peer)

    for m in (3, 2, 1):
        mixed = terms(far_z(m) * 2 + k)
        mates[m].wait_recv()
        z_send[m] = (mixed + y_in[m].astype(F32)).astype(BF)
        along(m).start()
    mixed = terms(z * 2 + k)
    mates[0].wait_recv()
    mixed = mixed + y_in[0].astype(F32)
    total[...] = mixed

    @pl.when(y != k)
    def _():
        z_send[0] = mixed.astype(BF)
        along(0).start()

    cols = pl.ds(pl.multiple_of(place * q_dev, 128), q_dev)
    for copy in o_copies:
        copy.wait_send()
    pred_part[0] = predicted
    pred_out[...] = pred_part[0, :, cols]
    for m in (3, 2, 1, 0):
        mates[m].wait_send()

    @pl.when(y != k)
    def _():
        along(0).wait_recv()
        total[...] = z_in[0].astype(F32)
        along(0).wait_send()

    summed = total[...]
    for m in (1, 2, 3):
        along(m).wait_recv()
        summed = summed + z_in[m].astype(F32)
    grad_out[:, :128] = summed[:deep]
    grad_out[: deep // 2, 128:] = summed[deep:, : width - 128]
    grad_out[deep // 2 :, 128:] = summed[deep:, width - 128 :]
    for m in (1, 2, 3):
        along(m).wait_send()


def finish(pred_in, grad_in, pred_o, grad_o):
    pred_o[...] = pred_in[...]
    grad_o[...] = grad_in[...]

def fused_device(
    cell_feats,
    cell_types,
    cell_routes,
    positions,
    targets,
    type_weight,
    query_weight,
    key_weight,
    out_weight,
    anchor_gain,
    query_gain,
    key_gain,
):
    width = D // 4
    cells = cell_feats.shape[1]
    q_dev = positions.shape[2]
    queries = 4 * q_dev
    outs = targets.shape[1]
    deep = D // 8
    vmem = pl.BlockSpec(memory_space=pltpu.VMEM)
    dma = pltpu.SemaphoreType.DMA
    predicted, grad = pl.pallas_call(
        fused_kernel,
        out_shape=(
            pltpu.VMEM((outs, q_dev), F32),
            pltpu.VMEM((deep, width), F32),
        ),
        in_specs=[pl.BlockSpec(memory_space=pltpu.HBM)] * 12,
        out_specs=(vmem, vmem),
        scratch_shapes=[
            pltpu.VMEM((cells, cell_feats.shape[2]), BF),
            pltpu.SMEM(cell_types.shape, jnp.int32),
            pltpu.VMEM((cell_routes.shape[2], cells), jnp.int32),
            pltpu.VMEM((3, 1, q_dev), F32),
            pltpu.VMEM((outs, q_dev), F32),
            pltpu.VMEM(type_weight.shape, BF),
            pltpu.VMEM((outs, D), BF),
            pltpu.VMEM((1, D), F32),
            pltpu.VMEM((1, D), F32),
            pltpu.VMEM((1, D), F32),
            pltpu.VMEM((D, D), BF),
            pltpu.VMEM((D, 2 * width), BF),
            pltpu.VMEM((2 * width, D), BF),
            pltpu.VMEM((2 * width, 128), F32),
            pltpu.VMEM((cells, D), BF),
            pltpu.VMEM((4, 8, D), F32),
            pltpu.VMEM((4, 8, D), BF),
            pltpu.VMEM((8, 8, D), BF),
            pltpu.VMEM((D, 256), BF),
            pltpu.VMEM((4, 8, 256), BF),
            pltpu.VMEM((16, 8, 256), BF),
            pltpu.VMEM((4, 3, 1, q_dev), F32),
            pltpu.VMEM((4, outs, q_dev), F32),
            pltpu.VMEM((4, outs, queries), F32),
            pltpu.VMEM((D, queries), BF),
            pltpu.VMEM((width, queries), F32),
            pltpu.VMEM((256, queries), BF),
            pltpu.VMEM((width // HEAD_DIM, 128, queries), F32),
            pltpu.VMEM((width, queries), BF),
            pltpu.VMEM((4, 3 * deep // 2, 128), BF),
            pltpu.VMEM((4, 3 * deep // 2, 128), BF),
            pltpu.VMEM((4, 3 * deep // 2, 128), BF),
            pltpu.VMEM((4, 3 * deep // 2, 128), BF),
            pltpu.VMEM((3 * deep // 2, 128), F32),
            dma((12,)),
            dma((4,)),
            dma((1,)),
            dma((3,)),
            dma((3,)),
            dma((3,)),
            dma((3,)),
            dma((31,)),
            dma((1,)),
            dma((3,)),
            dma((3,)),
            dma((8,)),
            dma((8,)),
        ],
        compiler_params=pltpu.CompilerParams(
            collective_id=0, has_side_effects=True, vmem_limit_bytes=64 * 1024 * 1024 - 256 * 1024
        ),
    )(
        cell_feats[0],
        cell_types,
        cell_routes[0].T,
        positions[0].reshape(3, 1, q_dev),
        targets[0],
        type_weight,
        query_weight,
        key_weight,
        out_weight.T,
        anchor_gain,
        query_gain,
        key_gain,
    )
    predicted, grad = pl.pallas_call(
        finish,
        out_shape=(jax.ShapeDtypeStruct((outs, q_dev), F32), jax.ShapeDtypeStruct((deep, width), F32)),
        in_specs=[vmem, vmem],
        out_specs=(vmem, vmem),
        compiler_params=pltpu.CompilerParams(vmem_limit_bytes=1024 * 1024),
    )(predicted, grad)
    return (predicted[None], grad)


def solution(mesh):
    in_specs = (
        P(("groups", "dp"), ("cells", "ctx"), None),
        P(("groups", "dp"), ("cells", "ctx")),
        P(("groups", "dp"), ("cells", "ctx"), None),
        P(("groups", "dp"), None, ("cells", "ctx")),
        P(("groups", "dp"), None, ("cells", "ctx")),
        P(),
        P(),
        P(),
        P(),
        P(),
        P(),
        P(),
    )
    out_specs = (P(("groups", "dp"), None, ("cells", "ctx")), P(("groups", "cells"), ("ctx", "dp")))
    sizes = mesh.shape
    fits = sizes["groups"] == 1 and sizes["dp"] == 1 and sizes["ctx"] == 4 and sizes["cells"] == 8
    body = fused_device if fits else general_device
    return jax.shard_map(
        body, mesh=mesh, in_specs=in_specs, out_specs=out_specs, check_vma=False
    )
```

```python
import functools
import math

import jax
import jax.numpy as jnp
from jax import lax
from jax.experimental import pallas as pl
from jax.experimental.pallas import tpu as pltpu
from jax.sharding import PartitionSpec as P

D = 768
HEAD_DIM = 64
SN_DEV = 4
FREQ = 128


EPS = 1e-06


def head_norm(values):
    shaped = values.reshape(values.shape[:-1] + (values.shape[-1] // HEAD_DIM, HEAD_DIM))
    inverse = lax.rsqrt(jnp.mean(shaped * shaped, axis=-1, keepdims=True) + EPS)
    return (shaped * inverse).reshape(values.shape)


def embed_positions(coords):
    freq_ids = jnp.arange(FREQ, dtype=jnp.float32)
    rate_table = math.pi * jnp.exp2(freq_ids * (6.0 / FREQ))
    angles = jnp.transpose(coords)[:, :, None] * rate_table[None, None, :]
    sin_cos = jnp.stack([jnp.sin(angles), jnp.cos(angles)], axis=2)
    return sin_cos.reshape(coords.shape[1], 6 * FREQ).astype(jnp.bfloat16)


def cell_embed(cell_rows, type_ids, type_weight):
    row_count = cell_rows.shape[0]
    per_block = row_count // type_ids.shape[0]
    shaped = cell_rows.reshape(type_ids.shape[0], per_block, cell_rows.shape[1])
    chosen = type_weight[0][None]
    for type_id in range(1, type_weight.shape[0]):
        chosen = jnp.where((type_ids == type_id)[:, None, None], type_weight[type_id][None], chosen)
    pre_act = jnp.einsum("bnf,bfd->bnd", shaped, chosen, preferred_element_type=jnp.float32)
    return jnp.tanh(pre_act).astype(jnp.bfloat16).reshape(row_count, -1)


def make_keys(anchors, key_weight, key_gain):
    key_lin = jnp.dot(anchors, key_weight, preferred_element_type=jnp.float32)
    return (head_norm(key_lin) * key_gain).astype(jnp.bfloat16)


def general_device(
    cell_feats,
    cell_types,
    cell_routes,
    positions,
    targets,
    type_weight,
    query_weight,
    key_weight,
    out_weight,
    anchor_gain,
    query_gain,
    key_gain,
):
    slab_count = lax.axis_size("cells")
    column_count = lax.axis_size("ctx")
    cell_rows = cell_feats[0]
    type_ids = cell_types[0]
    routes = cell_routes[0]
    embedded = cell_embed(cell_rows, type_ids, type_weight)
    slots = jnp.arange(slab_count * SN_DEV, dtype=jnp.int32)
    owned = (slots // SN_DEV * column_count + lax.axis_index("ctx")) * SN_DEV + slots % SN_DEV
    table = jnp.sum((routes[None, :, :] == owned[:, None, None]).astype(jnp.int32), axis=2)
    partial = jnp.dot(table.astype(jnp.bfloat16), embedded, preferred_element_type=jnp.float32)
    pooled = lax.psum_scatter(partial, "cells", scatter_dimension=0, tiled=True)
    inverse = lax.rsqrt(jnp.mean(pooled * pooled, axis=-1, keepdims=True) + EPS)
    anchors = (pooled * inverse * anchor_gain).astype(jnp.bfloat16)
    own_keys = make_keys(anchors, key_weight, key_gain)
    all_keys, all_anchors = (
        lax.all_gather(own_keys, ("cells", "ctx"), axis=0, tiled=True),
        lax.all_gather(anchors, ("cells", "ctx"), axis=0, tiled=True),
    )
    embed = embed_positions(positions[0])
    query_lin = jnp.dot(embed, query_weight, preferred_element_type=jnp.float32)
    query_hat = (head_norm(query_lin) * query_gain).astype(jnp.bfloat16)
    query_count = embed.shape[0]
    head_count = D // HEAD_DIM
    group_size = 4
    score_scale = HEAD_DIM ** (-0.5)
    query_heads = query_hat.reshape(query_count, head_count, HEAD_DIM)
    key_heads = all_keys.reshape(-1, head_count, HEAD_DIM)
    value_heads = all_anchors.reshape(-1, head_count, HEAD_DIM)
    probs_saved = []
    outputs = []
    for first_head in range(0, head_count, group_size):
        last_head = first_head + group_size
        scores = (
            jnp.einsum(
                "qhd,khd->hqk",
                query_heads[:, first_head:last_head],
                key_heads[:, first_head:last_head],
                preferred_element_type=jnp.float32,
            )
            * score_scale
        )
        exponent = jnp.exp(scores)
        probs_f32 = exponent / jnp.sum(exponent, axis=-1, keepdims=True)
        probs_saved.append(probs_f32)
        outputs.append(
            jnp.einsum(
                "hqk,khd->qhd",
                probs_f32.astype(jnp.bfloat16),
                value_heads[:, first_head:last_head],
                preferred_element_type=jnp.float32,
            )
        )
    attended = jnp.concatenate(outputs, axis=1).reshape(query_count, D).astype(jnp.bfloat16)
    predicted = lax.dot_general(
        out_weight, attended, (((0,), (1,)), ((), ())), preferred_element_type=jnp.float32
    )
    residue = predicted - targets[0]
    grad_attended = lax.dot_general(
        residue,
        out_weight.astype(jnp.float32),
        (((0,), (1,)), ((), ())),
        precision=lax.Precision.HIGHEST,
    ).astype(jnp.bfloat16)
    grad_heads = grad_attended.reshape(query_count, head_count, HEAD_DIM)
    pieces = []
    for group_index, first_head in enumerate(range(0, head_count, group_size)):
        last_head = first_head + group_size
        probs_f32 = probs_saved[group_index]
        grad_weights = jnp.einsum(
            "qhd,khd->hqk",
            grad_heads[:, first_head:last_head],
            value_heads[:, first_head:last_head],
            preferred_element_type=jnp.float32,
        )
        grad_scores = probs_f32 * (
            grad_weights - jnp.sum(probs_f32 * grad_weights, axis=-1, keepdims=True)
        )
        pieces.append(
            jnp.einsum(
                "hqk,khd->qhd",
                grad_scores.astype(jnp.bfloat16),
                key_heads[:, first_head:last_head],
                preferred_element_type=jnp.float32,
            )
            * score_scale
        )
    grad_qhat = jnp.concatenate(pieces, axis=1).reshape(query_count, D)
    weighted = (grad_qhat * query_gain).reshape(query_count, head_count, HEAD_DIM)
    shaped = query_lin.reshape(query_count, head_count, HEAD_DIM)
    norm_inverse = lax.rsqrt(jnp.mean(shaped * shaped, axis=-1, keepdims=True) + EPS)
    unit_rows = shaped * norm_inverse
    grad_qlin = (
        (
            (weighted - unit_rows * jnp.mean(weighted * unit_rows, axis=-1, keepdims=True))
            * norm_inverse
        )
        .reshape(query_count, D)
        .astype(jnp.bfloat16)
    )
    summed = lax.psum_scatter(
        lax.dot_general(
            embed, grad_qlin, (((0,), (0,)), ((), ())), preferred_element_type=jnp.float32
        ),
        "cells",
        scatter_dimension=0,
        tiled=True,
    )
    grad_query = lax.psum_scatter(summed, ("ctx", "dp"), scatter_dimension=1, tiled=True)
    return (predicted[None], grad_query)


BF = jnp.bfloat16
F32 = jnp.float32
MESH = pl.DeviceIdType.MESH
SIN_TERMS = [math.pi ** n * (-1) ** (n // 2) / math.factorial(n) for n in (1, 3, 5, 7, 9, 11, 13)]
COS_TERMS = [math.pi ** n * (-1) ** (n // 2) / math.factorial(n) for n in (0, 2, 4, 6, 8, 10, 12)]


def mm(a, b):
    return jnp.dot(a, b, preferred_element_type=F32)


def series(terms, square):
    total = jnp.full_like(square, terms[-1])
    for term in terms[-2::-1]:
        total = total * square + term
    return total


def rate_table():
    ids = lax.broadcasted_iota(jnp.int32, (FREQ, FREQ), 0)
    rates = jnp.ones((FREQ, FREQ), F32)
    for bit in range(FREQ.bit_length() - 1):
        rates = rates * jnp.where((ids & (1 << bit)) != 0, 2.0 ** (6.0 * (1 << bit) / FREQ), 1.0).astype(F32)
    return rates


def fused_kernel(
    feats_h,
    types_h,
    routes_h,
    pos_h,
    tgt_h,
    type_w_h,
    query_w,
    key_w_h,
    out_wt_h,
    anchor_g_h,
    query_g_h,
    key_g_h,
    pred_out,
    grad_out,
    feats,
    types,
    routes,
    pos,
    tgt,
    type_w,
    out_wt,
    anchor_g,
    query_g,
    key_g,
    key_w,
    qwin,
    qwin_t,
    gain_t,
    emb,
    part,
    part_b,
    part_in,
    w_out,
    kv_out,
    kv_in,
    pos_all,
    tgt_all,
    pred_part,
    emb_t,
    qlin,
    hats,
    probs,
    glin,
    y_send,
    y_in,
    z_send,
    z_in,
    total,
    local_sem,
    a_send,
    a_recv,
    p_send,
    p_recv,
    t_send,
    t_recv,
    k_send,
    k_recv,
    o_send,
    o_recv,
    g_send,
    g_recv,
    ready,
):
    c = lax.axis_index("cells")
    x = lax.axis_index("ctx")
    z, y = c // 2, lax.rem(c, 2)
    xx, k = x // 2, lax.rem(x, 2)
    width = D // 4
    pair = 2 * width
    heads = width // HEAD_DIM
    odd = y == 1
    start = pl.multiple_of(xx * pair, 128)
    q_dev = pos.shape[-1]
    place = y * 2 + xx

    def flip(value, on):
        return 1 - value if on else value

    def far_z(m):
        return flip(z // 2, m // 2) * 2 + flip(lax.rem(z, 2), m % 2)

    def device(m, dy, dx, dk):
        return {"cells": far_z(m) * 2 + flip(y, dy), "ctx": flip(xx, dx) * 2 + flip(k, dk)}

    others = [(m, dy, dx, dk) for m in (3, 2, 1, 0) for dy in (1, 0) for dx in (1, 0) for dk in (1, 0)][:-1]

    loads = [
        pltpu.make_async_copy(src, dst, local_sem.at[i])
        for i, (src, dst) in enumerate(
            (
                (types_h, types),
                (type_w_h, type_w),
                (feats_h, feats),
                (routes_h, routes),
                (pos_h, pos),
                (tgt_h, tgt),
                (out_wt_h, out_wt),
                (anchor_g_h, anchor_g.at[0]),
                (query_g_h, query_g.at[0]),
                (key_g_h, key_g.at[0]),
                (query_w.at[:, pl.ds(start, pair)], qwin),
                (key_w_h, key_w),
            )
        )
    ]
    for load in loads[:4]:
        load.start()
    barrier = pltpu.get_barrier_semaphore()
    half = z // 2
    is_owner = (c >= 2) & (c < 6)
    greeted = [(m, dy, 0, 0) for m in (1, 2) for dy in (0, 1)]
    greeted += [(0, 1, 0, 0), (0, 0, 1, 0), (0, 1, 1, 0), (0, 0, 0, 1), (0, 0, 1, 1)]

    def greet(spot):
        pl.semaphore_signal(barrier, inc=1, device_id=device(*spot), device_id_type=MESH)

    for spot in greeted:
        greet(spot)

    @pl.when(is_owner)
    def _():
        greet((3, 0, 0, 0))
        greet((3, 1, 0, 0))

    for load in loads[4:]:
        load.start()

    def own(values):
        return jnp.where(odd, values[:, width:], values[:, :width])

    def copy_to(src, dst, send_sem, recv_sem, peer):
        return pltpu.make_async_remote_copy(
            src_ref=src, dst_ref=dst, send_sem=send_sem, recv_sem=recv_sem, device_id=peer, device_id_type=MESH
        )

    for load in loads[:3]:
        load.wait()
    block = feats.shape[0] // types.shape[1]
    for b in range(types.shape[1]):
        pre = mm(feats[b * block : (b + 1) * block, :], type_w[types[0, b]])
        emb[b * block : (b + 1) * block, :] = jnp.tanh(pre).astype(BF)
    for load in loads[3:6]:
        load.wait()
    row = lax.broadcasted_iota(jnp.int32, (4 * 8, feats.shape[0]), 0)
    slab = ((row // 16) * 2 + lax.rem(row, 8) // 4) * 2 + lax.rem(row // 8, 2)
    label = (slab * 4 + x) * SN_DEV + lax.rem(row, 4)
    table = (
        jnp.where(routes[0:1, :] == label, 1.0, 0.0) + jnp.where(routes[1:2, :] == label, 1.0, 0.0)
    ).astype(BF)
    sums = mm(table, emb[...])
    for o in range(4):
        part[o] = sums[8 * o : 8 * o + 8, :]
        part_b[o] = sums[8 * o : 8 * o + 8, :].astype(BF)
    pos_all[place] = pos[...]
    tgt_all[place] = tgt[...]

    def pool_copy(i):
        dh, dy = ((1, 1), (1, 0), (0, 1), (0, 0))[i]
        o = flip(half, dh) * 2 + flip(y, dy)
        return copy_to(
            part_b.at[o],
            part_in.at[lax.rem(c - (2 + o) + 8, 8)],
            a_send.at[i],
            a_recv.at[0],
            {"cells": 2 + o, "ctx": x},
        )

    pl.semaphore_wait(barrier, len(greeted) + jnp.where(is_owner, 2, 0))
    for i in range(3):
        pool_copy(i).start()

    @pl.when(jnp.logical_not(is_owner))
    def _():
        pool_copy(3).start()

    @pl.when(is_owner)
    def _():
        for dx, dk in ((1, 1), (1, 0), (0, 1)):
            pl.semaphore_signal(ready, inc=1, device_id=device(0, 0, dx, dk), device_id_type=MESH)

    p_copies = []
    t_copies = []
    quad = ((1, 1), (1, 0), (0, 1))
    for i, (dy, dx) in enumerate(quad):
        p_copies.append(copy_to(pos, pos_all.at[place], p_send.at[i], p_recv.at[i], device(0, dy, dx, 0)))
        p_copies[i].start()
    for i, (dy, dx) in enumerate(quad):
        t_copies.append(copy_to(tgt, tgt_all.at[place], t_send.at[i], t_recv.at[i], device(0, dy, dx, 0)))
        t_copies[i].start()

    for load in loads[6:]:
        load.wait()
    rates = rate_table()

    def embed_block(i):
        cols = pl.ds(pl.multiple_of(i * q_dev, 128), q_dev)
        for d in range(3):
            turns = rates * pos_all[i, d]
            whole = jnp.floor(turns + 0.5)
            rest = turns - whole
            parity = whole * 0.5
            sign = 1.0 - 4.0 * (parity - jnp.floor(parity))
            square = rest * rest
            spot = (2 * d) * FREQ
            emb_t[spot : spot + FREQ, cols] = (series(SIN_TERMS, square) * rest * sign).astype(BF)
            emb_t[spot + FREQ : spot + 2 * FREQ, cols] = (series(COS_TERMS, square) * sign).astype(BF)

    out_f = out_wt[...].astype(F32)
    out_t = jnp.concatenate([out_f, jnp.zeros_like(out_f)], axis=0).T.astype(BF)
    lane8 = lax.broadcasted_iota(jnp.int32, (8, 256), 1)
    pick = jnp.where(lax.rem(lane8, 4) == lax.broadcasted_iota(jnp.int32, (8, 256), 0), 1.0, 0.0).astype(BF)
    lane_d = lax.broadcasted_iota(jnp.int32, (D, 256), 1)
    inside = lax.rem(lane_d, 16) // 4
    head_of = (lane_d // 64) * heads + inside
    keep = (lax.broadcasted_iota(jnp.int32, (D, 256), 0) // HEAD_DIM == head_of) & (inside < heads)
    keep = keep & (lax.rem(lane_d, 64) < 48)
    w_out[...] = jnp.where(keep, mm(out_t, pick), 0.0).astype(BF)

    def key_copy(i):
        m, dy, dx, dk = others[i]
        group = flip(xx, dx) * 2 + flip(y, dy)
        return copy_to(
            kv_out.at[group],
            kv_in.at[(c - 2) * 4 + x],
            k_send.at[i],
            k_recv.at[0],
            device(m, dy, dx, dk),
        )

    @pl.when(is_owner)
    def _():
        arrived = part_in.at[pl.ds(1, 7)]
        copy_to(arrived, arrived, a_send.at[0], a_recv.at[0], {"cells": c, "ctx": x}).wait_recv()
        pooled = part[c - 2]
        for s in range(1, 8):
            pooled = pooled + part_in[s].astype(F32)
        inverse = lax.rsqrt(jnp.mean(pooled * pooled, axis=1, keepdims=True) + EPS)
        anchors = (pooled * inverse * anchor_g[...]).astype(BF)
        key_lin = mm(anchors, key_w[...])
        out_lin = mm(anchors, w_out[...])
        low = lax.broadcasted_iota(jnp.int32, (8, 128), 1) < HEAD_DIM
        pieces = []
        for j in range(D // 128):
            piece = key_lin[:, 128 * j : 128 * j + 128]
            square = piece * piece
            first = jnp.sum(jnp.where(low, square, 0.0), axis=1, keepdims=True)
            second = jnp.sum(jnp.where(low, 0.0, square), axis=1, keepdims=True)
            pieces.append(piece * lax.rsqrt(jnp.where(low, first, second) * (1.0 / HEAD_DIM) + EPS))
        keys = jnp.concatenate(pieces, axis=1) * key_g[...]
        coarse = out_lin.astype(BF).astype(F32)
        mixed = jnp.where(lax.rem(lane8, 64) // 16 == 1, out_lin - coarse, coarse)
        for g in range(4):
            kv_out[g] = jnp.concatenate(
                [keys[:, width * g : width * g + width], mixed[:, 64 * g : 64 * g + 64]], axis=1
            ).astype(BF)
        pl.semaphore_wait(ready, 3)
        for i in range(len(others)):
            key_copy(i).start()
        kv_in[(c - 2) * 4 + x] = kv_out[xx * 2 + y]

    embed_block(place)
    qwin_t[...] = qwin[...].T
    gain_t[...] = jnp.broadcast_to(query_g[:, pl.ds(start, pair)], (128, pair)).T

    for i, (dy, dx) in enumerate(quad):
        p_copies[i].wait_recv()
        embed_block(flip(y, dy) * 2 + flip(xx, dx))

    rows_mine = pl.ds(pl.multiple_of(y * width, 64), width)
    qlin[...] = mm(qwin_t[rows_mine, :], emb_t[...])
    gains = gain_t[rows_mine, :][:, 0:1]

    def norm_of(h):
        piece = qlin[h * HEAD_DIM : (h + 1) * HEAD_DIM, :]
        return lax.rsqrt(jnp.mean(piece * piece, axis=0, keepdims=True) + EPS)

    for h in range(heads):
        rows = slice(h * HEAD_DIM, (h + 1) * HEAD_DIM)
        hats[rows, :] = (qlin[rows, :] * norm_of(h) * gains[rows, :]).astype(BF)
    hats[width:, :] = jnp.zeros((256 - width, hats.shape[1]), BF)

    def keys_arrive(count):
        landed = kv_in.at[pl.ds(0, count)]
        copy_to(landed, landed, k_send.at[0], k_recv.at[0], {"cells": c, "ctx": x}).wait_recv()

    @pl.when(is_owner)
    def _():
        keys_arrive(15)

    @pl.when(jnp.logical_not(is_owner))
    def _():
        keys_arrive(16)

    both_f = jnp.concatenate([kv_in[s].astype(F32) for s in range(16)], axis=0)
    both = both_f.astype(BF)
    both_t = both.T
    scale = HEAD_DIM ** (-0.5)
    lane = lax.broadcasted_iota(jnp.int32, (both.shape[0], 128), 1)
    tile0, tile1 = both_f[:, :128], both_f[:, 128:]
    lefts = [
        jnp.where(lane < HEAD_DIM, tile0, 0.0).astype(BF),
        jnp.where(lane >= HEAD_DIM, tile0, 0.0).astype(BF),
        jnp.where(lane < HEAD_DIM, tile1, 0.0).astype(BF),
    ]
    queries = qlin.shape[1]
    out_row = lax.broadcasted_iota(jnp.int32, (16, queries), 0) // 4
    by_head = jnp.zeros((16, queries), F32)
    for h in range(heads):
        exponent = jnp.exp(mm(lefts[h], hats[(h // 2) * 128 : (h // 2) * 128 + 128, :]) * scale)
        share = exponent * (1.0 / jnp.sum(exponent, axis=0, keepdims=True))
        probs[h] = share
        outs = mm(both_t[width : width + 32, :], share.astype(BF))
        by_head = jnp.where(out_row == h, outs[:16] + outs[16:], by_head)
    pred_part[0] = by_head[0:4] + by_head[4:8] + by_head[8:12]
    o_copies = []
    for i, (dy, dx) in enumerate(quad):
        o_copies.append(
            copy_to(pred_part.at[0], pred_part.at[1 + i], o_send.at[i], o_recv.at[i], device(0, dy, dx, 0))
        )
        o_copies[i].start()

    for i in range(3):
        pool_copy(i).wait_send()

    @pl.when(jnp.logical_not(is_owner))
    def _():
        pool_copy(3).wait_send()

    @pl.when(is_owner)
    def _():
        for i in range(len(others)):
            key_copy(i).wait_send()

    for copy in p_copies + t_copies:
        copy.wait_send()
    for copy in t_copies:
        copy.wait_recv()
    goals = jnp.concatenate([tgt_all[i] for i in range(4)], axis=1)
    backs = [
        jnp.where((lane >= 64) & (lax.rem(lane, 16) // 4 == h), tile1, 0.0).astype(BF) for h in range(heads)
    ]
    for copy in o_copies:
        copy.wait_recv()
    predicted = pred_part[0] + pred_part[1] + pred_part[2] + pred_part[3]
    residue = predicted - goals
    coarse = residue.astype(BF).astype(F32)
    rest = residue - coarse
    none = jnp.zeros((64, queries), F32)
    split = jnp.concatenate([none] + [coarse] * 8 + [rest] * 8, axis=0).astype(BF)
    weighed = by_head * jnp.concatenate([residue] * 4, axis=0)
    for h in range(heads):
        rows = slice(h * HEAD_DIM, (h + 1) * HEAD_DIM)
        inner = jnp.sum(weighed[4 * h : 4 * h + 4], axis=0, keepdims=True)
        grad_s = (probs[h] * (mm(backs[h], split) - inner)).astype(BF)
        grad_q = mm(both_t[rows, :], grad_s) * scale
        weighted = grad_q * gains[rows, :]
        inverse = norm_of(h)
        unit = qlin[rows, :] * inverse
        shared = jnp.mean(weighted * unit, axis=0, keepdims=True)
        glin[rows, :] = ((weighted - unit * shared) * inverse).astype(BF)

    glin_t = glin[...].T
    deep = D // 8

    def terms(slab):
        rows = pl.ds(pl.multiple_of(slab * deep, 16), deep)
        full = mm(emb_t[rows, :], glin_t)
        rest = jnp.concatenate([full[: deep // 2, 128:], full[deep // 2 :, 128:]], axis=1)
        return jnp.concatenate([full[:, :128], rest], axis=0)

    mates = {}
    for m in (3, 2, 1, 0):
        y_send[m] = terms(far_z(m) * 2 + 1 - k).astype(BF)
        mates[m] = copy_to(y_send.at[m], y_in.at[m], g_send.at[m], g_recv.at[m], device(0, 0, 0, 1))
        mates[m].start()

    def along(m):
        peer = {"cells": far_z(m) * 2 + k, "ctx": xx * 2 + y}
        return copy_to(z_send.at[m], z_in.at[m], g_send.at[4 + m], g_recv.at[4 + m], peer)

    for m in (3, 2, 1):
        mixed = terms(far_z(m) * 2 + k)
        mates[m].wait_recv()
        z_send[m] = (mixed + y_in[m].astype(F32)).astype(BF)
        along(m).start()
    mixed = terms(z * 2 + k)
    mates[0].wait_recv()
    mixed = mixed + y_in[0].astype(F32)
    total[...] = mixed

    @pl.when(y != k)
    def _():
        z_send[0] = mixed.astype(BF)
        along(0).start()

    cols = pl.ds(pl.multiple_of(place * q_dev, 128), q_dev)
    for copy in o_copies:
        copy.wait_send()
    pred_part[0] = predicted
    pred_out[...] = pred_part[0, :, cols]
    for m in (3, 2, 1, 0):
        mates[m].wait_send()

    @pl.when(y != k)
    def _():
        along(0).wait_recv()
        total[...] = z_in[0].astype(F32)
        along(0).wait_send()

    summed = total[...]
    for m in (1, 2, 3):
        along(m).wait_recv()
        summed = summed + z_in[m].astype(F32)
    grad_out[:, :128] = summed[:deep]
    grad_out[: deep // 2, 128:] = summed[deep:, : width - 128]
    grad_out[deep // 2 :, 128:] = summed[deep:, width - 128 :]
    for m in (1, 2, 3):
        along(m).wait_send()


def finish(pred_in, grad_in, pred_o, grad_o):
    pred_o[...] = pred_in[...]
    grad_o[...] = grad_in[...]

def fused_device(
    cell_feats,
    cell_types,
    cell_routes,
    positions,
    targets,
    type_weight,
    query_weight,
    key_weight,
    out_weight,
    anchor_gain,
    query_gain,
    key_gain,
):
    width = D // 4
    cells = cell_feats.shape[1]
    q_dev = positions.shape[2]
    queries = 4 * q_dev
    outs = targets.shape[1]
    deep = D // 8
    vmem = pl.BlockSpec(memory_space=pltpu.VMEM)
    dma = pltpu.SemaphoreType.DMA
    predicted, grad = pl.pallas_call(
        fused_kernel,
        out_shape=(
            pltpu.VMEM((outs, q_dev), F32),
            pltpu.VMEM((deep, width), F32),
        ),
        in_specs=[pl.BlockSpec(memory_space=pltpu.HBM)] * 12,
        out_specs=(vmem, vmem),
        scratch_shapes=[
            pltpu.VMEM((cells, cell_feats.shape[2]), BF),
            pltpu.SMEM(cell_types.shape, jnp.int32),
            pltpu.VMEM((cell_routes.shape[2], cells), jnp.int32),
            pltpu.VMEM((3, 1, q_dev), F32),
            pltpu.VMEM((outs, q_dev), F32),
            pltpu.VMEM(type_weight.shape, BF),
            pltpu.VMEM((outs, D), BF),
            pltpu.VMEM((1, D), F32),
            pltpu.VMEM((1, D), F32),
            pltpu.VMEM((1, D), F32),
            pltpu.VMEM((D, D), BF),
            pltpu.VMEM((D, 2 * width), BF),
            pltpu.VMEM((2 * width, D), BF),
            pltpu.VMEM((2 * width, 128), F32),
            pltpu.VMEM((cells, D), BF),
            pltpu.VMEM((4, 8, D), F32),
            pltpu.VMEM((4, 8, D), BF),
            pltpu.VMEM((8, 8, D), BF),
            pltpu.VMEM((D, 256), BF),
            pltpu.VMEM((4, 8, 256), BF),
            pltpu.VMEM((16, 8, 256), BF),
            pltpu.VMEM((4, 3, 1, q_dev), F32),
            pltpu.VMEM((4, outs, q_dev), F32),
            pltpu.VMEM((4, outs, queries), F32),
            pltpu.VMEM((D, queries), BF),
            pltpu.VMEM((width, queries), F32),
            pltpu.VMEM((256, queries), BF),
            pltpu.VMEM((width // HEAD_DIM, 128, queries), F32),
            pltpu.VMEM((width, queries), BF),
            pltpu.VMEM((4, 3 * deep // 2, 128), BF),
            pltpu.VMEM((4, 3 * deep // 2, 128), BF),
            pltpu.VMEM((4, 3 * deep // 2, 128), BF),
            pltpu.VMEM((4, 3 * deep // 2, 128), BF),
            pltpu.VMEM((3 * deep // 2, 128), F32),
            dma((12,)),
            dma((4,)),
            dma((1,)),
            dma((3,)),
            dma((3,)),
            dma((3,)),
            dma((3,)),
            dma((31,)),
            dma((1,)),
            dma((3,)),
            dma((3,)),
            dma((8,)),
            dma((8,)),
            pltpu.SemaphoreType.REGULAR,
        ],
        compiler_params=pltpu.CompilerParams(
            collective_id=0, has_side_effects=True, vmem_limit_bytes=64 * 1024 * 1024 - 256 * 1024
        ),
    )(
        cell_feats[0],
        cell_types,
        cell_routes[0].T,
        positions[0].reshape(3, 1, q_dev),
        targets[0],
        type_weight,
        query_weight,
        key_weight,
        out_weight.T,
        anchor_gain,
        query_gain,
        key_gain,
    )
    predicted, grad = pl.pallas_call(
        finish,
        out_shape=(jax.ShapeDtypeStruct((outs, q_dev), F32), jax.ShapeDtypeStruct((deep, width), F32)),
        in_specs=[vmem, vmem],
        out_specs=(vmem, vmem),
        compiler_params=pltpu.CompilerParams(vmem_limit_bytes=1024 * 1024),
    )(predicted, grad)
    return (predicted[None], grad)


def solution(mesh):
    in_specs = (
        P(("groups", "dp"), ("cells", "ctx"), None),
        P(("groups", "dp"), ("cells", "ctx")),
        P(("groups", "dp"), ("cells", "ctx"), None),
        P(("groups", "dp"), None, ("cells", "ctx")),
        P(("groups", "dp"), None, ("cells", "ctx")),
        P(),
        P(),
        P(),
        P(),
        P(),
        P(),
        P(),
    )
    out_specs = (P(("groups", "dp"), None, ("cells", "ctx")), P(("groups", "cells"), ("ctx", "dp")))
    sizes = mesh.shape
    fits = sizes["groups"] == 1 and sizes["dp"] == 1 and sizes["ctx"] == 4 and sizes["cells"] == 8
    body = fused_device if fits else general_device
    return jax.shard_map(
        body, mesh=mesh, in_specs=in_specs, out_specs=out_specs, check_vma=False
    )
```

```python
import functools
import math

import jax
import jax.numpy as jnp
from jax import lax
from jax.experimental import pallas as pl
from jax.experimental.pallas import tpu as pltpu
from jax.sharding import PartitionSpec as P

D = 768
HEAD_DIM = 64
SN_DEV = 4
FREQ = 128


EPS = 1e-06


def head_norm(values):
    shaped = values.reshape(values.shape[:-1] + (values.shape[-1] // HEAD_DIM, HEAD_DIM))
    inverse = lax.rsqrt(jnp.mean(shaped * shaped, axis=-1, keepdims=True) + EPS)
    return (shaped * inverse).reshape(values.shape)


def embed_positions(coords):
    freq_ids = jnp.arange(FREQ, dtype=jnp.float32)
    rate_table = math.pi * jnp.exp2(freq_ids * (6.0 / FREQ))
    angles = jnp.transpose(coords)[:, :, None] * rate_table[None, None, :]
    sin_cos = jnp.stack([jnp.sin(angles), jnp.cos(angles)], axis=2)
    return sin_cos.reshape(coords.shape[1], 6 * FREQ).astype(jnp.bfloat16)


def cell_embed(cell_rows, type_ids, type_weight):
    row_count = cell_rows.shape[0]
    per_block = row_count // type_ids.shape[0]
    shaped = cell_rows.reshape(type_ids.shape[0], per_block, cell_rows.shape[1])
    chosen = type_weight[0][None]
    for type_id in range(1, type_weight.shape[0]):
        chosen = jnp.where((type_ids == type_id)[:, None, None], type_weight[type_id][None], chosen)
    pre_act = jnp.einsum("bnf,bfd->bnd", shaped, chosen, preferred_element_type=jnp.float32)
    return jnp.tanh(pre_act).astype(jnp.bfloat16).reshape(row_count, -1)


def make_keys(anchors, key_weight, key_gain):
    key_lin = jnp.dot(anchors, key_weight, preferred_element_type=jnp.float32)
    return (head_norm(key_lin) * key_gain).astype(jnp.bfloat16)


def general_device(
    cell_feats,
    cell_types,
    cell_routes,
    positions,
    targets,
    type_weight,
    query_weight,
    key_weight,
    out_weight,
    anchor_gain,
    query_gain,
    key_gain,
):
    slab_count = lax.axis_size("cells")
    column_count = lax.axis_size("ctx")
    cell_rows = cell_feats[0]
    type_ids = cell_types[0]
    routes = cell_routes[0]
    embedded = cell_embed(cell_rows, type_ids, type_weight)
    slots = jnp.arange(slab_count * SN_DEV, dtype=jnp.int32)
    owned = (slots // SN_DEV * column_count + lax.axis_index("ctx")) * SN_DEV + slots % SN_DEV
    table = jnp.sum((routes[None, :, :] == owned[:, None, None]).astype(jnp.int32), axis=2)
    partial = jnp.dot(table.astype(jnp.bfloat16), embedded, preferred_element_type=jnp.float32)
    pooled = lax.psum_scatter(partial, "cells", scatter_dimension=0, tiled=True)
    inverse = lax.rsqrt(jnp.mean(pooled * pooled, axis=-1, keepdims=True) + EPS)
    anchors = (pooled * inverse * anchor_gain).astype(jnp.bfloat16)
    own_keys = make_keys(anchors, key_weight, key_gain)
    all_keys, all_anchors = (
        lax.all_gather(own_keys, ("cells", "ctx"), axis=0, tiled=True),
        lax.all_gather(anchors, ("cells", "ctx"), axis=0, tiled=True),
    )
    embed = embed_positions(positions[0])
    query_lin = jnp.dot(embed, query_weight, preferred_element_type=jnp.float32)
    query_hat = (head_norm(query_lin) * query_gain).astype(jnp.bfloat16)
    query_count = embed.shape[0]
    head_count = D // HEAD_DIM
    group_size = 4
    score_scale = HEAD_DIM ** (-0.5)
    query_heads = query_hat.reshape(query_count, head_count, HEAD_DIM)
    key_heads = all_keys.reshape(-1, head_count, HEAD_DIM)
    value_heads = all_anchors.reshape(-1, head_count, HEAD_DIM)
    probs_saved = []
    outputs = []
    for first_head in range(0, head_count, group_size):
        last_head = first_head + group_size
        scores = (
            jnp.einsum(
                "qhd,khd->hqk",
                query_heads[:, first_head:last_head],
                key_heads[:, first_head:last_head],
                preferred_element_type=jnp.float32,
            )
            * score_scale
        )
        exponent = jnp.exp(scores)
        probs_f32 = exponent / jnp.sum(exponent, axis=-1, keepdims=True)
        probs_saved.append(probs_f32)
        outputs.append(
            jnp.einsum(
                "hqk,khd->qhd",
                probs_f32.astype(jnp.bfloat16),
                value_heads[:, first_head:last_head],
                preferred_element_type=jnp.float32,
            )
        )
    attended = jnp.concatenate(outputs, axis=1).reshape(query_count, D).astype(jnp.bfloat16)
    predicted = lax.dot_general(
        out_weight, attended, (((0,), (1,)), ((), ())), preferred_element_type=jnp.float32
    )
    residue = predicted - targets[0]
    grad_attended = lax.dot_general(
        residue,
        out_weight.astype(jnp.float32),
        (((0,), (1,)), ((), ())),
        precision=lax.Precision.HIGHEST,
    ).astype(jnp.bfloat16)
    grad_heads = grad_attended.reshape(query_count, head_count, HEAD_DIM)
    pieces = []
    for group_index, first_head in enumerate(range(0, head_count, group_size)):
        last_head = first_head + group_size
        probs_f32 = probs_saved[group_index]
        grad_weights = jnp.einsum(
            "qhd,khd->hqk",
            grad_heads[:, first_head:last_head],
            value_heads[:, first_head:last_head],
            preferred_element_type=jnp.float32,
        )
        grad_scores = probs_f32 * (
            grad_weights - jnp.sum(probs_f32 * grad_weights, axis=-1, keepdims=True)
        )
        pieces.append(
            jnp.einsum(
                "hqk,khd->qhd",
                grad_scores.astype(jnp.bfloat16),
                key_heads[:, first_head:last_head],
                preferred_element_type=jnp.float32,
            )
            * score_scale
        )
    grad_qhat = jnp.concatenate(pieces, axis=1).reshape(query_count, D)
    weighted = (grad_qhat * query_gain).reshape(query_count, head_count, HEAD_DIM)
    shaped = query_lin.reshape(query_count, head_count, HEAD_DIM)
    norm_inverse = lax.rsqrt(jnp.mean(shaped * shaped, axis=-1, keepdims=True) + EPS)
    unit_rows = shaped * norm_inverse
    grad_qlin = (
        (
            (weighted - unit_rows * jnp.mean(weighted * unit_rows, axis=-1, keepdims=True))
            * norm_inverse
        )
        .reshape(query_count, D)
        .astype(jnp.bfloat16)
    )
    summed = lax.psum_scatter(
        lax.dot_general(
            embed, grad_qlin, (((0,), (0,)), ((), ())), preferred_element_type=jnp.float32
        ),
        "cells",
        scatter_dimension=0,
        tiled=True,
    )
    grad_query = lax.psum_scatter(summed, ("ctx", "dp"), scatter_dimension=1, tiled=True)
    return (predicted[None], grad_query)


BF = jnp.bfloat16
F32 = jnp.float32
MESH = pl.DeviceIdType.MESH
SIN_TERMS = [math.pi ** n * (-1) ** (n // 2) / math.factorial(n) for n in (1, 3, 5, 7, 9, 11, 13)]
COS_TERMS = [math.pi ** n * (-1) ** (n // 2) / math.factorial(n) for n in (0, 2, 4, 6, 8, 10, 12)]


def mm(a, b):
    return jnp.dot(a, b, preferred_element_type=F32)


def series(terms, square):
    total = jnp.full_like(square, terms[-1])
    for term in terms[-2::-1]:
        total = total * square + term
    return total


def rate_table():
    ids = lax.broadcasted_iota(jnp.int32, (FREQ, FREQ), 0)
    rates = jnp.ones((FREQ, FREQ), F32)
    for bit in range(FREQ.bit_length() - 1):
        rates = rates * jnp.where((ids & (1 << bit)) != 0, 2.0 ** (6.0 * (1 << bit) / FREQ), 1.0).astype(F32)
    return rates


def fused_kernel(
    feats_h,
    types_h,
    routes_h,
    pos_h,
    tgt_h,
    type_w_h,
    query_w,
    key_w_h,
    out_wt_h,
    anchor_g_h,
    query_g_h,
    key_g_h,
    pred_out,
    grad_out,
    feats,
    types,
    routes,
    pos,
    tgt,
    type_w,
    out_wt,
    anchor_g,
    query_g,
    key_g,
    key_w,
    qwin,
    qwin_t,
    gain_t,
    emb,
    part,
    part_b,
    part_in,
    w_out,
    kv_out,
    kv_in,
    both_all,
    pred_part,
    emb_t,
    qlin,
    hats,
    probs,
    glin,
    y_send,
    y_in,
    z_send,
    z_in,
    total,
    local_sem,
    a_send,
    a_recv,
    p_send,
    p_recv,
    k_send,
    k_recv,
    o_send,
    o_recv,
    g_send,
    g_recv,
    ready,
):
    c = lax.axis_index("cells")
    x = lax.axis_index("ctx")
    z, y = c // 2, lax.rem(c, 2)
    xx, k = x // 2, lax.rem(x, 2)
    width = D // 4
    pair = 2 * width
    heads = width // HEAD_DIM
    odd = y == 1
    start = pl.multiple_of(xx * pair, 128)
    q_dev = pos.shape[-1]
    place = y * 2 + xx

    def flip(value, on):
        return 1 - value if on else value

    def far_z(m):
        return flip(z // 2, m // 2) * 2 + flip(lax.rem(z, 2), m % 2)

    def device(m, dy, dx, dk):
        return {"cells": far_z(m) * 2 + flip(y, dy), "ctx": flip(xx, dx) * 2 + flip(k, dk)}

    others = [(m, dy, dx, dk) for m in (3, 2, 1, 0) for dy in (1, 0) for dx in (1, 0) for dk in (1, 0)][:-1]

    loads = [
        pltpu.make_async_copy(src, dst, local_sem.at[i])
        for i, (src, dst) in enumerate(
            (
                (types_h, types),
                (type_w_h, type_w),
                (feats_h, feats),
                (routes_h, routes),
                (pos_h, pos),
                (tgt_h, tgt),
                (out_wt_h, out_wt),
                (anchor_g_h, anchor_g.at[0]),
                (query_g_h, query_g.at[0]),
                (key_g_h, key_g.at[0]),
                (query_w.at[:, pl.ds(start, pair)], qwin),
                (key_w_h, key_w),
            )
        )
    ]
    for load in loads[:4]:
        load.start()
    barrier = pltpu.get_barrier_semaphore()
    half = z // 2
    is_owner = (c >= 2) & (c < 6)
    greeted = [(m, dy, 0, 0) for m in (1, 2) for dy in (0, 1)]
    greeted += [(0, 1, 0, 0), (0, 0, 1, 0), (0, 1, 1, 0), (0, 0, 0, 1), (0, 0, 1, 1)]

    def greet(spot):
        pl.semaphore_signal(barrier, inc=1, device_id=device(*spot), device_id_type=MESH)

    for spot in greeted:
        greet(spot)

    @pl.when(is_owner)
    def _():
        greet((3, 0, 0, 0))
        greet((3, 1, 0, 0))

    for load in loads[4:]:
        load.start()

    def own(values):
        return jnp.where(odd, values[:, width:], values[:, :width])

    def copy_to(src, dst, send_sem, recv_sem, peer):
        return pltpu.make_async_remote_copy(
            src_ref=src, dst_ref=dst, send_sem=send_sem, recv_sem=recv_sem, device_id=peer, device_id_type=MESH
        )

    for load in loads[:3]:
        load.wait()
    block = feats.shape[0] // types.shape[1]
    for b in range(types.shape[1]):
        pre = mm(feats[b * block : (b + 1) * block, :], type_w[types[0, b]])
        emb[b * block : (b + 1) * block, :] = jnp.tanh(pre).astype(BF)
    for load in loads[3:6]:
        load.wait()
    row = lax.broadcasted_iota(jnp.int32, (4 * 8, feats.shape[0]), 0)
    slab = ((row // 16) * 2 + lax.rem(row, 8) // 4) * 2 + lax.rem(row // 8, 2)
    label = (slab * 4 + x) * SN_DEV + lax.rem(row, 4)
    table = (
        jnp.where(routes[0:1, :] == label, 1.0, 0.0) + jnp.where(routes[1:2, :] == label, 1.0, 0.0)
    ).astype(BF)
    sums = mm(table, emb[...])
    for o in range(4):
        part[o] = sums[8 * o : 8 * o + 8, :]
        part_b[o] = sums[8 * o : 8 * o + 8, :].astype(BF)
    both_all[place, 0:3, :] = pos[:, 0, :]
    both_all[place, 4:8, :] = tgt[...]

    def pool_copy(i):
        dh, dy = ((1, 1), (1, 0), (0, 1), (0, 0))[i]
        o = flip(half, dh) * 2 + flip(y, dy)
        return copy_to(
            part_b.at[o],
            part_in.at[lax.rem(c - (2 + o) + 8, 8)],
            a_send.at[i],
            a_recv.at[0],
            {"cells": 2 + o, "ctx": x},
        )

    pl.semaphore_wait(barrier, len(greeted) + jnp.where(is_owner, 2, 0))
    for i in range(3):
        pool_copy(i).start()

    @pl.when(jnp.logical_not(is_owner))
    def _():
        pool_copy(3).start()

    @pl.when(is_owner)
    def _():
        for dx, dk in ((1, 1), (1, 0), (0, 1)):
            pl.semaphore_signal(ready, inc=1, device_id=device(0, 0, dx, dk), device_id_type=MESH)

    p_copies = []
    quad = ((1, 1), (1, 0), (0, 1))
    for i, (dy, dx) in enumerate(quad):
        mine = both_all.at[place]
        p_copies.append(copy_to(mine, mine, p_send.at[i], p_recv.at[i], device(0, dy, dx, 0)))
        p_copies[i].start()

    for load in loads[6:]:
        load.wait()
    rates = rate_table()

    def embed_block(i):
        cols = pl.ds(pl.multiple_of(i * q_dev, 128), q_dev)
        for d in range(3):
            turns = rates * both_all[i, pl.ds(d, 1), :]
            whole = jnp.floor(turns + 0.5)
            rest = turns - whole
            parity = whole * 0.5
            sign = 1.0 - 4.0 * (parity - jnp.floor(parity))
            square = rest * rest
            spot = (2 * d) * FREQ
            emb_t[spot : spot + FREQ, cols] = (series(SIN_TERMS, square) * rest * sign).astype(BF)
            emb_t[spot + FREQ : spot + 2 * FREQ, cols] = (series(COS_TERMS, square) * sign).astype(BF)

    out_f = out_wt[...].astype(F32)
    out_t = jnp.concatenate([out_f, jnp.zeros_like(out_f)], axis=0).T.astype(BF)
    lane8 = lax.broadcasted_iota(jnp.int32, (8, 256), 1)
    pick = jnp.where(lax.rem(lane8, 4) == lax.broadcasted_iota(jnp.int32, (8, 256), 0), 1.0, 0.0).astype(BF)
    lane_d = lax.broadcasted_iota(jnp.int32, (D, 256), 1)
    inside = lax.rem(lane_d, 16) // 4
    head_of = (lane_d // 64) * heads + inside
    keep = (lax.broadcasted_iota(jnp.int32, (D, 256), 0) // HEAD_DIM == head_of) & (inside < heads)
    keep = keep & (lax.rem(lane_d, 64) < 48)
    w_out[...] = jnp.where(keep, mm(out_t, pick), 0.0).astype(BF)

    def key_copy(i):
        m, dy, dx, dk = others[i]
        group = flip(xx, dx) * 2 + flip(y, dy)
        return copy_to(
            kv_out.at[group],
            kv_in.at[(c - 2) * 4 + x],
            k_send.at[i],
            k_recv.at[0],
            device(m, dy, dx, dk),
        )

    @pl.when(is_owner)
    def _():
        arrived = part_in.at[pl.ds(1, 7)]
        copy_to(arrived, arrived, a_send.at[0], a_recv.at[0], {"cells": c, "ctx": x}).wait_recv()
        pooled = part[c - 2]
        for s in range(1, 8):
            pooled = pooled + part_in[s].astype(F32)
        inverse = lax.rsqrt(jnp.mean(pooled * pooled, axis=1, keepdims=True) + EPS)
        anchors = (pooled * inverse * anchor_g[...]).astype(BF)
        key_lin = mm(anchors, key_w[...])
        out_lin = mm(anchors, w_out[...])
        low = lax.broadcasted_iota(jnp.int32, (8, 128), 1) < HEAD_DIM
        pieces = []
        for j in range(D // 128):
            piece = key_lin[:, 128 * j : 128 * j + 128]
            square = piece * piece
            first = jnp.sum(jnp.where(low, square, 0.0), axis=1, keepdims=True)
            second = jnp.sum(jnp.where(low, 0.0, square), axis=1, keepdims=True)
            pieces.append(piece * lax.rsqrt(jnp.where(low, first, second) * (1.0 / HEAD_DIM) + EPS))
        keys = jnp.concatenate(pieces, axis=1) * key_g[...]
        coarse = out_lin.astype(BF).astype(F32)
        mixed = jnp.where(lax.rem(lane8, 64) // 16 == 1, out_lin - coarse, coarse)
        for g in range(4):
            kv_out[g] = jnp.concatenate(
                [keys[:, width * g : width * g + width], mixed[:, 64 * g : 64 * g + 64]], axis=1
            ).astype(BF)
        pl.semaphore_wait(ready, 3)
        for i in range(len(others)):
            key_copy(i).start()
        kv_in[(c - 2) * 4 + x] = kv_out[xx * 2 + y]

    embed_block(place)
    qwin_t[...] = qwin[...].T
    gain_t[...] = jnp.broadcast_to(query_g[:, pl.ds(start, pair)], (128, pair)).T

    for i, (dy, dx) in enumerate(quad):
        p_copies[i].wait_recv()
        embed_block(flip(y, dy) * 2 + flip(xx, dx))

    rows_mine = pl.ds(pl.multiple_of(y * width, 64), width)
    qlin[...] = mm(qwin_t[rows_mine, :], emb_t[...])
    gains = gain_t[rows_mine, :][:, 0:1]

    def norm_of(h):
        piece = qlin[h * HEAD_DIM : (h + 1) * HEAD_DIM, :]
        return lax.rsqrt(jnp.mean(piece * piece, axis=0, keepdims=True) + EPS)

    for h in range(heads):
        rows = slice(h * HEAD_DIM, (h + 1) * HEAD_DIM)
        hats[rows, :] = (qlin[rows, :] * norm_of(h) * gains[rows, :]).astype(BF)
    hats[width:, :] = jnp.zeros((256 - width, hats.shape[1]), BF)

    def keys_arrive(count):
        landed = kv_in.at[pl.ds(0, count)]
        copy_to(landed, landed, k_send.at[0], k_recv.at[0], {"cells": c, "ctx": x}).wait_recv()

    @pl.when(is_owner)
    def _():
        keys_arrive(15)

    @pl.when(jnp.logical_not(is_owner))
    def _():
        keys_arrive(16)

    both_f = jnp.concatenate([kv_in[s].astype(F32) for s in range(16)], axis=0)
    both = both_f.astype(BF)
    both_t = both.T
    scale = HEAD_DIM ** (-0.5)
    lane = lax.broadcasted_iota(jnp.int32, (both.shape[0], 128), 1)
    tile0, tile1 = both_f[:, :128], both_f[:, 128:]
    lefts = [
        jnp.where(lane < HEAD_DIM, tile0, 0.0).astype(BF),
        jnp.where(lane >= HEAD_DIM, tile0, 0.0).astype(BF),
        jnp.where(lane < HEAD_DIM, tile1, 0.0).astype(BF),
    ]
    queries = qlin.shape[1]
    out_row = lax.broadcasted_iota(jnp.int32, (16, queries), 0) // 4
    by_head = jnp.zeros((16, queries), F32)
    shares = []
    for h in range(heads):
        exponent = jnp.exp2(mm(lefts[h], hats[(h // 2) * 128 : (h // 2) * 128 + 128, :]) * (scale * math.log2(math.e)))
        probs[h] = exponent
        shares.append(1.0 / jnp.sum(exponent, axis=0, keepdims=True))
        outs = mm(both_t[width : width + 32, :], exponent.astype(BF))
        by_head = jnp.where(out_row == h, (outs[:16] + outs[16:]) * shares[h], by_head)
    pred_part[0] = by_head[0:4] + by_head[4:8] + by_head[8:12]
    o_copies = []
    for i, (dy, dx) in enumerate(quad):
        o_copies.append(
            copy_to(pred_part.at[0], pred_part.at[1 + i], o_send.at[i], o_recv.at[i], device(0, dy, dx, 0))
        )
        o_copies[i].start()

    for i in range(3):
        pool_copy(i).wait_send()

    @pl.when(jnp.logical_not(is_owner))
    def _():
        pool_copy(3).wait_send()

    @pl.when(is_owner)
    def _():
        for i in range(len(others)):
            key_copy(i).wait_send()

    for copy in p_copies:
        copy.wait_send()
    for h in range(heads):
        probs[h] = probs[h] * shares[h]
    goals = jnp.concatenate([both_all[i, 4:8, :] for i in range(4)], axis=1)
    backs = [
        jnp.where((lane >= 64) & (lax.rem(lane, 16) // 4 == h), tile1, 0.0).astype(BF) for h in range(heads)
    ]
    for copy in o_copies:
        copy.wait_recv()
    predicted = pred_part[0] + pred_part[1] + pred_part[2] + pred_part[3]
    residue = predicted - goals
    coarse = residue.astype(BF).astype(F32)
    rest = residue - coarse
    none = jnp.zeros((64, queries), F32)
    split = jnp.concatenate([none] + [coarse] * 8 + [rest] * 8, axis=0).astype(BF)
    weighed = by_head * jnp.concatenate([residue] * 4, axis=0)
    deep = D // 8
    tall = deep // 2
    groups = ((0, 1, 2),)
    order = (3, 2, 1, 0)

    def blocks(group, side):
        slabs = [emb_t[pl.ds(pl.multiple_of((far_z(m) * 2 + side) * deep, 16), deep), :] for m in order]
        cols = glin[group[0] * HEAD_DIM : (group[-1] + 1) * HEAD_DIM, :]
        full = lax.dot_general(
            jnp.concatenate(slabs, axis=0), cols, (((1,), (1,)), ((), ())), preferred_element_type=F32
        )
        packed = {}
        for i, m in enumerate(order):
            for j, h in enumerate(group):
                piece = full[deep * i : deep * i + deep, HEAD_DIM * j : HEAD_DIM * j + HEAD_DIM]
                packed[m, h] = jnp.concatenate([piece[:tall], piece[tall:]], axis=1)
        return packed

    def to_mate(g):
        span = pl.ds(groups[g][0], len(groups[g]))
        return copy_to(y_send.at[span], y_in.at[span], g_send.at[g], g_recv.at[g], device(0, 0, 0, 1))

    def along(g, m):
        span = pl.ds(groups[g][0], len(groups[g]))
        peer = {"cells": far_z(m) * 2 + k, "ctx": xx * 2 + y}
        spot = 3 + 4 * g + m
        return copy_to(z_send.at[m, span], z_in.at[m, span], g_send.at[spot], g_recv.at[spot], peer)

    for g, group in enumerate(groups):
        for h in group:
            rows = slice(h * HEAD_DIM, (h + 1) * HEAD_DIM)
            inner = jnp.sum(weighed[4 * h : 4 * h + 4], axis=0, keepdims=True)
            grad_s = (probs[h] * (mm(backs[h], split) - inner)).astype(BF)
            weighted = mm(both_t[rows, :], grad_s) * (gains[rows, :] * scale)
            inverse = norm_of(h)
            unit = qlin[rows, :] * inverse
            shared = jnp.mean(weighted * unit, axis=0, keepdims=True)
            glin[rows, :] = ((weighted - unit * shared) * inverse).astype(BF)
        packed = blocks(group, 1 - k)
        for m in order:
            for h in group:
                y_send[h, m] = packed[m, h].astype(BF)
        to_mate(g).start()
    kept = [blocks(group, k) for group in groups]
    for g, group in enumerate(groups):
        to_mate(g).wait_recv()
        for m in order[:3]:
            for h in group:
                z_send[m, h] = (kept[g][m, h] + y_in[h, m].astype(F32)).astype(BF)
            along(g, m).start()
        for h in group:
            near = kept[g][0, h] + y_in[h, 0].astype(F32)
            total[h] = near
            z_send[0, h] = near.astype(BF)

        @pl.when(y != k)
        def _():
            along(g, 0).start()

    cols = pl.ds(pl.multiple_of(place * q_dev, 128), q_dev)
    for copy in o_copies:
        copy.wait_send()
    pred_part[0] = predicted
    pred_out[...] = pred_part[0, :, cols]
    for g in range(len(groups)):
        to_mate(g).wait_send()
    for g, group in enumerate(groups):

        @pl.when(y != k)
        def _():
            along(g, 0).wait_recv()
            for h in group:
                total[h] = z_in[0, h].astype(F32)

        for m in (1, 2, 3):
            along(g, m).wait_recv()
        for h in group:
            summed = total[h]
            for m in (1, 2, 3):
                summed = summed + z_in[m, h].astype(F32)
            spot = slice(h * HEAD_DIM, (h + 1) * HEAD_DIM)
            grad_out[:tall, spot] = summed[:, :HEAD_DIM]
            grad_out[tall:, spot] = summed[:, HEAD_DIM:]
    for g in range(len(groups)):
        for m in (1, 2, 3):
            along(g, m).wait_send()

        @pl.when(y != k)
        def _():
            along(g, 0).wait_send()


def finish(pred_in, grad_in, pred_o, grad_o):
    pred_o[...] = pred_in[...]
    grad_o[...] = grad_in[...]

def fused_device(
    cell_feats,
    cell_types,
    cell_routes,
    positions,
    targets,
    type_weight,
    query_weight,
    key_weight,
    out_weight,
    anchor_gain,
    query_gain,
    key_gain,
):
    width = D // 4
    cells = cell_feats.shape[1]
    q_dev = positions.shape[2]
    queries = 4 * q_dev
    outs = targets.shape[1]
    deep = D // 8
    vmem = pl.BlockSpec(memory_space=pltpu.VMEM)
    dma = pltpu.SemaphoreType.DMA
    predicted, grad = pl.pallas_call(
        fused_kernel,
        out_shape=(
            pltpu.VMEM((outs, q_dev), F32),
            pltpu.VMEM((deep, width), F32),
        ),
        in_specs=[pl.BlockSpec(memory_space=pltpu.HBM)] * 12,
        out_specs=(vmem, vmem),
        scratch_shapes=[
            pltpu.VMEM((cells, cell_feats.shape[2]), BF),
            pltpu.SMEM(cell_types.shape, jnp.int32),
            pltpu.VMEM((cell_routes.shape[2], cells), jnp.int32),
            pltpu.VMEM((3, 1, q_dev), F32),
            pltpu.VMEM((outs, q_dev), F32),
            pltpu.VMEM(type_weight.shape, BF),
            pltpu.VMEM((outs, D), BF),
            pltpu.VMEM((1, D), F32),
            pltpu.VMEM((1, D), F32),
            pltpu.VMEM((1, D), F32),
            pltpu.VMEM((D, D), BF),
            pltpu.VMEM((D, 2 * width), BF),
            pltpu.VMEM((2 * width, D), BF),
            pltpu.VMEM((2 * width, 128), F32),
            pltpu.VMEM((cells, D), BF),
            pltpu.VMEM((4, 8, D), F32),
            pltpu.VMEM((4, 8, D), BF),
            pltpu.VMEM((8, 8, D), BF),
            pltpu.VMEM((D, 256), BF),
            pltpu.VMEM((4, 8, 256), BF),
            pltpu.VMEM((16, 8, 256), BF),
            pltpu.VMEM((4, 8, q_dev), F32),
            pltpu.VMEM((4, outs, queries), F32),
            pltpu.VMEM((D, queries), BF),
            pltpu.VMEM((width, queries), F32),
            pltpu.VMEM((256, queries), BF),
            pltpu.VMEM((width // HEAD_DIM, 128, queries), F32),
            pltpu.VMEM((width, queries), BF),
            pltpu.VMEM((3, 4, deep // 2, 128), BF),
            pltpu.VMEM((3, 4, deep // 2, 128), BF),
            pltpu.VMEM((4, 3, deep // 2, 128), BF),
            pltpu.VMEM((4, 3, deep // 2, 128), BF),
            pltpu.VMEM((3, deep // 2, 128), F32),
            dma((12,)),
            dma((4,)),
            dma((1,)),
            dma((3,)),
            dma((3,)),
            dma((31,)),
            dma((1,)),
            dma((3,)),
            dma((3,)),
            dma((15,)),
            dma((15,)),
            pltpu.SemaphoreType.REGULAR,
        ],
        compiler_params=pltpu.CompilerParams(
            collective_id=0, has_side_effects=True, vmem_limit_bytes=64 * 1024 * 1024 - 256 * 1024
        ),
    )(
        cell_feats[0],
        cell_types,
        cell_routes[0].T,
        positions[0].reshape(3, 1, q_dev),
        targets[0],
        type_weight,
        query_weight,
        key_weight,
        out_weight.T,
        anchor_gain,
        query_gain,
        key_gain,
    )
    predicted, grad = pl.pallas_call(
        finish,
        out_shape=(jax.ShapeDtypeStruct((outs, q_dev), F32), jax.ShapeDtypeStruct((deep, width), F32)),
        in_specs=[vmem, vmem],
        out_specs=(vmem, vmem),
        compiler_params=pltpu.CompilerParams(vmem_limit_bytes=1024 * 1024),
    )(predicted, grad)
    return (predicted[None], grad)


def solution(mesh):
    in_specs = (
        P(("groups", "dp"), ("cells", "ctx"), None),
        P(("groups", "dp"), ("cells", "ctx")),
        P(("groups", "dp"), ("cells", "ctx"), None),
        P(("groups", "dp"), None, ("cells", "ctx")),
        P(("groups", "dp"), None, ("cells", "ctx")),
        P(),
        P(),
        P(),
        P(),
        P(),
        P(),
        P(),
    )
    out_specs = (P(("groups", "dp"), None, ("cells", "ctx")), P(("groups", "cells"), ("ctx", "dp")))
    sizes = mesh.shape
    fits = sizes["groups"] == 1 and sizes["dp"] == 1 and sizes["ctx"] == 4 and sizes["cells"] == 8
    body = fused_device if fits else general_device
    return jax.shard_map(
        body, mesh=mesh, in_specs=in_specs, out_specs=out_specs, check_vma=False
    )
```

```python
import functools
import math

import jax
import jax.numpy as jnp
from jax import lax
from jax.experimental import pallas as pl
from jax.experimental.pallas import tpu as pltpu
from jax.sharding import PartitionSpec as P

D = 768
HEAD_DIM = 64
SN_DEV = 4
FREQ = 128


EPS = 1e-06


def head_norm(values):
    shaped = values.reshape(values.shape[:-1] + (values.shape[-1] // HEAD_DIM, HEAD_DIM))
    inverse = lax.rsqrt(jnp.mean(shaped * shaped, axis=-1, keepdims=True) + EPS)
    return (shaped * inverse).reshape(values.shape)


def embed_positions(coords):
    freq_ids = jnp.arange(FREQ, dtype=jnp.float32)
    rate_table = math.pi * jnp.exp2(freq_ids * (6.0 / FREQ))
    angles = jnp.transpose(coords)[:, :, None] * rate_table[None, None, :]
    sin_cos = jnp.stack([jnp.sin(angles), jnp.cos(angles)], axis=2)
    return sin_cos.reshape(coords.shape[1], 6 * FREQ).astype(jnp.bfloat16)


def cell_embed(cell_rows, type_ids, type_weight):
    row_count = cell_rows.shape[0]
    per_block = row_count // type_ids.shape[0]
    shaped = cell_rows.reshape(type_ids.shape[0], per_block, cell_rows.shape[1])
    chosen = type_weight[0][None]
    for type_id in range(1, type_weight.shape[0]):
        chosen = jnp.where((type_ids == type_id)[:, None, None], type_weight[type_id][None], chosen)
    pre_act = jnp.einsum("bnf,bfd->bnd", shaped, chosen, preferred_element_type=jnp.float32)
    return jnp.tanh(pre_act).astype(jnp.bfloat16).reshape(row_count, -1)


def make_keys(anchors, key_weight, key_gain):
    key_lin = jnp.dot(anchors, key_weight, preferred_element_type=jnp.float32)
    return (head_norm(key_lin) * key_gain).astype(jnp.bfloat16)


def general_device(
    cell_feats,
    cell_types,
    cell_routes,
    positions,
    targets,
    type_weight,
    query_weight,
    key_weight,
    out_weight,
    anchor_gain,
    query_gain,
    key_gain,
):
    slab_count = lax.axis_size("cells")
    column_count = lax.axis_size("ctx")
    cell_rows = cell_feats[0]
    type_ids = cell_types[0]
    routes = cell_routes[0]
    embedded = cell_embed(cell_rows, type_ids, type_weight)
    slots = jnp.arange(slab_count * SN_DEV, dtype=jnp.int32)
    owned = (slots // SN_DEV * column_count + lax.axis_index("ctx")) * SN_DEV + slots % SN_DEV
    table = jnp.sum((routes[None, :, :] == owned[:, None, None]).astype(jnp.int32), axis=2)
    partial = jnp.dot(table.astype(jnp.bfloat16), embedded, preferred_element_type=jnp.float32)
    pooled = lax.psum_scatter(partial, "cells", scatter_dimension=0, tiled=True)
    inverse = lax.rsqrt(jnp.mean(pooled * pooled, axis=-1, keepdims=True) + EPS)
    anchors = (pooled * inverse * anchor_gain).astype(jnp.bfloat16)
    own_keys = make_keys(anchors, key_weight, key_gain)
    all_keys, all_anchors = (
        lax.all_gather(own_keys, ("cells", "ctx"), axis=0, tiled=True),
        lax.all_gather(anchors, ("cells", "ctx"), axis=0, tiled=True),
    )
    embed = embed_positions(positions[0])
    query_lin = jnp.dot(embed, query_weight, preferred_element_type=jnp.float32)
    query_hat = (head_norm(query_lin) * query_gain).astype(jnp.bfloat16)
    query_count = embed.shape[0]
    head_count = D // HEAD_DIM
    group_size = 4
    score_scale = HEAD_DIM ** (-0.5)
    query_heads = query_hat.reshape(query_count, head_count, HEAD_DIM)
    key_heads = all_keys.reshape(-1, head_count, HEAD_DIM)
    value_heads = all_anchors.reshape(-1, head_count, HEAD_DIM)
    probs_saved = []
    outputs = []
    for first_head in range(0, head_count, group_size):
        last_head = first_head + group_size
        scores = (
            jnp.einsum(
                "qhd,khd->hqk",
                query_heads[:, first_head:last_head],
                key_heads[:, first_head:last_head],
                preferred_element_type=jnp.float32,
            )
            * score_scale
        )
        exponent = jnp.exp(scores)
        probs_f32 = exponent / jnp.sum(exponent, axis=-1, keepdims=True)
        probs_saved.append(probs_f32)
        outputs.append(
            jnp.einsum(
                "hqk,khd->qhd",
                probs_f32.astype(jnp.bfloat16),
                value_heads[:, first_head:last_head],
                preferred_element_type=jnp.float32,
            )
        )
    attended = jnp.concatenate(outputs, axis=1).reshape(query_count, D).astype(jnp.bfloat16)
    predicted = lax.dot_general(
        out_weight, attended, (((0,), (1,)), ((), ())), preferred_element_type=jnp.float32
    )
    residue = predicted - targets[0]
    grad_attended = lax.dot_general(
        residue,
        out_weight.astype(jnp.float32),
        (((0,), (1,)), ((), ())),
        precision=lax.Precision.HIGHEST,
    ).astype(jnp.bfloat16)
    grad_heads = grad_attended.reshape(query_count, head_count, HEAD_DIM)
    pieces = []
    for group_index, first_head in enumerate(range(0, head_count, group_size)):
        last_head = first_head + group_size
        probs_f32 = probs_saved[group_index]
        grad_weights = jnp.einsum(
            "qhd,khd->hqk",
            grad_heads[:, first_head:last_head],
            value_heads[:, first_head:last_head],
            preferred_element_type=jnp.float32,
        )
        grad_scores = probs_f32 * (
            grad_weights - jnp.sum(probs_f32 * grad_weights, axis=-1, keepdims=True)
        )
        pieces.append(
            jnp.einsum(
                "hqk,khd->qhd",
                grad_scores.astype(jnp.bfloat16),
                key_heads[:, first_head:last_head],
                preferred_element_type=jnp.float32,
            )
            * score_scale
        )
    grad_qhat = jnp.concatenate(pieces, axis=1).reshape(query_count, D)
    weighted = (grad_qhat * query_gain).reshape(query_count, head_count, HEAD_DIM)
    shaped = query_lin.reshape(query_count, head_count, HEAD_DIM)
    norm_inverse = lax.rsqrt(jnp.mean(shaped * shaped, axis=-1, keepdims=True) + EPS)
    unit_rows = shaped * norm_inverse
    grad_qlin = (
        (
            (weighted - unit_rows * jnp.mean(weighted * unit_rows, axis=-1, keepdims=True))
            * norm_inverse
        )
        .reshape(query_count, D)
        .astype(jnp.bfloat16)
    )
    summed = lax.psum_scatter(
        lax.dot_general(
            embed, grad_qlin, (((0,), (0,)), ((), ())), preferred_element_type=jnp.float32
        ),
        "cells",
        scatter_dimension=0,
        tiled=True,
    )
    grad_query = lax.psum_scatter(summed, ("ctx", "dp"), scatter_dimension=1, tiled=True)
    return (predicted[None], grad_query)


BF = jnp.bfloat16
F32 = jnp.float32
MESH = pl.DeviceIdType.MESH
SIN_TERMS = [math.pi ** n * (-1) ** (n // 2) / math.factorial(n) for n in (1, 3, 5, 7, 9, 11, 13)]
COS_TERMS = [math.pi ** n * (-1) ** (n // 2) / math.factorial(n) for n in (0, 2, 4, 6, 8, 10, 12)]


def mm(a, b):
    return jnp.dot(a, b, preferred_element_type=F32)


def series(terms, square):
    total = jnp.full_like(square, terms[-1])
    for term in terms[-2::-1]:
        total = total * square + term
    return total


def rate_table():
    ids = lax.broadcasted_iota(jnp.int32, (FREQ, FREQ), 0)
    rates = jnp.ones((FREQ, FREQ), F32)
    for bit in range(FREQ.bit_length() - 1):
        rates = rates * jnp.where((ids & (1 << bit)) != 0, 2.0 ** (6.0 * (1 << bit) / FREQ), 1.0).astype(F32)
    return rates


def fused_kernel(
    feats_h,
    types_h,
    routes_h,
    pos_h,
    tgt_h,
    type_w_h,
    query_w,
    key_w_h,
    out_wt_h,
    anchor_g_h,
    query_g_h,
    key_g_h,
    pred_out,
    grad_out,
    feats,
    types,
    routes,
    pos,
    tgt,
    type_w,
    out_wt,
    anchor_g,
    query_g,
    key_g,
    key_w,
    qwin,
    qwin_t,
    gain_t,
    emb,
    part,
    part_b,
    part_in,
    w_out,
    kv_out,
    kv_in,
    both_all,
    pred_part,
    emb_t,
    qlin,
    hats,
    probs,
    glin,
    y_send,
    y_in,
    z_send,
    z_in,
    total,
    local_sem,
    a_send,
    a_recv,
    p_send,
    p_recv,
    k_send,
    k_recv,
    o_send,
    o_recv,
    g_send,
    g_recv,
    ready,
):
    c = lax.axis_index("cells")
    x = lax.axis_index("ctx")
    z, y = c // 2, lax.rem(c, 2)
    xx, k = x // 2, lax.rem(x, 2)
    width = D // 4
    pair = 2 * width
    heads = width // HEAD_DIM
    odd = y == 1
    start = pl.multiple_of(xx * pair, 128)
    q_dev = pos.shape[-1]
    place = y * 2 + xx

    def flip(value, on):
        return 1 - value if on else value

    def far_z(m):
        return flip(z // 2, m // 2) * 2 + flip(lax.rem(z, 2), m % 2)

    def device(m, dy, dx, dk):
        return {"cells": far_z(m) * 2 + flip(y, dy), "ctx": flip(xx, dx) * 2 + flip(k, dk)}

    others = [(m, dy, dx, dk) for m in (3, 2, 1, 0) for dy in (1, 0) for dx in (1, 0) for dk in (1, 0)][:-1]

    loads = [
        pltpu.make_async_copy(src, dst, local_sem.at[i])
        for i, (src, dst) in enumerate(
            (
                (types_h, types),
                (type_w_h, type_w),
                (feats_h, feats),
                (routes_h, routes),
                (pos_h, pos),
                (tgt_h, tgt),
                (out_wt_h, out_wt),
                (anchor_g_h, anchor_g.at[0]),
                (query_g_h, query_g.at[0]),
                (key_g_h, key_g.at[0]),
                (query_w.at[:, pl.ds(start, pair)], qwin),
                (key_w_h, key_w),
            )
        )
    ]
    for load in loads[:4]:
        load.start()
    barrier = pltpu.get_barrier_semaphore()
    half = z // 2
    is_owner = (c >= 2) & (c < 6)
    greeted = [(m, dy, 0, 0) for m in (1, 2) for dy in (0, 1)]
    greeted += [(0, 1, 0, 0), (0, 0, 1, 0), (0, 1, 1, 0), (0, 0, 0, 1), (0, 0, 1, 1)]

    def greet(spot):
        pl.semaphore_signal(barrier, inc=1, device_id=device(*spot), device_id_type=MESH)

    for spot in greeted:
        greet(spot)

    @pl.when(is_owner)
    def _():
        greet((3, 0, 0, 0))
        greet((3, 1, 0, 0))

    for load in loads[4:]:
        load.start()

    def own(values):
        return jnp.where(odd, values[:, width:], values[:, :width])

    def copy_to(src, dst, send_sem, recv_sem, peer):
        return pltpu.make_async_remote_copy(
            src_ref=src, dst_ref=dst, send_sem=send_sem, recv_sem=recv_sem, device_id=peer, device_id_type=MESH
        )

    for load in loads[:3]:
        load.wait()
    block = feats.shape[0] // types.shape[1]
    for b in range(types.shape[1]):
        pre = mm(feats[b * block : (b + 1) * block, :], type_w[types[0, b]])
        emb[b * block : (b + 1) * block, :] = jnp.tanh(pre).astype(BF)
    for load in loads[3:6]:
        load.wait()
    row = lax.broadcasted_iota(jnp.int32, (4 * 8, feats.shape[0]), 0)
    slab = ((row // 16) * 2 + lax.rem(row, 8) // 4) * 2 + lax.rem(row // 8, 2)
    label = (slab * 4 + x) * SN_DEV + lax.rem(row, 4)
    table = (
        jnp.where(routes[0:1, :] == label, 1.0, 0.0) + jnp.where(routes[1:2, :] == label, 1.0, 0.0)
    ).astype(BF)
    sums = mm(table, emb[...])
    for o in range(4):
        part[o] = sums[8 * o : 8 * o + 8, :]
        part_b[o] = sums[8 * o : 8 * o + 8, :].astype(BF)
    both_all[place, 0:3, :] = pos[:, 0, :]
    both_all[place, 4:8, :] = tgt[...]

    def pool_copy(i):
        dh, dy = ((1, 1), (1, 0), (0, 1), (0, 0))[i]
        o = flip(half, dh) * 2 + flip(y, dy)
        return copy_to(
            part_b.at[o],
            part_in.at[lax.rem(c - (2 + o) + 8, 8)],
            a_send.at[i],
            a_recv.at[0],
            {"cells": 2 + o, "ctx": x},
        )

    pl.semaphore_wait(barrier, len(greeted) + jnp.where(is_owner, 2, 0))
    for i in range(3):
        pool_copy(i).start()

    @pl.when(jnp.logical_not(is_owner))
    def _():
        pool_copy(3).start()

    @pl.when(is_owner)
    def _():
        for dx, dk in ((1, 1), (1, 0), (0, 1)):
            pl.semaphore_signal(ready, inc=1, device_id=device(0, 0, dx, dk), device_id_type=MESH)

    p_copies = []
    quad = ((1, 1), (1, 0), (0, 1))
    for i, (dy, dx) in enumerate(quad):
        mine = both_all.at[place]
        p_copies.append(copy_to(mine, mine, p_send.at[i], p_recv.at[i], device(0, dy, dx, 0)))
        p_copies[i].start()

    for load in loads[6:]:
        load.wait()
    rates = rate_table()

    def embed_block(i):
        cols = pl.ds(pl.multiple_of(i * q_dev, 128), q_dev)
        for d in range(3):
            turns = rates * both_all[i, pl.ds(d, 1), :]
            whole = jnp.floor(turns + 0.5)
            rest = turns - whole
            parity = whole * 0.5
            sign = 1.0 - 4.0 * (parity - jnp.floor(parity))
            square = rest * rest
            spot = (2 * d) * FREQ
            emb_t[spot : spot + FREQ, cols] = (series(SIN_TERMS, square) * rest * sign).astype(BF)
            emb_t[spot + FREQ : spot + 2 * FREQ, cols] = (series(COS_TERMS, square) * sign).astype(BF)

    out_f = out_wt[...].astype(F32)
    out_t = jnp.concatenate([out_f, jnp.zeros_like(out_f)], axis=0).T.astype(BF)
    lane8 = lax.broadcasted_iota(jnp.int32, (8, 256), 1)
    pick = jnp.where(lax.rem(lane8, 4) == lax.broadcasted_iota(jnp.int32, (8, 256), 0), 1.0, 0.0).astype(BF)
    lane_d = lax.broadcasted_iota(jnp.int32, (D, 256), 1)
    inside = lax.rem(lane_d, 16) // 4
    head_of = (lane_d // 64) * heads + inside
    keep = (lax.broadcasted_iota(jnp.int32, (D, 256), 0) // HEAD_DIM == head_of) & (inside < heads)
    keep = keep & (lax.rem(lane_d, 64) < 48)
    w_out[...] = jnp.where(keep, mm(out_t, pick), 0.0).astype(BF)

    by_hops = sorted(others, key=lambda spot: -((0, 1, 2, 1)[spot[0]] * 2 + spot[1] * 2 + spot[2] * 2 + spot[3]))

    def key_copy(i):
        m, dy, dx, dk = by_hops[i]
        group = flip(xx, dx) * 2 + flip(y, dy)
        return copy_to(
            kv_out.at[group],
            kv_in.at[(c - 2) * 4 + x],
            k_send.at[i],
            k_recv.at[0],
            device(m, dy, dx, dk),
        )

    @pl.when(is_owner)
    def _():
        arrived = part_in.at[pl.ds(1, 7)]
        copy_to(arrived, arrived, a_send.at[0], a_recv.at[0], {"cells": c, "ctx": x}).wait_recv()
        pooled = part[c - 2]
        for s in range(1, 8):
            pooled = pooled + part_in[s].astype(F32)
        inverse = lax.rsqrt(jnp.mean(pooled * pooled, axis=1, keepdims=True) + EPS)
        anchors = (pooled * inverse * anchor_g[...]).astype(BF)
        key_lin = mm(anchors, key_w[...])
        out_lin = mm(anchors, w_out[...])
        low = lax.broadcasted_iota(jnp.int32, (8, 128), 1) < HEAD_DIM
        pieces = []
        for j in range(D // 128):
            piece = key_lin[:, 128 * j : 128 * j + 128]
            square = piece * piece
            first = jnp.sum(jnp.where(low, square, 0.0), axis=1, keepdims=True)
            second = jnp.sum(jnp.where(low, 0.0, square), axis=1, keepdims=True)
            pieces.append(piece * lax.rsqrt(jnp.where(low, first, second) * (1.0 / HEAD_DIM) + EPS))
        keys = jnp.concatenate(pieces, axis=1) * key_g[...]
        coarse = out_lin.astype(BF).astype(F32)
        mixed = jnp.where(lax.rem(lane8, 64) // 16 == 1, out_lin - coarse, coarse)
        for g in range(4):
            kv_out[g] = jnp.concatenate(
                [keys[:, width * g : width * g + width], mixed[:, 64 * g : 64 * g + 64]], axis=1
            ).astype(BF)
        pl.semaphore_wait(ready, 3)
        for i in range(len(others)):
            key_copy(i).start()
        kv_in[(c - 2) * 4 + x] = kv_out[xx * 2 + y]

    embed_block(place)
    qwin_t[...] = qwin[...].T
    gain_t[...] = jnp.broadcast_to(query_g[:, pl.ds(start, pair)], (128, pair)).T

    for i, (dy, dx) in enumerate(quad):
        p_copies[i].wait_recv()
        embed_block(flip(y, dy) * 2 + flip(xx, dx))

    rows_mine = pl.ds(pl.multiple_of(y * width, 64), width)
    qlin[...] = mm(qwin_t[rows_mine, :], emb_t[...])
    gains = gain_t[rows_mine, :][:, 0:1]

    def norm_of(h):
        piece = qlin[h * HEAD_DIM : (h + 1) * HEAD_DIM, :]
        return lax.rsqrt(jnp.mean(piece * piece, axis=0, keepdims=True) + EPS)

    for h in range(heads):
        rows = slice(h * HEAD_DIM, (h + 1) * HEAD_DIM)
        hats[rows, :] = (qlin[rows, :] * norm_of(h) * gains[rows, :]).astype(BF)
    hats[width:, :] = jnp.zeros((256 - width, hats.shape[1]), BF)

    def keys_arrive(count):
        landed = kv_in.at[pl.ds(0, count)]
        copy_to(landed, landed, k_send.at[0], k_recv.at[0], {"cells": c, "ctx": x}).wait_recv()

    @pl.when(is_owner)
    def _():
        keys_arrive(15)

    @pl.when(jnp.logical_not(is_owner))
    def _():
        keys_arrive(16)

    both_f = jnp.concatenate([kv_in[s].astype(F32) for s in range(16)], axis=0)
    both = both_f.astype(BF)
    both_t = both.T
    scale = HEAD_DIM ** (-0.5)
    lane = lax.broadcasted_iota(jnp.int32, (both.shape[0], 128), 1)
    tile0, tile1 = both_f[:, :128], both_f[:, 128:]
    lefts = [
        jnp.where(lane < HEAD_DIM, tile0, 0.0).astype(BF),
        jnp.where(lane >= HEAD_DIM, tile0, 0.0).astype(BF),
        jnp.where(lane < HEAD_DIM, tile1, 0.0).astype(BF),
    ]
    queries = qlin.shape[1]
    out_row = lax.broadcasted_iota(jnp.int32, (16, queries), 0) // 4
    by_head = jnp.zeros((16, queries), F32)
    shares = []
    for h in range(heads):
        exponent = jnp.exp2(mm(lefts[h], hats[(h // 2) * 128 : (h // 2) * 128 + 128, :]) * (scale * math.log2(math.e)))
        probs[h] = exponent
        shares.append(1.0 / jnp.sum(exponent, axis=0, keepdims=True))
        outs = mm(both_t[width : width + 32, :], exponent.astype(BF))
        by_head = jnp.where(out_row == h, (outs[:16] + outs[16:]) * shares[h], by_head)
    pred_part[0] = by_head[0:4] + by_head[4:8] + by_head[8:12]
    o_copies = []
    for i, (dy, dx) in enumerate(quad):
        o_copies.append(
            copy_to(pred_part.at[0], pred_part.at[1 + i], o_send.at[i], o_recv.at[i], device(0, dy, dx, 0))
        )
        o_copies[i].start()

    for i in range(3):
        pool_copy(i).wait_send()

    @pl.when(jnp.logical_not(is_owner))
    def _():
        pool_copy(3).wait_send()

    @pl.when(is_owner)
    def _():
        for i in range(len(others)):
            key_copy(i).wait_send()

    for copy in p_copies:
        copy.wait_send()
    for h in range(heads):
        probs[h] = probs[h] * shares[h]
    goals = jnp.concatenate([both_all[i, 4:8, :] for i in range(4)], axis=1)
    backs = [
        jnp.where((lane >= 64) & (lax.rem(lane, 16) // 4 == h), tile1, 0.0).astype(BF) for h in range(heads)
    ]
    for copy in o_copies:
        copy.wait_recv()
    predicted = pred_part[0] + pred_part[1] + pred_part[2] + pred_part[3]
    residue = predicted - goals
    coarse = residue.astype(BF).astype(F32)
    rest = residue - coarse
    none = jnp.zeros((64, queries), F32)
    split = jnp.concatenate([none] + [coarse] * 8 + [rest] * 8, axis=0).astype(BF)
    weighed = by_head * jnp.concatenate([residue] * 4, axis=0)
    for h in range(heads):
        rows = slice(h * HEAD_DIM, (h + 1) * HEAD_DIM)
        inner = jnp.sum(weighed[4 * h : 4 * h + 4], axis=0, keepdims=True)
        grad_s = (probs[h] * (mm(backs[h], split) - inner)).astype(BF)
        weighted = mm(both_t[rows, :], grad_s) * (gains[rows, :] * scale)
        inverse = norm_of(h)
        unit = qlin[rows, :] * inverse
        shared = jnp.mean(weighted * unit, axis=0, keepdims=True)
        glin[rows, :] = ((weighted - unit * shared) * inverse).astype(BF)

    deep = D // 8
    tall = deep // 2
    middle = (z == 1) | (z == 2)
    places = [jnp.where(middle, a, b) for a, b in ((2, 3), (1, 2), (3, 1))]
    layers = [jnp.where(middle, far_z(a), far_z(b)) for a, b in ((2, 3), (1, 2), (3, 1))] + [z]

    def blocks(side, steps):
        slabs = [emb_t[pl.ds(pl.multiple_of((layers[j] * 2 + side) * deep, 16), deep), :] for j in steps]
        full = lax.dot_general(
            jnp.concatenate(slabs, axis=0), glin[...], (((1,), (1,)), ((), ())), preferred_element_type=F32
        )
        packed = {}
        for i, j in enumerate(steps):
            pieces = []
            for h in range(heads):
                piece = full[deep * i : deep * i + deep, HEAD_DIM * h : HEAD_DIM * h + HEAD_DIM]
                pieces.append(jnp.concatenate([piece[:tall], piece[tall:]], axis=1))
            packed[j] = jnp.concatenate(pieces, axis=0)
        return packed

    sent_blocks = blocks(1 - k, (0, 1, 2, 3))
    for j in range(4):
        y_send[j] = sent_blocks[j].astype(BF)
    to_mate = copy_to(y_send, y_in, g_send.at[4], g_recv.at[4], device(0, 0, 0, 1))
    to_mate.start()

    def along(j):
        slot = 0 if j == 3 else places[j]
        peer = {"cells": layers[j] * 2 + k, "ctx": xx * 2 + y}
        return copy_to(z_send.at[j], z_in.at[slot], g_send.at[j], g_recv.at[slot], peer)

    kept = blocks(k, (0,))
    to_mate.wait_recv()
    z_send[0] = (kept[0] + y_in[0].astype(F32)).astype(BF)
    along(0).start()
    kept = blocks(k, (1, 2, 3))
    for j in (1, 2):
        z_send[j] = (kept[j] + y_in[j].astype(F32)).astype(BF)
        along(j).start()
    near = kept[3] + y_in[3].astype(F32)
    total[...] = near

    @pl.when(y != k)
    def _():
        z_send[3] = near.astype(BF)
        along(3).start()

    cols = pl.ds(pl.multiple_of(place * q_dev, 128), q_dev)
    for copy in o_copies:
        copy.wait_send()
    pred_part[0] = predicted
    pred_out[...] = pred_part[0, :, cols]
    to_mate.wait_send()

    def arrived(slot):
        return copy_to(z_send.at[0], z_in.at[slot], g_send.at[0], g_recv.at[slot], device(0, 0, 0, 1))

    @pl.when(y != k)
    def _():
        arrived(0).wait_recv()
        total[...] = z_in[0].astype(F32)

    summed = total[...]
    for slot in (1, 2, 3):
        arrived(slot).wait_recv()
        summed = summed + z_in[slot].astype(F32)
    for h in range(heads):
        spot = slice(h * HEAD_DIM, (h + 1) * HEAD_DIM)
        grad_out[:tall, spot] = summed[tall * h : tall * h + tall, :HEAD_DIM]
        grad_out[tall:, spot] = summed[tall * h : tall * h + tall, HEAD_DIM:]
    for j in range(3):
        along(j).wait_send()

    @pl.when(y != k)
    def _():
        along(3).wait_send()


def finish(pred_in, grad_in, pred_o, grad_o):
    pred_o[...] = pred_in[...]
    grad_o[...] = grad_in[...]

def fused_device(
    cell_feats,
    cell_types,
    cell_routes,
    positions,
    targets,
    type_weight,
    query_weight,
    key_weight,
    out_weight,
    anchor_gain,
    query_gain,
    key_gain,
):
    width = D // 4
    cells = cell_feats.shape[1]
    q_dev = positions.shape[2]
    queries = 4 * q_dev
    outs = targets.shape[1]
    deep = D // 8
    vmem = pl.BlockSpec(memory_space=pltpu.VMEM)
    dma = pltpu.SemaphoreType.DMA
    predicted, grad = pl.pallas_call(
        fused_kernel,
        out_shape=(
            pltpu.VMEM((outs, q_dev), F32),
            pltpu.VMEM((deep, width), F32),
        ),
        in_specs=[pl.BlockSpec(memory_space=pltpu.HBM)] * 12,
        out_specs=(vmem, vmem),
        scratch_shapes=[
            pltpu.VMEM((cells, cell_feats.shape[2]), BF),
            pltpu.SMEM(cell_types.shape, jnp.int32),
            pltpu.VMEM((cell_routes.shape[2], cells), jnp.int32),
            pltpu.VMEM((3, 1, q_dev), F32),
            pltpu.VMEM((outs, q_dev), F32),
            pltpu.VMEM(type_weight.shape, BF),
            pltpu.VMEM((outs, D), BF),
            pltpu.VMEM((1, D), F32),
            pltpu.VMEM((1, D), F32),
            pltpu.VMEM((1, D), F32),
            pltpu.VMEM((D, D), BF),
            pltpu.VMEM((D, 2 * width), BF),
            pltpu.VMEM((2 * width, D), BF),
            pltpu.VMEM((2 * width, 128), F32),
            pltpu.VMEM((cells, D), BF),
            pltpu.VMEM((4, 8, D), F32),
            pltpu.VMEM((4, 8, D), BF),
            pltpu.VMEM((8, 8, D), BF),
            pltpu.VMEM((D, 256), BF),
            pltpu.VMEM((4, 8, 256), BF),
            pltpu.VMEM((16, 8, 256), BF),
            pltpu.VMEM((4, 8, q_dev), F32),
            pltpu.VMEM((4, outs, queries), F32),
            pltpu.VMEM((D, queries), BF),
            pltpu.VMEM((width, queries), F32),
            pltpu.VMEM((256, queries), BF),
            pltpu.VMEM((width // HEAD_DIM, 128, queries), F32),
            pltpu.VMEM((width, queries), BF),
            pltpu.VMEM((4, 3 * deep // 2, 128), BF),
            pltpu.VMEM((4, 3 * deep // 2, 128), BF),
            pltpu.VMEM((4, 3 * deep // 2, 128), BF),
            pltpu.VMEM((4, 3 * deep // 2, 128), BF),
            pltpu.VMEM((3 * deep // 2, 128), F32),
            dma((12,)),
            dma((4,)),
            dma((1,)),
            dma((3,)),
            dma((3,)),
            dma((31,)),
            dma((1,)),
            dma((3,)),
            dma((3,)),
            dma((5,)),
            dma((5,)),
            pltpu.SemaphoreType.REGULAR,
        ],
        compiler_params=pltpu.CompilerParams(
            collective_id=0, has_side_effects=True, vmem_limit_bytes=64 * 1024 * 1024 - 256 * 1024
        ),
    )(
        cell_feats[0],
        cell_types,
        cell_routes[0].T,
        positions[0].reshape(3, 1, q_dev),
        targets[0],
        type_weight,
        query_weight,
        key_weight,
        out_weight.T,
        anchor_gain,
        query_gain,
        key_gain,
    )
    predicted, grad = pl.pallas_call(
        finish,
        out_shape=(jax.ShapeDtypeStruct((outs, q_dev), F32), jax.ShapeDtypeStruct((deep, width), F32)),
        in_specs=[vmem, vmem],
        out_specs=(vmem, vmem),
        compiler_params=pltpu.CompilerParams(vmem_limit_bytes=1024 * 1024),
    )(predicted, grad)
    return (predicted[None], grad)


def solution(mesh):
    in_specs = (
        P(("groups", "dp"), ("cells", "ctx"), None),
        P(("groups", "dp"), ("cells", "ctx")),
        P(("groups", "dp"), ("cells", "ctx"), None),
        P(("groups", "dp"), None, ("cells", "ctx")),
        P(("groups", "dp"), None, ("cells", "ctx")),
        P(),
        P(),
        P(),
        P(),
        P(),
        P(),
        P(),
    )
    out_specs = (P(("groups", "dp"), None, ("cells", "ctx")), P(("groups", "cells"), ("ctx", "dp")))
    sizes = mesh.shape
    fits = sizes["groups"] == 1 and sizes["dp"] == 1 and sizes["ctx"] == 4 and sizes["cells"] == 8
    body = fused_device if fits else general_device
    return jax.shard_map(
        body, mesh=mesh, in_specs=in_specs, out_specs=out_specs, check_vma=False
    )
```

```python
import functools
import math

import jax
import jax.numpy as jnp
from jax import lax
from jax.experimental import pallas as pl
from jax.experimental.pallas import tpu as pltpu
from jax.sharding import PartitionSpec as P

D = 768
HEAD_DIM = 64
SN_DEV = 4
FREQ = 128


EPS = 1e-06


def head_norm(values):
    shaped = values.reshape(values.shape[:-1] + (values.shape[-1] // HEAD_DIM, HEAD_DIM))
    inverse = lax.rsqrt(jnp.mean(shaped * shaped, axis=-1, keepdims=True) + EPS)
    return (shaped * inverse).reshape(values.shape)


def embed_positions(coords):
    freq_ids = jnp.arange(FREQ, dtype=jnp.float32)
    rate_table = math.pi * jnp.exp2(freq_ids * (6.0 / FREQ))
    angles = jnp.transpose(coords)[:, :, None] * rate_table[None, None, :]
    sin_cos = jnp.stack([jnp.sin(angles), jnp.cos(angles)], axis=2)
    return sin_cos.reshape(coords.shape[1], 6 * FREQ).astype(jnp.bfloat16)


def cell_embed(cell_rows, type_ids, type_weight):
    row_count = cell_rows.shape[0]
    per_block = row_count // type_ids.shape[0]
    shaped = cell_rows.reshape(type_ids.shape[0], per_block, cell_rows.shape[1])
    chosen = type_weight[0][None]
    for type_id in range(1, type_weight.shape[0]):
        chosen = jnp.where((type_ids == type_id)[:, None, None], type_weight[type_id][None], chosen)
    pre_act = jnp.einsum("bnf,bfd->bnd", shaped, chosen, preferred_element_type=jnp.float32)
    return jnp.tanh(pre_act).astype(jnp.bfloat16).reshape(row_count, -1)


def make_keys(anchors, key_weight, key_gain):
    key_lin = jnp.dot(anchors, key_weight, preferred_element_type=jnp.float32)
    return (head_norm(key_lin) * key_gain).astype(jnp.bfloat16)


def general_device(
    cell_feats,
    cell_types,
    cell_routes,
    positions,
    targets,
    type_weight,
    query_weight,
    key_weight,
    out_weight,
    anchor_gain,
    query_gain,
    key_gain,
):
    slab_count = lax.axis_size("cells")
    column_count = lax.axis_size("ctx")
    cell_rows = cell_feats[0]
    type_ids = cell_types[0]
    routes = cell_routes[0]
    embedded = cell_embed(cell_rows, type_ids, type_weight)
    slots = jnp.arange(slab_count * SN_DEV, dtype=jnp.int32)
    owned = (slots // SN_DEV * column_count + lax.axis_index("ctx")) * SN_DEV + slots % SN_DEV
    table = jnp.sum((routes[None, :, :] == owned[:, None, None]).astype(jnp.int32), axis=2)
    partial = jnp.dot(table.astype(jnp.bfloat16), embedded, preferred_element_type=jnp.float32)
    pooled = lax.psum_scatter(partial, "cells", scatter_dimension=0, tiled=True)
    inverse = lax.rsqrt(jnp.mean(pooled * pooled, axis=-1, keepdims=True) + EPS)
    anchors = (pooled * inverse * anchor_gain).astype(jnp.bfloat16)
    own_keys = make_keys(anchors, key_weight, key_gain)
    all_keys, all_anchors = (
        lax.all_gather(own_keys, ("cells", "ctx"), axis=0, tiled=True),
        lax.all_gather(anchors, ("cells", "ctx"), axis=0, tiled=True),
    )
    embed = embed_positions(positions[0])
    query_lin = jnp.dot(embed, query_weight, preferred_element_type=jnp.float32)
    query_hat = (head_norm(query_lin) * query_gain).astype(jnp.bfloat16)
    query_count = embed.shape[0]
    head_count = D // HEAD_DIM
    group_size = 4
    score_scale = HEAD_DIM ** (-0.5)
    query_heads = query_hat.reshape(query_count, head_count, HEAD_DIM)
    key_heads = all_keys.reshape(-1, head_count, HEAD_DIM)
    value_heads = all_anchors.reshape(-1, head_count, HEAD_DIM)
    probs_saved = []
    outputs = []
    for first_head in range(0, head_count, group_size):
        last_head = first_head + group_size
        scores = (
            jnp.einsum(
                "qhd,khd->hqk",
                query_heads[:, first_head:last_head],
                key_heads[:, first_head:last_head],
                preferred_element_type=jnp.float32,
            )
            * score_scale
        )
        exponent = jnp.exp(scores)
        probs_f32 = exponent / jnp.sum(exponent, axis=-1, keepdims=True)
        probs_saved.append(probs_f32)
        outputs.append(
            jnp.einsum(
                "hqk,khd->qhd",
                probs_f32.astype(jnp.bfloat16),
                value_heads[:, first_head:last_head],
                preferred_element_type=jnp.float32,
            )
        )
    attended = jnp.concatenate(outputs, axis=1).reshape(query_count, D).astype(jnp.bfloat16)
    predicted = lax.dot_general(
        out_weight, attended, (((0,), (1,)), ((), ())), preferred_element_type=jnp.float32
    )
    residue = predicted - targets[0]
    grad_attended = lax.dot_general(
        residue,
        out_weight.astype(jnp.float32),
        (((0,), (1,)), ((), ())),
        precision=lax.Precision.HIGHEST,
    ).astype(jnp.bfloat16)
    grad_heads = grad_attended.reshape(query_count, head_count, HEAD_DIM)
    pieces = []
    for group_index, first_head in enumerate(range(0, head_count, group_size)):
        last_head = first_head + group_size
        probs_f32 = probs_saved[group_index]
        grad_weights = jnp.einsum(
            "qhd,khd->hqk",
            grad_heads[:, first_head:last_head],
            value_heads[:, first_head:last_head],
            preferred_element_type=jnp.float32,
        )
        grad_scores = probs_f32 * (
            grad_weights - jnp.sum(probs_f32 * grad_weights, axis=-1, keepdims=True)
        )
        pieces.append(
            jnp.einsum(
                "hqk,khd->qhd",
                grad_scores.astype(jnp.bfloat16),
                key_heads[:, first_head:last_head],
                preferred_element_type=jnp.float32,
            )
            * score_scale
        )
    grad_qhat = jnp.concatenate(pieces, axis=1).reshape(query_count, D)
    weighted = (grad_qhat * query_gain).reshape(query_count, head_count, HEAD_DIM)
    shaped = query_lin.reshape(query_count, head_count, HEAD_DIM)
    norm_inverse = lax.rsqrt(jnp.mean(shaped * shaped, axis=-1, keepdims=True) + EPS)
    unit_rows = shaped * norm_inverse
    grad_qlin = (
        (
            (weighted - unit_rows * jnp.mean(weighted * unit_rows, axis=-1, keepdims=True))
            * norm_inverse
        )
        .reshape(query_count, D)
        .astype(jnp.bfloat16)
    )
    summed = lax.psum_scatter(
        lax.dot_general(
            embed, grad_qlin, (((0,), (0,)), ((), ())), preferred_element_type=jnp.float32
        ),
        "cells",
        scatter_dimension=0,
        tiled=True,
    )
    grad_query = lax.psum_scatter(summed, ("ctx", "dp"), scatter_dimension=1, tiled=True)
    return (predicted[None], grad_query)


BF = jnp.bfloat16
F32 = jnp.float32
MESH = pl.DeviceIdType.MESH
SIN_TERMS = [math.pi ** n * (-1) ** (n // 2) / math.factorial(n) for n in (1, 3, 5, 7, 9, 11, 13)]
COS_TERMS = [math.pi ** n * (-1) ** (n // 2) / math.factorial(n) for n in (0, 2, 4, 6, 8, 10, 12)]


def mm(a, b):
    return jnp.dot(a, b, preferred_element_type=F32)


def series(terms, square):
    total = jnp.full_like(square, terms[-1])
    for term in terms[-2::-1]:
        total = total * square + term
    return total


def rate_table():
    ids = lax.broadcasted_iota(jnp.int32, (FREQ, FREQ), 0)
    rates = jnp.ones((FREQ, FREQ), F32)
    for bit in range(FREQ.bit_length() - 1):
        rates = rates * jnp.where((ids & (1 << bit)) != 0, 2.0 ** (6.0 * (1 << bit) / FREQ), 1.0).astype(F32)
    return rates


def fused_kernel(
    feats_h,
    types_h,
    routes_h,
    pos_h,
    tgt_h,
    type_w_h,
    query_w,
    key_w_h,
    out_wt_h,
    anchor_g_h,
    query_g_h,
    key_g_h,
    pred_out,
    grad_out,
    feats,
    types,
    routes,
    pos,
    tgt,
    type_w,
    out_wt,
    anchor_g,
    query_g,
    key_g,
    key_w,
    qwin,
    qwin_t,
    gain_t,
    emb,
    part,
    part_b,
    part_in,
    w_out,
    kv_out,
    kv_in,
    both_all,
    pred_part,
    emb_t,
    qlin,
    hats,
    unit,
    wide,
    lean,
    probs,
    glin,
    y_send,
    y_in,
    z_send,
    z_in,
    total,
    local_sem,
    a_send,
    a_recv,
    p_send,
    p_recv,
    k_send,
    k_recv,
    o_send,
    o_recv,
    g_send,
    g_recv,
    ready,
):
    c = lax.axis_index("cells")
    x = lax.axis_index("ctx")
    z, y = c // 2, lax.rem(c, 2)
    xx, k = x // 2, lax.rem(x, 2)
    width = D // 4
    pair = 2 * width
    heads = width // HEAD_DIM
    odd = y == 1
    start = pl.multiple_of(xx * pair, 128)
    q_dev = pos.shape[-1]
    place = y * 2 + xx

    def flip(value, on):
        return 1 - value if on else value

    def far_z(m):
        return flip(z // 2, m // 2) * 2 + flip(lax.rem(z, 2), m % 2)

    def device(m, dy, dx, dk):
        return {"cells": far_z(m) * 2 + flip(y, dy), "ctx": flip(xx, dx) * 2 + flip(k, dk)}

    others = [(m, dy, dx, dk) for m in (3, 2, 1, 0) for dy in (1, 0) for dx in (1, 0) for dk in (1, 0)][:-1]

    loads = [
        pltpu.make_async_copy(src, dst, local_sem.at[i])
        for i, (src, dst) in enumerate(
            (
                (types_h, types),
                (type_w_h, type_w),
                (feats_h, feats),
                (routes_h, routes),
                (pos_h, pos),
                (tgt_h, tgt),
                (out_wt_h, out_wt),
                (anchor_g_h, anchor_g.at[0]),
                (query_g_h, query_g.at[0]),
                (key_g_h, key_g.at[0]),
                (query_w.at[:, pl.ds(start, pair)], qwin),
                (key_w_h, key_w),
            )
        )
    ]
    for load in loads[:4]:
        load.start()
    barrier = pltpu.get_barrier_semaphore()
    half = z // 2
    is_owner = (c >= 2) & (c < 6) & (k == 1)

    def greet(peer):
        pl.semaphore_signal(barrier, inc=1, device_id=peer, device_id_type=MESH)

    def owner_at(dh, dy):
        return flip(half, dh) * 2 + flip(y, dy)

    @pl.when(is_owner)
    def _():
        for m in (2, 3, 1, 0):
            for dy in (1, 0):
                for dk in (1, 0):
                    if m or dy or dk:
                        greet(device(m, dy, 0, dk))

    @pl.when(jnp.logical_not(is_owner))
    def _():
        for dh, dy in ((1, 1), (1, 0), (0, 1), (0, 0)):
            greet({"cells": 2 + owner_at(dh, dy), "ctx": xx * 2 + 1})

    for dy, dx in ((1, 1), (1, 0), (0, 1)):
        greet(device(0, dy, dx, 0))

    for load in loads[4:]:
        load.start()

    def own(values):
        return jnp.where(odd, values[:, width:], values[:, :width])

    def copy_to(src, dst, send_sem, recv_sem, peer):
        return pltpu.make_async_remote_copy(
            src_ref=src, dst_ref=dst, send_sem=send_sem, recv_sem=recv_sem, device_id=peer, device_id_type=MESH
        )

    for load in loads[:3]:
        load.wait()
    block = feats.shape[0] // types.shape[1]
    for b in range(types.shape[1]):
        pre = mm(feats[b * block : (b + 1) * block, :], type_w[types[0, b]])
        emb[b * block : (b + 1) * block, :] = jnp.tanh(pre).astype(BF)
    for load in loads[3:6]:
        load.wait()
    row = lax.broadcasted_iota(jnp.int32, (4 * 8, feats.shape[0]), 0)
    slab = ((row // 16) * 2 + lax.rem(row, 8) // 4) * 2 + lax.rem(row // 8, 2)
    label = (slab * 4 + x) * SN_DEV + lax.rem(row, 4)
    table = (
        jnp.where(routes[0:1, :] == label, 1.0, 0.0) + jnp.where(routes[1:2, :] == label, 1.0, 0.0)
    ).astype(BF)
    sums = mm(table, emb[...])
    for o in range(4):
        part[o] = sums[8 * o : 8 * o + 8, :]
        part_b[o] = sums[8 * o : 8 * o + 8, :].astype(BF)
    both_all[place, 0:3, :] = pos[:, 0, :]
    both_all[place, 4:8, :] = tgt[...]

    def pool_copy(i):
        dh, dy = ((1, 1), (1, 0), (0, 1), (0, 0))[i]
        o = owner_at(dh, dy)
        return copy_to(
            part_b.at[o],
            part_in.at[k * 8 + lax.rem(c - (2 + o) + 8, 8)],
            a_send.at[i],
            a_recv.at[0],
            {"cells": 2 + o, "ctx": xx * 2 + 1},
        )

    pl.semaphore_wait(barrier, 3 + jnp.where(is_owner, 15, 4))
    for i in range(3):
        pool_copy(i).start()

    @pl.when(jnp.logical_not(is_owner))
    def _():
        pool_copy(3).start()

    @pl.when(is_owner)
    def _():
        pl.semaphore_signal(ready, inc=1, device_id=device(0, 0, 1, 0), device_id_type=MESH)

    p_copies = []
    quad = ((1, 1), (1, 0), (0, 1))
    for i, (dy, dx) in enumerate(quad):
        mine = both_all.at[place]
        p_copies.append(copy_to(mine, mine, p_send.at[i], p_recv.at[i], device(0, dy, dx, 0)))
        p_copies[i].start()

    for load in loads[6:]:
        load.wait()
    rates = rate_table()

    def embed_block(i):
        cols = pl.ds(pl.multiple_of(i * q_dev, 128), q_dev)
        for d in range(3):
            turns = rates * both_all[i, pl.ds(d, 1), :]
            whole = jnp.floor(turns + 0.5)
            rest = turns - whole
            parity = whole * 0.5
            sign = 1.0 - 4.0 * (parity - jnp.floor(parity))
            square = rest * rest
            spot = (2 * d) * FREQ
            emb_t[spot : spot + FREQ, cols] = (series(SIN_TERMS, square) * rest * sign).astype(BF)
            emb_t[spot + FREQ : spot + 2 * FREQ, cols] = (series(COS_TERMS, square) * sign).astype(BF)

    out_f = out_wt[...].astype(F32)
    out_t = jnp.concatenate([out_f, jnp.zeros_like(out_f)], axis=0).T.astype(BF)
    lane8 = lax.broadcasted_iota(jnp.int32, (8, 256), 1)
    pick = jnp.where(lax.rem(lane8, 4) == lax.broadcasted_iota(jnp.int32, (8, 256), 0), 1.0, 0.0).astype(BF)
    lane_d = lax.broadcasted_iota(jnp.int32, (D, 256), 1)
    inside = lax.rem(lane_d, 16) // 4
    head_of = (lane_d // 64) * heads + inside
    keep = (lax.broadcasted_iota(jnp.int32, (D, 256), 0) // HEAD_DIM == head_of) & (inside < heads)
    keep = keep & (lax.rem(lane_d, 64) < 48)
    w_out[...] = jnp.where(keep, mm(out_t, pick), 0.0).astype(BF)

    by_hops = sorted(others, key=lambda spot: -((0, 1, 2, 1)[spot[0]] * 2 + spot[1] * 2 + spot[2] * 2 + spot[3]))

    def key_copy(i):
        m, dy, dx, dk = by_hops[i]
        group = flip(xx, dx) * 2 + flip(y, dy)
        return copy_to(
            kv_out.at[group],
            kv_in.at[(c - 2) * 2 + xx],
            k_send.at[i],
            k_recv.at[half],
            device(m, dy, dx, dk),
        )

    @pl.when(is_owner)
    def _():
        arrived = part_in.at[pl.ds(0, 15)]
        copy_to(arrived, arrived, a_send.at[0], a_recv.at[0], {"cells": c, "ctx": x}).wait_recv()
        first, second = part_in[0].astype(F32), part[c - 2]
        for s in range(1, 8):
            first = first + part_in[s].astype(F32)
            second = second + part_in[8 + s].astype(F32)
        pooled = jnp.concatenate([first, second], axis=0)
        scaled = (pooled * anchor_g[...]).astype(BF)
        inverse = lax.rsqrt(jnp.mean(pooled * pooled, axis=1, keepdims=True) + EPS)
        key_lin = mm(scaled, key_w[...]) * inverse
        out_lin = mm(scaled, w_out[...]) * inverse
        low = lax.broadcasted_iota(jnp.int32, (16, 128), 1) < HEAD_DIM
        pieces = []
        for j in range(D // 128):
            piece = key_lin[:, 128 * j : 128 * j + 128]
            square = piece * piece
            first = jnp.sum(jnp.where(low, square, 0.0), axis=1, keepdims=True)
            second = jnp.sum(jnp.where(low, 0.0, square), axis=1, keepdims=True)
            pieces.append(piece * lax.rsqrt(jnp.where(low, first, second) * (1.0 / HEAD_DIM) + EPS))
        keys = jnp.concatenate(pieces, axis=1) * key_g[...]
        coarse = out_lin.astype(BF).astype(F32)
        mixed = jnp.where(lax.rem(lax.broadcasted_iota(jnp.int32, (16, 256), 1), 64) // 16 == 1, out_lin - coarse, coarse)
        for g in range(4):
            kv_out[g] = jnp.concatenate(
                [keys[:, width * g : width * g + width], mixed[:, 64 * g : 64 * g + 64]], axis=1
            ).astype(BF)
        pl.semaphore_wait(ready, 1)
        for i in range(len(others)):
            key_copy(i).start()
        kv_in[(c - 2) * 2 + xx] = kv_out[xx * 2 + y]

    embed_block(place)
    qwin_t[...] = qwin[...].T
    gain_t[...] = jnp.broadcast_to(query_g[:, pl.ds(start, pair)], (128, pair)).T

    for i, (dy, dx) in enumerate(quad):
        p_copies[i].wait_recv()
        embed_block(flip(y, dy) * 2 + flip(xx, dx))

    rows_mine = pl.ds(pl.multiple_of(y * width, 64), width)
    qlin[...] = mm(qwin_t[rows_mine, :], emb_t[...])
    gains = gain_t[rows_mine, :][:, 0:1]

    def norm_of(h):
        piece = qlin[h * HEAD_DIM : (h + 1) * HEAD_DIM, :]
        return lax.rsqrt(jnp.mean(piece * piece, axis=0, keepdims=True) + EPS)

    for h in range(heads):
        rows = slice(h * HEAD_DIM, (h + 1) * HEAD_DIM)
        hats[rows, :] = (qlin[rows, :] * norm_of(h) * gains[rows, :]).astype(BF)
    hats[width:, :] = jnp.zeros((256 - width, hats.shape[1]), BF)

    def keys_arrive(part_of, count):
        landed = kv_in.at[pl.ds(0, count)]
        copy_to(landed, landed, k_send.at[0], k_recv.at[part_of], {"cells": c, "ctx": x}).wait_recv()

    scale = HEAD_DIM ** (-0.5)
    lane = lax.broadcasted_iota(jnp.int32, (64, 128), 1)
    queries = qlin.shape[1]

    def attend(part_of, spot):
        found = jnp.concatenate([kv_in[part_of * 4 + s].astype(F32) for s in range(4)], axis=0)
        tile0, tile1 = found[:, :128], found[:, 128:]
        lefts = [
            jnp.where(lane < HEAD_DIM, tile0, 0.0).astype(BF),
            jnp.where(lane >= HEAD_DIM, tile0, 0.0).astype(BF),
            jnp.where(lane < HEAD_DIM, tile1, 0.0).astype(BF),
        ]
        out_cols = tile1.astype(BF).T[64:96, :]
        tops, outs = [], []
        for h in range(heads):
            exponent = jnp.exp2(
                mm(lefts[h], hats[(h // 2) * 128 : (h // 2) * 128 + 128, :]) * (scale * math.log2(math.e))
            )
            probs[h, spot : spot + 64, :] = exponent
            tops.append(jnp.sum(exponent, axis=0, keepdims=True))
            both_outs = mm(out_cols, exponent.astype(BF))
            outs.append(both_outs[:16] + both_outs[16:])
        return found, tops, outs

    @pl.when(is_owner)
    def _():
        keys_arrive(half, 3)

    @pl.when(jnp.logical_not(is_owner))
    def _():
        keys_arrive(half, 4)

    near_f, near_tops, near_outs = attend(half, 0)
    keys_arrive(1 - half, 4)
    far_f, far_tops, far_outs = attend(1 - half, 64)
    out_row = lax.broadcasted_iota(jnp.int32, (16, queries), 0) // 4
    by_head = jnp.zeros((16, queries), F32)
    shares = []
    for h in range(heads):
        shares.append(1.0 / (near_tops[h] + far_tops[h]))
        by_head = jnp.where(out_row == h, (near_outs[h] + far_outs[h]) * shares[h], by_head)
    pred_part[0] = by_head[0:4] + by_head[4:8] + by_head[8:12]
    o_copies = []
    for i, (dy, dx) in enumerate(quad):
        o_copies.append(
            copy_to(pred_part.at[0], pred_part.at[1 + i], o_send.at[i], o_recv.at[i], device(0, dy, dx, 0))
        )
        o_copies[i].start()

    for i in range(3):
        pool_copy(i).wait_send()

    @pl.when(jnp.logical_not(is_owner))
    def _():
        pool_copy(3).wait_send()

    @pl.when(is_owner)
    def _():
        for i in range(len(others)):
            key_copy(i).wait_send()

    for copy in p_copies:
        copy.wait_send()
    for h in range(heads):
        probs[h] = probs[h] * shares[h]
    goals = jnp.concatenate([both_all[i, 4:8, :] for i in range(4)], axis=1)
    both_f = jnp.concatenate([near_f, far_f], axis=0)
    both_t = both_f.astype(BF).T
    tile1 = both_f[:, 128:]
    lane = lax.broadcasted_iota(jnp.int32, tile1.shape, 1)
    backs = [
        jnp.where((lane >= 64) & (lax.rem(lane, 16) // 4 == h), tile1, 0.0).astype(BF) for h in range(heads)
    ]
    for h in range(heads):
        rows = slice(h * HEAD_DIM, (h + 1) * HEAD_DIM)
        inverse = norm_of(h)
        unit_rows = qlin[rows, :] * inverse
        unit[rows, :] = unit_rows
        wide[rows, :] = (gains[rows, :] * scale) * inverse
        lean[rows, :] = (gains[rows, :] * (scale / HEAD_DIM)) * (unit_rows * inverse)
    for copy in o_copies:
        copy.wait_recv()
    predicted = pred_part[0] + pred_part[1] + pred_part[2] + pred_part[3]
    residue = predicted - goals
    coarse = residue.astype(BF).astype(F32)
    rest = residue - coarse
    none = jnp.zeros((64, queries), F32)
    split = jnp.concatenate([none] + [coarse] * 8 + [rest] * 8, axis=0).astype(BF)
    weighed = by_head * jnp.concatenate([residue] * 4, axis=0)
    for h in range(heads):
        rows = slice(h * HEAD_DIM, (h + 1) * HEAD_DIM)
        inner = jnp.sum(weighed[4 * h : 4 * h + 4], axis=0, keepdims=True)
        grad_s = (probs[h] * (mm(backs[h], split) - inner)).astype(BF)
        grad_q = mm(both_t[rows, :], grad_s)
        shared = jnp.sum(grad_q * lean[rows, :], axis=0, keepdims=True)
        glin[rows, :] = (grad_q * wide[rows, :] - unit[rows, :] * shared).astype(BF)

    deep = D // 8
    tall = deep // 2
    middle = (z == 1) | (z == 2)
    places = [jnp.where(middle, a, b) for a, b in ((2, 3), (1, 2), (3, 1))]
    layers = [jnp.where(middle, far_z(a), far_z(b)) for a, b in ((2, 3), (1, 2), (3, 1))] + [z]

    def blocks(side, steps):
        slabs = [emb_t[pl.ds(pl.multiple_of((layers[j] * 2 + side) * deep, 16), deep), :] for j in steps]
        full = lax.dot_general(
            jnp.concatenate(slabs, axis=0), glin[...], (((1,), (1,)), ((), ())), preferred_element_type=F32
        )
        packed = {}
        for i, j in enumerate(steps):
            pieces = []
            for h in range(heads):
                piece = full[deep * i : deep * i + deep, HEAD_DIM * h : HEAD_DIM * h + HEAD_DIM]
                pieces.append(jnp.concatenate([piece[:tall], piece[tall:]], axis=1))
            packed[j] = jnp.concatenate(pieces, axis=0)
        return packed

    sent_blocks = blocks(1 - k, (0, 1, 2, 3))
    for j in range(4):
        y_send[j] = sent_blocks[j].astype(BF)
    to_mate = copy_to(y_send, y_in, g_send.at[4], g_recv.at[4], device(0, 0, 0, 1))
    to_mate.start()

    def along(j):
        slot = 0 if j == 3 else places[j]
        peer = {"cells": layers[j] * 2 + k, "ctx": xx * 2 + y}
        return copy_to(z_send.at[j], z_in.at[slot], g_send.at[j], g_recv.at[slot], peer)

    kept = blocks(k, (0,))
    to_mate.wait_recv()
    z_send[0] = (kept[0] + y_in[0].astype(F32)).astype(BF)
    along(0).start()
    kept = blocks(k, (1, 2, 3))
    for j in (1, 2):
        z_send[j] = (kept[j] + y_in[j].astype(F32)).astype(BF)
        along(j).start()
    near = kept[3] + y_in[3].astype(F32)
    total[...] = near

    @pl.when(y != k)
    def _():
        z_send[3] = near.astype(BF)
        along(3).start()

    cols = pl.ds(pl.multiple_of(place * q_dev, 128), q_dev)
    for copy in o_copies:
        copy.wait_send()
    pred_part[0] = predicted
    pred_out[...] = pred_part[0, :, cols]
    to_mate.wait_send()
    for j in range(3):
        along(j).wait_send()

    @pl.when(y != k)
    def _():
        along(3).wait_send()


    def arrived(slot):
        return copy_to(z_send.at[0], z_in.at[slot], g_send.at[0], g_recv.at[slot], device(0, 0, 0, 1))

    @pl.when(y != k)
    def _():
        arrived(0).wait_recv()
        total[...] = z_in[0].astype(F32)

    summed = total[...]
    for slot in (1, 2, 3):
        arrived(slot).wait_recv()
        summed = summed + z_in[slot].astype(F32)
    for h in range(heads):
        spot = slice(h * HEAD_DIM, (h + 1) * HEAD_DIM)
        grad_out[:tall, spot] = summed[tall * h : tall * h + tall, :HEAD_DIM]
        grad_out[tall:, spot] = summed[tall * h : tall * h + tall, HEAD_DIM:]

def finish(pred_in, grad_in, pred_o, grad_o):
    pred_o[...] = pred_in[...]
    grad_o[...] = grad_in[...]

def fused_device(
    cell_feats,
    cell_types,
    cell_routes,
    positions,
    targets,
    type_weight,
    query_weight,
    key_weight,
    out_weight,
    anchor_gain,
    query_gain,
    key_gain,
):
    width = D // 4
    cells = cell_feats.shape[1]
    q_dev = positions.shape[2]
    queries = 4 * q_dev
    outs = targets.shape[1]
    deep = D // 8
    vmem = pl.BlockSpec(memory_space=pltpu.VMEM)
    dma = pltpu.SemaphoreType.DMA
    predicted, grad = pl.pallas_call(
        fused_kernel,
        out_shape=(
            pltpu.VMEM((outs, q_dev), F32),
            pltpu.VMEM((deep, width), F32),
        ),
        in_specs=[pl.BlockSpec(memory_space=pltpu.HBM)] * 12,
        out_specs=(vmem, vmem),
        scratch_shapes=[
            pltpu.VMEM((cells, cell_feats.shape[2]), BF),
            pltpu.SMEM(cell_types.shape, jnp.int32),
            pltpu.VMEM((cell_routes.shape[2], cells), jnp.int32),
            pltpu.VMEM((3, 1, q_dev), F32),
            pltpu.VMEM((outs, q_dev), F32),
            pltpu.VMEM(type_weight.shape, BF),
            pltpu.VMEM((outs, D), BF),
            pltpu.VMEM((1, D), F32),
            pltpu.VMEM((1, D), F32),
            pltpu.VMEM((1, D), F32),
            pltpu.VMEM((D, D), BF),
            pltpu.VMEM((D, 2 * width), BF),
            pltpu.VMEM((2 * width, D), BF),
            pltpu.VMEM((2 * width, 128), F32),
            pltpu.VMEM((cells, D), BF),
            pltpu.VMEM((4, 8, D), F32),
            pltpu.VMEM((4, 8, D), BF),
            pltpu.VMEM((16, 8, D), BF),
            pltpu.VMEM((D, 256), BF),
            pltpu.VMEM((4, 16, 256), BF),
            pltpu.VMEM((8, 16, 256), BF),
            pltpu.VMEM((4, 8, q_dev), F32),
            pltpu.VMEM((4, outs, queries), F32),
            pltpu.VMEM((D, queries), BF),
            pltpu.VMEM((width, queries), F32),
            pltpu.VMEM((256, queries), BF),
            pltpu.VMEM((width, queries), F32),
            pltpu.VMEM((width, queries), F32),
            pltpu.VMEM((width, queries), F32),
            pltpu.VMEM((width // HEAD_DIM, 128, queries), F32),
            pltpu.VMEM((width, queries), BF),
            pltpu.VMEM((4, 3 * deep // 2, 128), BF),
            pltpu.VMEM((4, 3 * deep // 2, 128), BF),
            pltpu.VMEM((4, 3 * deep // 2, 128), BF),
            pltpu.VMEM((4, 3 * deep // 2, 128), BF),
            pltpu.VMEM((3 * deep // 2, 128), F32),
            dma((12,)),
            dma((4,)),
            dma((1,)),
            dma((3,)),
            dma((3,)),
            dma((31,)),
            dma((2,)),
            dma((3,)),
            dma((3,)),
            dma((5,)),
            dma((5,)),
            pltpu.SemaphoreType.REGULAR,
        ],
        compiler_params=pltpu.CompilerParams(
            collective_id=0, has_side_effects=True, vmem_limit_bytes=64 * 1024 * 1024 - 256 * 1024
        ),
    )(
        cell_feats[0],
        cell_types,
        cell_routes[0].T,
        positions[0].reshape(3, 1, q_dev),
        targets[0],
        type_weight,
        query_weight,
        key_weight,
        out_weight.T,
        anchor_gain,
        query_gain,
        key_gain,
    )
    predicted, grad = pl.pallas_call(
        finish,
        out_shape=(jax.ShapeDtypeStruct((outs, q_dev), F32), jax.ShapeDtypeStruct((deep, width), F32)),
        in_specs=[vmem, vmem],
        out_specs=(vmem, vmem),
        compiler_params=pltpu.CompilerParams(vmem_limit_bytes=1024 * 1024),
    )(predicted, grad)
    return (predicted[None], grad)


def solution(mesh):
    in_specs = (
        P(("groups", "dp"), ("cells", "ctx"), None),
        P(("groups", "dp"), ("cells", "ctx")),
        P(("groups", "dp"), ("cells", "ctx"), None),
        P(("groups", "dp"), None, ("cells", "ctx")),
        P(("groups", "dp"), None, ("cells", "ctx")),
        P(),
        P(),
        P(),
        P(),
        P(),
        P(),
        P(),
    )
    out_specs = (P(("groups", "dp"), None, ("cells", "ctx")), P(("groups", "cells"), ("ctx", "dp")))
    sizes = mesh.shape
    fits = sizes["groups"] == 1 and sizes["dp"] == 1 and sizes["ctx"] == 4 and sizes["cells"] == 8
    body = fused_device if fits else general_device
    return jax.shard_map(
        body, mesh=mesh, in_specs=in_specs, out_specs=out_specs, check_vma=False
    )
```

```python
import functools
import math

import jax
import jax.numpy as jnp
from jax import lax
from jax.experimental import pallas as pl
from jax.experimental.pallas import tpu as pltpu
from jax.sharding import PartitionSpec as P

D = 768
HEAD_DIM = 64
SN_DEV = 4
FREQ = 128


EPS = 1e-06


def head_norm(values):
    shaped = values.reshape(values.shape[:-1] + (values.shape[-1] // HEAD_DIM, HEAD_DIM))
    inverse = lax.rsqrt(jnp.mean(shaped * shaped, axis=-1, keepdims=True) + EPS)
    return (shaped * inverse).reshape(values.shape)


def embed_positions(coords):
    freq_ids = jnp.arange(FREQ, dtype=jnp.float32)
    rate_table = math.pi * jnp.exp2(freq_ids * (6.0 / FREQ))
    angles = jnp.transpose(coords)[:, :, None] * rate_table[None, None, :]
    sin_cos = jnp.stack([jnp.sin(angles), jnp.cos(angles)], axis=2)
    return sin_cos.reshape(coords.shape[1], 6 * FREQ).astype(jnp.bfloat16)


def cell_embed(cell_rows, type_ids, type_weight):
    row_count = cell_rows.shape[0]
    per_block = row_count // type_ids.shape[0]
    shaped = cell_rows.reshape(type_ids.shape[0], per_block, cell_rows.shape[1])
    chosen = type_weight[0][None]
    for type_id in range(1, type_weight.shape[0]):
        chosen = jnp.where((type_ids == type_id)[:, None, None], type_weight[type_id][None], chosen)
    pre_act = jnp.einsum("bnf,bfd->bnd", shaped, chosen, preferred_element_type=jnp.float32)
    return jnp.tanh(pre_act).astype(jnp.bfloat16).reshape(row_count, -1)


def make_keys(anchors, key_weight, key_gain):
    key_lin = jnp.dot(anchors, key_weight, preferred_element_type=jnp.float32)
    return (head_norm(key_lin) * key_gain).astype(jnp.bfloat16)


def general_device(
    cell_feats,
    cell_types,
    cell_routes,
    positions,
    targets,
    type_weight,
    query_weight,
    key_weight,
    out_weight,
    anchor_gain,
    query_gain,
    key_gain,
):
    slab_count = lax.axis_size("cells")
    column_count = lax.axis_size("ctx")
    cell_rows = cell_feats[0]
    type_ids = cell_types[0]
    routes = cell_routes[0]
    embedded = cell_embed(cell_rows, type_ids, type_weight)
    slots = jnp.arange(slab_count * SN_DEV, dtype=jnp.int32)
    owned = (slots // SN_DEV * column_count + lax.axis_index("ctx")) * SN_DEV + slots % SN_DEV
    table = jnp.sum((routes[None, :, :] == owned[:, None, None]).astype(jnp.int32), axis=2)
    partial = jnp.dot(table.astype(jnp.bfloat16), embedded, preferred_element_type=jnp.float32)
    pooled = lax.psum_scatter(partial, "cells", scatter_dimension=0, tiled=True)
    inverse = lax.rsqrt(jnp.mean(pooled * pooled, axis=-1, keepdims=True) + EPS)
    anchors = (pooled * inverse * anchor_gain).astype(jnp.bfloat16)
    own_keys = make_keys(anchors, key_weight, key_gain)
    all_keys, all_anchors = (
        lax.all_gather(own_keys, ("cells", "ctx"), axis=0, tiled=True),
        lax.all_gather(anchors, ("cells", "ctx"), axis=0, tiled=True),
    )
    embed = embed_positions(positions[0])
    query_lin = jnp.dot(embed, query_weight, preferred_element_type=jnp.float32)
    query_hat = (head_norm(query_lin) * query_gain).astype(jnp.bfloat16)
    query_count = embed.shape[0]
    head_count = D // HEAD_DIM
    group_size = 4
    score_scale = HEAD_DIM ** (-0.5)
    query_heads = query_hat.reshape(query_count, head_count, HEAD_DIM)
    key_heads = all_keys.reshape(-1, head_count, HEAD_DIM)
    value_heads = all_anchors.reshape(-1, head_count, HEAD_DIM)
    probs_saved = []
    outputs = []
    for first_head in range(0, head_count, group_size):
        last_head = first_head + group_size
        scores = (
            jnp.einsum(
                "qhd,khd->hqk",
                query_heads[:, first_head:last_head],
                key_heads[:, first_head:last_head],
                preferred_element_type=jnp.float32,
            )
            * score_scale
        )
        exponent = jnp.exp(scores)
        probs_f32 = exponent / jnp.sum(exponent, axis=-1, keepdims=True)
        probs_saved.append(probs_f32)
        outputs.append(
            jnp.einsum(
                "hqk,khd->qhd",
                probs_f32.astype(jnp.bfloat16),
                value_heads[:, first_head:last_head],
                preferred_element_type=jnp.float32,
            )
        )
    attended = jnp.concatenate(outputs, axis=1).reshape(query_count, D).astype(jnp.bfloat16)
    predicted = lax.dot_general(
        out_weight, attended, (((0,), (1,)), ((), ())), preferred_element_type=jnp.float32
    )
    residue = predicted - targets[0]
    grad_attended = lax.dot_general(
        residue,
        out_weight.astype(jnp.float32),
        (((0,), (1,)), ((), ())),
        precision=lax.Precision.HIGHEST,
    ).astype(jnp.bfloat16)
    grad_heads = grad_attended.reshape(query_count, head_count, HEAD_DIM)
    pieces = []
    for group_index, first_head in enumerate(range(0, head_count, group_size)):
        last_head = first_head + group_size
        probs_f32 = probs_saved[group_index]
        grad_weights = jnp.einsum(
            "qhd,khd->hqk",
            grad_heads[:, first_head:last_head],
            value_heads[:, first_head:last_head],
            preferred_element_type=jnp.float32,
        )
        grad_scores = probs_f32 * (
            grad_weights - jnp.sum(probs_f32 * grad_weights, axis=-1, keepdims=True)
        )
        pieces.append(
            jnp.einsum(
                "hqk,khd->qhd",
                grad_scores.astype(jnp.bfloat16),
                key_heads[:, first_head:last_head],
                preferred_element_type=jnp.float32,
            )
            * score_scale
        )
    grad_qhat = jnp.concatenate(pieces, axis=1).reshape(query_count, D)
    weighted = (grad_qhat * query_gain).reshape(query_count, head_count, HEAD_DIM)
    shaped = query_lin.reshape(query_count, head_count, HEAD_DIM)
    norm_inverse = lax.rsqrt(jnp.mean(shaped * shaped, axis=-1, keepdims=True) + EPS)
    unit_rows = shaped * norm_inverse
    grad_qlin = (
        (
            (weighted - unit_rows * jnp.mean(weighted * unit_rows, axis=-1, keepdims=True))
            * norm_inverse
        )
        .reshape(query_count, D)
        .astype(jnp.bfloat16)
    )
    summed = lax.psum_scatter(
        lax.dot_general(
            embed, grad_qlin, (((0,), (0,)), ((), ())), preferred_element_type=jnp.float32
        ),
        "cells",
        scatter_dimension=0,
        tiled=True,
    )
    grad_query = lax.psum_scatter(summed, ("ctx", "dp"), scatter_dimension=1, tiled=True)
    return (predicted[None], grad_query)


BF = jnp.bfloat16
F32 = jnp.float32
MESH = pl.DeviceIdType.MESH
SIN_TERMS = [math.pi ** n * (-1) ** (n // 2) / math.factorial(n) for n in (1, 3, 5, 7, 9, 11, 13)]
COS_TERMS = [math.pi ** n * (-1) ** (n // 2) / math.factorial(n) for n in (0, 2, 4, 6, 8, 10, 12)]


def mm(a, b):
    return jnp.dot(a, b, preferred_element_type=F32)


def series(terms, square):
    total = jnp.full_like(square, terms[-1])
    for term in terms[-2::-1]:
        total = total * square + term
    return total


def rate_table():
    ids = lax.broadcasted_iota(jnp.int32, (FREQ, FREQ), 0)
    rates = jnp.ones((FREQ, FREQ), F32)
    for bit in range(FREQ.bit_length() - 1):
        rates = rates * jnp.where((ids & (1 << bit)) != 0, 2.0 ** (6.0 * (1 << bit) / FREQ), 1.0).astype(F32)
    return rates


def fused_kernel(
    feats_h,
    types_h,
    routes_h,
    pos_h,
    tgt_h,
    type_w_h,
    query_w,
    key_w_h,
    out_wt_h,
    anchor_g_h,
    query_g_h,
    key_g_h,
    pred_out,
    grad_out,
    feats,
    types,
    routes,
    pos,
    tgt,
    type_w,
    out_wt,
    anchor_g,
    query_g,
    key_g,
    key_w,
    qwin,
    qwin_t,
    gain_t,
    emb,
    part,
    part_b,
    part_in,
    w_out,
    kv_out,
    kv_in,
    both_all,
    pred_part,
    emb_t,
    qlin,
    hats,
    unit,
    wide,
    lean,
    probs,
    glin,
    y_send,
    y_in,
    z_send,
    z_in,
    total,
    local_sem,
    a_send,
    a_recv,
    p_send,
    p_recv,
    k_send,
    k_recv,
    o_send,
    o_recv,
    g_send,
    g_recv,
    ready,
):
    c = lax.axis_index("cells")
    x = lax.axis_index("ctx")
    z, y = c // 2, lax.rem(c, 2)
    xx, k = x // 2, lax.rem(x, 2)
    width = D // 4
    pair = 2 * width
    heads = width // HEAD_DIM
    odd = y == 1
    start = pl.multiple_of(xx * pair, 128)
    q_dev = pos.shape[-1]
    place = y * 2 + xx

    def flip(value, on):
        return 1 - value if on else value

    def far_z(m):
        return flip(z // 2, m // 2) * 2 + flip(lax.rem(z, 2), m % 2)

    def device(m, dy, dx, dk):
        return {"cells": far_z(m) * 2 + flip(y, dy), "ctx": flip(xx, dx) * 2 + flip(k, dk)}

    others = [(m, dy, dx, dk) for m in (3, 2, 1, 0) for dy in (1, 0) for dx in (1, 0) for dk in (1, 0)][:-1]

    loads = [
        pltpu.make_async_copy(src, dst, local_sem.at[i])
        for i, (src, dst) in enumerate(
            (
                (types_h, types),
                (routes_h, routes),
                (feats_h, feats),
                (type_w_h, type_w),
                (pos_h, pos),
                (tgt_h, tgt),
                (out_wt_h, out_wt),
                (anchor_g_h, anchor_g.at[0]),
                (query_g_h, query_g.at[0]),
                (key_g_h, key_g.at[0]),
                (query_w.at[:, pl.ds(start, pair)], qwin),
                (key_w_h, key_w),
            )
        )
    ]
    for load in loads[:4]:
        load.start()
    barrier = pltpu.get_barrier_semaphore()
    half = z // 2
    is_owner = (c >= 2) & (c < 6) & (k == 1)

    def greet(peer):
        pl.semaphore_signal(barrier, inc=1, device_id=peer, device_id_type=MESH)

    def owner_at(dh, dy):
        return flip(half, dh) * 2 + flip(y, dy)

    @pl.when(is_owner)
    def _():
        for m in (2, 3, 1, 0):
            for dy in (1, 0):
                for dk in (1, 0):
                    if m or dy or dk:
                        greet(device(m, dy, 0, dk))

    @pl.when(jnp.logical_not(is_owner))
    def _():
        for dh, dy in ((1, 1), (1, 0), (0, 1), (0, 0)):
            greet({"cells": 2 + owner_at(dh, dy), "ctx": xx * 2 + 1})

    for dy, dx in ((1, 1), (1, 0), (0, 1)):
        greet(device(0, dy, dx, 0))

    for load in loads[4:]:
        load.start()

    def own(values):
        return jnp.where(odd, values[:, width:], values[:, :width])

    def copy_to(src, dst, send_sem, recv_sem, peer):
        return pltpu.make_async_remote_copy(
            src_ref=src, dst_ref=dst, send_sem=send_sem, recv_sem=recv_sem, device_id=peer, device_id_type=MESH
        )

    loads[1].wait()
    row = lax.broadcasted_iota(jnp.int32, (4 * 8, feats.shape[0]), 0)
    slab = ((row // 16) * 2 + lax.rem(row, 8) // 4) * 2 + lax.rem(row // 8, 2)
    label = (slab * 4 + x) * SN_DEV + lax.rem(row, 4)
    table = (
        jnp.where(routes[0:1, :] == label, 1.0, 0.0) + jnp.where(routes[1:2, :] == label, 1.0, 0.0)
    ).astype(BF)
    for i in (0, 2, 3):
        loads[i].wait()
    block = feats.shape[0] // types.shape[1]
    for b in range(types.shape[1]):
        pre = mm(feats[b * block : (b + 1) * block, :], type_w[types[0, b]])
        emb[b * block : (b + 1) * block, :] = jnp.tanh(pre).astype(BF)
    sums = mm(table, emb[...])
    for o in range(4):
        part[o] = sums[8 * o : 8 * o + 8, :]
        part_b[o] = sums[8 * o : 8 * o + 8, :].astype(BF)

    def pool_copy(i):
        dh, dy = ((1, 1), (1, 0), (0, 1), (0, 0))[i]
        o = owner_at(dh, dy)
        return copy_to(
            part_b.at[o],
            part_in.at[k * 8 + lax.rem(c - (2 + o) + 8, 8)],
            a_send.at[i],
            a_recv.at[0],
            {"cells": 2 + o, "ctx": xx * 2 + 1},
        )

    pl.semaphore_wait(barrier, 3 + jnp.where(is_owner, 15, 4))
    for i in range(3):
        pool_copy(i).start()

    @pl.when(jnp.logical_not(is_owner))
    def _():
        pool_copy(3).start()

    @pl.when(is_owner)
    def _():
        pl.semaphore_signal(ready, inc=1, device_id=device(0, 0, 1, 0), device_id_type=MESH)

    loads[4].wait()
    loads[5].wait()
    both_all[place, 0:3, :] = pos[:, 0, :]
    both_all[place, 4:8, :] = tgt[...]
    p_copies = []
    quad = ((1, 1), (1, 0), (0, 1))
    for i, (dy, dx) in enumerate(quad):
        mine = both_all.at[place]
        p_copies.append(copy_to(mine, mine, p_send.at[i], p_recv.at[i], device(0, dy, dx, 0)))
        p_copies[i].start()

    for load in loads[6:]:
        load.wait()
    rates = rate_table()

    def embed_block(i):
        cols = pl.ds(pl.multiple_of(i * q_dev, 128), q_dev)
        for d in range(3):
            turns = rates * both_all[i, pl.ds(d, 1), :]
            whole = jnp.floor(turns + 0.5)
            rest = turns - whole
            parity = whole * 0.5
            sign = 1.0 - 4.0 * (parity - jnp.floor(parity))
            square = rest * rest
            spot = (2 * d) * FREQ
            emb_t[spot : spot + FREQ, cols] = (series(SIN_TERMS, square) * rest * sign).astype(BF)
            emb_t[spot + FREQ : spot + 2 * FREQ, cols] = (series(COS_TERMS, square) * sign).astype(BF)

    out_f = out_wt[...].astype(F32)
    out_t = jnp.concatenate([out_f, jnp.zeros_like(out_f)], axis=0).T.astype(BF)
    lane8 = lax.broadcasted_iota(jnp.int32, (8, 256), 1)
    pick = jnp.where(lax.rem(lane8, 4) == lax.broadcasted_iota(jnp.int32, (8, 256), 0), 1.0, 0.0).astype(BF)
    lane_d = lax.broadcasted_iota(jnp.int32, (D, 256), 1)
    inside = lax.rem(lane_d, 16) // 4
    head_of = (lane_d // 64) * heads + inside
    keep = (lax.broadcasted_iota(jnp.int32, (D, 256), 0) // HEAD_DIM == head_of) & (inside < heads)
    keep = keep & (lax.rem(lane_d, 64) < 48)
    w_out[...] = jnp.where(keep, mm(out_t, pick), 0.0).astype(BF)

    by_hops = sorted(others, key=lambda spot: -((0, 1, 2, 1)[spot[0]] * 2 + spot[1] * 2 + spot[2] * 2 + spot[3]))

    def key_copy(i):
        m, dy, dx, dk = by_hops[i]
        group = flip(xx, dx) * 2 + flip(y, dy)
        return copy_to(
            kv_out.at[group],
            kv_in.at[(c - 2) * 2 + xx],
            k_send.at[i],
            k_recv.at[half],
            device(m, dy, dx, dk),
        )

    @pl.when(is_owner)
    def _():
        arrived = part_in.at[pl.ds(0, 15)]
        copy_to(arrived, arrived, a_send.at[0], a_recv.at[0], {"cells": c, "ctx": x}).wait_recv()
        first, second = part_in[0].astype(F32), part[c - 2]
        for s in range(1, 8):
            first = first + part_in[s].astype(F32)
            second = second + part_in[8 + s].astype(F32)
        pooled = jnp.concatenate([first, second], axis=0)
        scaled = (pooled * anchor_g[...]).astype(BF)
        inverse = lax.rsqrt(jnp.mean(pooled * pooled, axis=1, keepdims=True) + EPS)
        key_lin = mm(scaled, key_w[...]) * inverse
        out_lin = mm(scaled, w_out[...]) * inverse
        low = lax.broadcasted_iota(jnp.int32, (16, 128), 1) < HEAD_DIM
        pieces = []
        for j in range(D // 128):
            piece = key_lin[:, 128 * j : 128 * j + 128]
            square = piece * piece
            first = jnp.sum(jnp.where(low, square, 0.0), axis=1, keepdims=True)
            second = jnp.sum(jnp.where(low, 0.0, square), axis=1, keepdims=True)
            pieces.append(piece * lax.rsqrt(jnp.where(low, first, second) * (1.0 / HEAD_DIM) + EPS))
        keys = jnp.concatenate(pieces, axis=1) * key_g[...]
        coarse = out_lin.astype(BF).astype(F32)
        mixed = jnp.where(lax.rem(lax.broadcasted_iota(jnp.int32, (16, 256), 1), 64) // 16 == 1, out_lin - coarse, coarse)
        for g in range(4):
            kv_out[g] = jnp.concatenate(
                [keys[:, width * g : width * g + width], mixed[:, 64 * g : 64 * g + 64]], axis=1
            ).astype(BF)
        pl.semaphore_wait(ready, 1)
        for i in range(len(others)):
            key_copy(i).start()
        kv_in[(c - 2) * 2 + xx] = kv_out[xx * 2 + y]

    embed_block(place)
    qwin_t[...] = qwin[...].T
    gain_t[...] = jnp.broadcast_to(query_g[:, pl.ds(start, pair)], (128, pair)).T

    for i, (dy, dx) in enumerate(quad):
        p_copies[i].wait_recv()
        embed_block(flip(y, dy) * 2 + flip(xx, dx))

    rows_mine = pl.ds(pl.multiple_of(y * width, 64), width)
    qlin[...] = mm(qwin_t[rows_mine, :], emb_t[...])
    gains = gain_t[rows_mine, :][:, 0:1]

    def norm_of(h):
        piece = qlin[h * HEAD_DIM : (h + 1) * HEAD_DIM, :]
        return lax.rsqrt(jnp.mean(piece * piece, axis=0, keepdims=True) + EPS)

    for h in range(heads):
        rows = slice(h * HEAD_DIM, (h + 1) * HEAD_DIM)
        hats[rows, :] = (qlin[rows, :] * norm_of(h) * gains[rows, :]).astype(BF)
    hats[width:, :] = jnp.zeros((256 - width, hats.shape[1]), BF)

    def keys_arrive(part_of, count):
        landed = kv_in.at[pl.ds(0, count)]
        copy_to(landed, landed, k_send.at[0], k_recv.at[part_of], {"cells": c, "ctx": x}).wait_recv()

    scale = HEAD_DIM ** (-0.5)
    lane = lax.broadcasted_iota(jnp.int32, (64, 128), 1)
    queries = qlin.shape[1]

    def attend(part_of, spot):
        found = jnp.concatenate([kv_in[part_of * 4 + s].astype(F32) for s in range(4)], axis=0)
        tile0, tile1 = found[:, :128], found[:, 128:]
        lefts = [
            jnp.where(lane < HEAD_DIM, tile0, 0.0).astype(BF),
            jnp.where(lane >= HEAD_DIM, tile0, 0.0).astype(BF),
            jnp.where(lane < HEAD_DIM, tile1, 0.0).astype(BF),
        ]
        out_cols = tile1.astype(BF).T[64:96, :]
        tops, outs = [], []
        for h in range(heads):
            exponent = jnp.exp2(
                mm(lefts[h], hats[(h // 2) * 128 : (h // 2) * 128 + 128, :]) * (scale * math.log2(math.e))
            )
            probs[h, spot : spot + 64, :] = exponent
            tops.append(jnp.sum(exponent, axis=0, keepdims=True))
            both_outs = mm(out_cols, exponent.astype(BF))
            outs.append(both_outs[:16] + both_outs[16:])
        return found, tops, outs

    @pl.when(is_owner)
    def _():
        keys_arrive(half, 3)

    @pl.when(jnp.logical_not(is_owner))
    def _():
        keys_arrive(half, 4)

    near_f, near_tops, near_outs = attend(half, 0)
    keys_arrive(1 - half, 4)
    far_f, far_tops, far_outs = attend(1 - half, 64)
    out_row = lax.broadcasted_iota(jnp.int32, (16, queries), 0) // 4
    by_head = jnp.zeros((16, queries), F32)
    shares = []
    for h in range(heads):
        shares.append(1.0 / (near_tops[h] + far_tops[h]))
        by_head = jnp.where(out_row == h, (near_outs[h] + far_outs[h]) * shares[h], by_head)
    pred_part[0] = by_head[0:4] + by_head[4:8] + by_head[8:12]
    o_copies = []
    for i, (dy, dx) in enumerate(quad):
        o_copies.append(
            copy_to(pred_part.at[0], pred_part.at[1 + i], o_send.at[i], o_recv.at[i], device(0, dy, dx, 0))
        )
        o_copies[i].start()

    for i in range(3):
        pool_copy(i).wait_send()

    @pl.when(jnp.logical_not(is_owner))
    def _():
        pool_copy(3).wait_send()

    @pl.when(is_owner)
    def _():
        for i in range(len(others)):
            key_copy(i).wait_send()

    for copy in p_copies:
        copy.wait_send()
    for h in range(heads):
        probs[h] = probs[h] * shares[h]
    goals = jnp.concatenate([both_all[i, 4:8, :] for i in range(4)], axis=1)
    both_f = jnp.concatenate([near_f, far_f], axis=0)
    both_t = both_f.astype(BF).T
    tile1 = both_f[:, 128:]
    lane = lax.broadcasted_iota(jnp.int32, tile1.shape, 1)
    backs = [
        jnp.where((lane >= 64) & (lax.rem(lane, 16) // 4 == h), tile1, 0.0).astype(BF) for h in range(heads)
    ]
    for h in range(heads):
        rows = slice(h * HEAD_DIM, (h + 1) * HEAD_DIM)
        inverse = norm_of(h)
        unit_rows = qlin[rows, :] * inverse
        unit[rows, :] = unit_rows
        wide[rows, :] = (gains[rows, :] * scale) * inverse
        lean[rows, :] = (gains[rows, :] * (scale / HEAD_DIM)) * (unit_rows * inverse)
    for copy in o_copies:
        copy.wait_recv()
    predicted = pred_part[0] + pred_part[1] + pred_part[2] + pred_part[3]
    residue = predicted - goals
    coarse = residue.astype(BF).astype(F32)
    rest = residue - coarse
    none = jnp.zeros((64, queries), F32)
    split = jnp.concatenate([none] + [coarse] * 8 + [rest] * 8, axis=0).astype(BF)
    weighed = by_head * jnp.concatenate([residue] * 4, axis=0)
    for h in range(heads):
        rows = slice(h * HEAD_DIM, (h + 1) * HEAD_DIM)
        inner = jnp.sum(weighed[4 * h : 4 * h + 4], axis=0, keepdims=True)
        grad_s = (probs[h] * (mm(backs[h], split) - inner)).astype(BF)
        grad_q = mm(both_t[rows, :], grad_s)
        shared = jnp.sum(grad_q * lean[rows, :], axis=0, keepdims=True)
        glin[rows, :] = (grad_q * wide[rows, :] - unit[rows, :] * shared).astype(BF)

    deep = D // 8
    tall = deep // 2
    middle = (z == 1) | (z == 2)
    places = [jnp.where(middle, a, b) for a, b in ((2, 3), (1, 2), (3, 1))]
    layers = [jnp.where(middle, far_z(a), far_z(b)) for a, b in ((2, 3), (1, 2), (3, 1))] + [z]

    def blocks(side, steps):
        slabs = [emb_t[pl.ds(pl.multiple_of((layers[j] * 2 + side) * deep, 16), deep), :] for j in steps]
        full = lax.dot_general(
            jnp.concatenate(slabs, axis=0), glin[...], (((1,), (1,)), ((), ())), preferred_element_type=F32
        )
        packed = {}
        for i, j in enumerate(steps):
            pieces = []
            for h in range(heads):
                piece = full[deep * i : deep * i + deep, HEAD_DIM * h : HEAD_DIM * h + HEAD_DIM]
                pieces.append(jnp.concatenate([piece[:tall], piece[tall:]], axis=1))
            packed[j] = jnp.concatenate(pieces, axis=0)
        return packed

    sent_blocks = blocks(1 - k, (0, 1, 2, 3))
    for j in range(4):
        y_send[j] = sent_blocks[j].astype(BF)
    to_mate = copy_to(y_send, y_in, g_send.at[4], g_recv.at[4], device(0, 0, 0, 1))
    to_mate.start()

    def along(j):
        slot = 0 if j == 3 else places[j]
        peer = {"cells": layers[j] * 2 + k, "ctx": xx * 2 + y}
        return copy_to(z_send.at[j], z_in.at[slot], g_send.at[j], g_recv.at[slot], peer)

    kept = blocks(k, (0,))
    to_mate.wait_recv()
    z_send[0] = (kept[0] + y_in[0].astype(F32)).astype(BF)
    along(0).start()
    kept = blocks(k, (1, 2, 3))
    for j in (1, 2):
        z_send[j] = (kept[j] + y_in[j].astype(F32)).astype(BF)
        along(j).start()
    near = kept[3] + y_in[3].astype(F32)
    total[...] = near

    @pl.when(y != k)
    def _():
        z_send[3] = near.astype(BF)
        along(3).start()

    cols = pl.ds(pl.multiple_of(place * q_dev, 128), q_dev)
    for copy in o_copies:
        copy.wait_send()
    pred_part[0] = predicted
    pred_out[...] = pred_part[0, :, cols]
    to_mate.wait_send()
    for j in range(3):
        along(j).wait_send()

    @pl.when(y != k)
    def _():
        along(3).wait_send()


    def arrived(slot):
        return copy_to(z_send.at[0], z_in.at[slot], g_send.at[0], g_recv.at[slot], device(0, 0, 0, 1))

    @pl.when(y != k)
    def _():
        arrived(0).wait_recv()
        total[...] = z_in[0].astype(F32)

    summed = total[...]
    for slot in (1, 2, 3):
        arrived(slot).wait_recv()
        summed = summed + z_in[slot].astype(F32)
    for h in range(heads):
        spot = slice(h * HEAD_DIM, (h + 1) * HEAD_DIM)
        grad_out[:tall, spot] = summed[tall * h : tall * h + tall, :HEAD_DIM]
        grad_out[tall:, spot] = summed[tall * h : tall * h + tall, HEAD_DIM:]

def finish(pred_in, grad_in, pred_o, grad_o):
    pred_o[...] = pred_in[...]
    grad_o[...] = grad_in[...]

def fused_device(
    cell_feats,
    cell_types,
    cell_routes,
    positions,
    targets,
    type_weight,
    query_weight,
    key_weight,
    out_weight,
    anchor_gain,
    query_gain,
    key_gain,
):
    width = D // 4
    cells = cell_feats.shape[1]
    q_dev = positions.shape[2]
    queries = 4 * q_dev
    outs = targets.shape[1]
    deep = D // 8
    vmem = pl.BlockSpec(memory_space=pltpu.VMEM)
    dma = pltpu.SemaphoreType.DMA
    predicted, grad = pl.pallas_call(
        fused_kernel,
        out_shape=(
            pltpu.VMEM((outs, q_dev), F32),
            pltpu.VMEM((deep, width), F32),
        ),
        in_specs=[pl.BlockSpec(memory_space=pltpu.HBM)] * 12,
        out_specs=(vmem, vmem),
        scratch_shapes=[
            pltpu.VMEM((cells, cell_feats.shape[2]), BF),
            pltpu.SMEM(cell_types.shape, jnp.int32),
            pltpu.VMEM((cell_routes.shape[2], cells), jnp.int32),
            pltpu.VMEM((3, 1, q_dev), F32),
            pltpu.VMEM((outs, q_dev), F32),
            pltpu.VMEM(type_weight.shape, BF),
            pltpu.VMEM((outs, D), BF),
            pltpu.VMEM((1, D), F32),
            pltpu.VMEM((1, D), F32),
            pltpu.VMEM((1, D), F32),
            pltpu.VMEM((D, D), BF),
            pltpu.VMEM((D, 2 * width), BF),
            pltpu.VMEM((2 * width, D), BF),
            pltpu.VMEM((2 * width, 128), F32),
            pltpu.VMEM((cells, D), BF),
            pltpu.VMEM((4, 8, D), F32),
            pltpu.VMEM((4, 8, D), BF),
            pltpu.VMEM((16, 8, D), BF),
            pltpu.VMEM((D, 256), BF),
            pltpu.VMEM((4, 16, 256), BF),
            pltpu.VMEM((8, 16, 256), BF),
            pltpu.VMEM((4, 8, q_dev), F32),
            pltpu.VMEM((4, outs, queries), F32),
            pltpu.VMEM((D, queries), BF),
            pltpu.VMEM((width, queries), F32),
            pltpu.VMEM((256, queries), BF),
            pltpu.VMEM((width, queries), F32),
            pltpu.VMEM((width, queries), F32),
            pltpu.VMEM((width, queries), F32),
            pltpu.VMEM((width // HEAD_DIM, 128, queries), F32),
            pltpu.VMEM((width, queries), BF),
            pltpu.VMEM((4, 3 * deep // 2, 128), BF),
            pltpu.VMEM((4, 3 * deep // 2, 128), BF),
            pltpu.VMEM((4, 3 * deep // 2, 128), BF),
            pltpu.VMEM((4, 3 * deep // 2, 128), BF),
            pltpu.VMEM((3 * deep // 2, 128), F32),
            dma((12,)),
            dma((4,)),
            dma((1,)),
            dma((3,)),
            dma((3,)),
            dma((31,)),
            dma((2,)),
            dma((3,)),
            dma((3,)),
            dma((5,)),
            dma((5,)),
            pltpu.SemaphoreType.REGULAR,
        ],
        compiler_params=pltpu.CompilerParams(
            collective_id=0, has_side_effects=True, vmem_limit_bytes=64 * 1024 * 1024 - 256 * 1024
        ),
    )(
        cell_feats[0],
        cell_types,
        cell_routes[0].T,
        positions[0].reshape(3, 1, q_dev),
        targets[0],
        type_weight,
        query_weight,
        key_weight,
        out_weight.T,
        anchor_gain,
        query_gain,
        key_gain,
    )
    predicted, grad = pl.pallas_call(
        finish,
        out_shape=(jax.ShapeDtypeStruct((outs, q_dev), F32), jax.ShapeDtypeStruct((deep, width), F32)),
        in_specs=[vmem, vmem],
        out_specs=(vmem, vmem),
        compiler_params=pltpu.CompilerParams(vmem_limit_bytes=1024 * 1024),
    )(predicted, grad)
    return (predicted[None], grad)


def solution(mesh):
    in_specs = (
        P(("groups", "dp"), ("cells", "ctx"), None),
        P(("groups", "dp"), ("cells", "ctx")),
        P(("groups", "dp"), ("cells", "ctx"), None),
        P(("groups", "dp"), None, ("cells", "ctx")),
        P(("groups", "dp"), None, ("cells", "ctx")),
        P(),
        P(),
        P(),
        P(),
        P(),
        P(),
        P(),
    )
    out_specs = (P(("groups", "dp"), None, ("cells", "ctx")), P(("groups", "cells"), ("ctx", "dp")))
    sizes = mesh.shape
    fits = sizes["groups"] == 1 and sizes["dp"] == 1 and sizes["ctx"] == 4 and sizes["cells"] == 8
    body = fused_device if fits else general_device
    return jax.shard_map(
        body, mesh=mesh, in_specs=in_specs, out_specs=out_specs, check_vma=False
    )
```

```python
import functools
import math

import jax
import jax.numpy as jnp
from jax import lax
from jax.experimental import pallas as pl
from jax.experimental.pallas import tpu as pltpu
from jax.sharding import PartitionSpec as P

D = 768
HEAD_DIM = 64
SN_DEV = 4
FREQ = 128


EPS = 1e-06


def head_norm(values):
    shaped = values.reshape(values.shape[:-1] + (values.shape[-1] // HEAD_DIM, HEAD_DIM))
    inverse = lax.rsqrt(jnp.mean(shaped * shaped, axis=-1, keepdims=True) + EPS)
    return (shaped * inverse).reshape(values.shape)


def embed_positions(coords):
    freq_ids = jnp.arange(FREQ, dtype=jnp.float32)
    rate_table = math.pi * jnp.exp2(freq_ids * (6.0 / FREQ))
    angles = jnp.transpose(coords)[:, :, None] * rate_table[None, None, :]
    sin_cos = jnp.stack([jnp.sin(angles), jnp.cos(angles)], axis=2)
    return sin_cos.reshape(coords.shape[1], 6 * FREQ).astype(jnp.bfloat16)


def cell_embed(cell_rows, type_ids, type_weight):
    row_count = cell_rows.shape[0]
    per_block = row_count // type_ids.shape[0]
    shaped = cell_rows.reshape(type_ids.shape[0], per_block, cell_rows.shape[1])
    chosen = type_weight[0][None]
    for type_id in range(1, type_weight.shape[0]):
        chosen = jnp.where((type_ids == type_id)[:, None, None], type_weight[type_id][None], chosen)
    pre_act = jnp.einsum("bnf,bfd->bnd", shaped, chosen, preferred_element_type=jnp.float32)
    return jnp.tanh(pre_act).astype(jnp.bfloat16).reshape(row_count, -1)


def make_keys(anchors, key_weight, key_gain):
    key_lin = jnp.dot(anchors, key_weight, preferred_element_type=jnp.float32)
    return (head_norm(key_lin) * key_gain).astype(jnp.bfloat16)


def general_device(
    cell_feats,
    cell_types,
    cell_routes,
    positions,
    targets,
    type_weight,
    query_weight,
    key_weight,
    out_weight,
    anchor_gain,
    query_gain,
    key_gain,
):
    slab_count = lax.axis_size("cells")
    column_count = lax.axis_size("ctx")
    cell_rows = cell_feats[0]
    type_ids = cell_types[0]
    routes = cell_routes[0]
    embedded = cell_embed(cell_rows, type_ids, type_weight)
    slots = jnp.arange(slab_count * SN_DEV, dtype=jnp.int32)
    owned = (slots // SN_DEV * column_count + lax.axis_index("ctx")) * SN_DEV + slots % SN_DEV
    table = jnp.sum((routes[None, :, :] == owned[:, None, None]).astype(jnp.int32), axis=2)
    partial = jnp.dot(table.astype(jnp.bfloat16), embedded, preferred_element_type=jnp.float32)
    pooled = lax.psum_scatter(partial, "cells", scatter_dimension=0, tiled=True)
    inverse = lax.rsqrt(jnp.mean(pooled * pooled, axis=-1, keepdims=True) + EPS)
    anchors = (pooled * inverse * anchor_gain).astype(jnp.bfloat16)
    own_keys = make_keys(anchors, key_weight, key_gain)
    all_keys, all_anchors = (
        lax.all_gather(own_keys, ("cells", "ctx"), axis=0, tiled=True),
        lax.all_gather(anchors, ("cells", "ctx"), axis=0, tiled=True),
    )
    embed = embed_positions(positions[0])
    query_lin = jnp.dot(embed, query_weight, preferred_element_type=jnp.float32)
    query_hat = (head_norm(query_lin) * query_gain).astype(jnp.bfloat16)
    query_count = embed.shape[0]
    head_count = D // HEAD_DIM
    group_size = 4
    score_scale = HEAD_DIM ** (-0.5)
    query_heads = query_hat.reshape(query_count, head_count, HEAD_DIM)
    key_heads = all_keys.reshape(-1, head_count, HEAD_DIM)
    value_heads = all_anchors.reshape(-1, head_count, HEAD_DIM)
    probs_saved = []
    outputs = []
    for first_head in range(0, head_count, group_size):
        last_head = first_head + group_size
        scores = (
            jnp.einsum(
                "qhd,khd->hqk",
                query_heads[:, first_head:last_head],
                key_heads[:, first_head:last_head],
                preferred_element_type=jnp.float32,
            )
            * score_scale
        )
        exponent = jnp.exp(scores)
        probs_f32 = exponent / jnp.sum(exponent, axis=-1, keepdims=True)
        probs_saved.append(probs_f32)
        outputs.append(
            jnp.einsum(
                "hqk,khd->qhd",
                probs_f32.astype(jnp.bfloat16),
                value_heads[:, first_head:last_head],
                preferred_element_type=jnp.float32,
            )
        )
    attended = jnp.concatenate(outputs, axis=1).reshape(query_count, D).astype(jnp.bfloat16)
    predicted = lax.dot_general(
        out_weight, attended, (((0,), (1,)), ((), ())), preferred_element_type=jnp.float32
    )
    residue = predicted - targets[0]
    grad_attended = lax.dot_general(
        residue,
        out_weight.astype(jnp.float32),
        (((0,), (1,)), ((), ())),
        precision=lax.Precision.HIGHEST,
    ).astype(jnp.bfloat16)
    grad_heads = grad_attended.reshape(query_count, head_count, HEAD_DIM)
    pieces = []
    for group_index, first_head in enumerate(range(0, head_count, group_size)):
        last_head = first_head + group_size
        probs_f32 = probs_saved[group_index]
        grad_weights = jnp.einsum(
            "qhd,khd->hqk",
            grad_heads[:, first_head:last_head],
            value_heads[:, first_head:last_head],
            preferred_element_type=jnp.float32,
        )
        grad_scores = probs_f32 * (
            grad_weights - jnp.sum(probs_f32 * grad_weights, axis=-1, keepdims=True)
        )
        pieces.append(
            jnp.einsum(
                "hqk,khd->qhd",
                grad_scores.astype(jnp.bfloat16),
                key_heads[:, first_head:last_head],
                preferred_element_type=jnp.float32,
            )
            * score_scale
        )
    grad_qhat = jnp.concatenate(pieces, axis=1).reshape(query_count, D)
    weighted = (grad_qhat * query_gain).reshape(query_count, head_count, HEAD_DIM)
    shaped = query_lin.reshape(query_count, head_count, HEAD_DIM)
    norm_inverse = lax.rsqrt(jnp.mean(shaped * shaped, axis=-1, keepdims=True) + EPS)
    unit_rows = shaped * norm_inverse
    grad_qlin = (
        (
            (weighted - unit_rows * jnp.mean(weighted * unit_rows, axis=-1, keepdims=True))
            * norm_inverse
        )
        .reshape(query_count, D)
        .astype(jnp.bfloat16)
    )
    summed = lax.psum_scatter(
        lax.dot_general(
            embed, grad_qlin, (((0,), (0,)), ((), ())), preferred_element_type=jnp.float32
        ),
        "cells",
        scatter_dimension=0,
        tiled=True,
    )
    grad_query = lax.psum_scatter(summed, ("ctx", "dp"), scatter_dimension=1, tiled=True)
    return (predicted[None], grad_query)


BF = jnp.bfloat16
F32 = jnp.float32
MESH = pl.DeviceIdType.MESH
SIN_TERMS = [math.pi ** n * (-1) ** (n // 2) / math.factorial(n) for n in (1, 3, 5, 7, 9, 11, 13)]
COS_TERMS = [math.pi ** n * (-1) ** (n // 2) / math.factorial(n) for n in (0, 2, 4, 6, 8, 10, 12)]


def mm(a, b):
    return jnp.dot(a, b, preferred_element_type=F32)


def series(terms, square):
    total = jnp.full_like(square, terms[-1])
    for term in terms[-2::-1]:
        total = total * square + term
    return total


def rate_table():
    ids = lax.broadcasted_iota(jnp.int32, (FREQ, FREQ), 0)
    rates = jnp.ones((FREQ, FREQ), F32)
    for bit in range(FREQ.bit_length() - 1):
        rates = rates * jnp.where((ids & (1 << bit)) != 0, 2.0 ** (6.0 * (1 << bit) / FREQ), 1.0).astype(F32)
    return rates


def fused_kernel(
    feats_h,
    types_h,
    routes_h,
    pos_h,
    tgt_h,
    type_w_h,
    query_w,
    key_w_h,
    out_wt_h,
    anchor_g_h,
    query_g_h,
    key_g_h,
    pred_out,
    grad_out,
    feats,
    types,
    routes,
    pos,
    tgt,
    type_w,
    out_wt,
    anchor_g,
    query_g,
    key_g,
    key_w,
    qwin,
    qwin_t,
    gain_t,
    emb,
    part,
    part_b,
    part_in,
    w_out,
    kv_out,
    kv_in,
    both_all,
    pred_part,
    emb_t,
    qlin,
    hats,
    unit,
    wide,
    lean,
    probs,
    glin,
    y_send,
    y_in,
    z_send,
    z_in,
    total,
    local_sem,
    a_send,
    a_recv,
    p_send,
    p_recv,
    k_send,
    k_recv,
    o_send,
    o_recv,
    g_send,
    g_recv,
    ready,
):
    c = lax.axis_index("cells")
    x = lax.axis_index("ctx")
    z, y = c // 2, lax.rem(c, 2)
    xx, k = x // 2, lax.rem(x, 2)
    width = D // 4
    pair = 2 * width
    heads = width // HEAD_DIM
    odd = y == 1
    start = pl.multiple_of(xx * pair, 128)
    q_dev = pos.shape[-1]
    place = y * 2 + xx

    def flip(value, on):
        return 1 - value if on else value

    def far_z(m):
        return flip(z // 2, m // 2) * 2 + flip(lax.rem(z, 2), m % 2)

    def device(m, dy, dx, dk):
        return {"cells": far_z(m) * 2 + flip(y, dy), "ctx": flip(xx, dx) * 2 + flip(k, dk)}

    others = [(m, dy, dx, dk) for m in (3, 2, 1, 0) for dy in (1, 0) for dx in (1, 0) for dk in (1, 0)][:-1]

    loads = [
        pltpu.make_async_copy(src, dst, local_sem.at[i])
        for i, (src, dst) in enumerate(
            (
                (types_h, types),
                (routes_h, routes),
                (feats_h, feats),
                (type_w_h, type_w),
                (pos_h, pos),
                (tgt_h, tgt),
                (out_wt_h, out_wt),
                (anchor_g_h, anchor_g.at[0]),
                (query_g_h, query_g.at[0]),
                (key_g_h, key_g.at[0]),
                (query_w.at[:, pl.ds(start, pair)], qwin),
                (key_w_h, key_w),
            )
        )
    ]
    for load in loads[:4]:
        load.start()
    barrier = pltpu.get_barrier_semaphore()
    half = z // 2
    is_owner = (c >= 2) & (c < 6) & (k == 1)

    def greet(peer):
        pl.semaphore_signal(barrier, inc=1, device_id=peer, device_id_type=MESH)

    def owner_at(dh, dy):
        return flip(half, dh) * 2 + flip(y, dy)

    @pl.when(is_owner)
    def _():
        for m in (2, 3, 1, 0):
            for dy in (1, 0):
                for dk in (1, 0):
                    if m or dy or dk:
                        greet(device(m, dy, 0, dk))

    @pl.when(jnp.logical_not(is_owner))
    def _():
        for dh, dy in ((1, 1), (1, 0), (0, 1), (0, 0)):
            greet({"cells": 2 + owner_at(dh, dy), "ctx": xx * 2 + 1})

    for dy, dx in ((1, 1), (1, 0), (0, 1)):
        greet(device(0, dy, dx, 0))

    for load in loads[4:]:
        load.start()

    def own(values):
        return jnp.where(odd, values[:, width:], values[:, :width])

    def copy_to(src, dst, send_sem, recv_sem, peer):
        return pltpu.make_async_remote_copy(
            src_ref=src, dst_ref=dst, send_sem=send_sem, recv_sem=recv_sem, device_id=peer, device_id_type=MESH
        )

    loads[1].wait()
    row = lax.broadcasted_iota(jnp.int32, (4 * 8, feats.shape[0]), 0)
    slab = ((row // 16) * 2 + lax.rem(row, 8) // 4) * 2 + lax.rem(row // 8, 2)
    label = (slab * 4 + x) * SN_DEV + lax.rem(row, 4)
    table = (
        jnp.where(routes[0:1, :] == label, 1.0, 0.0) + jnp.where(routes[1:2, :] == label, 1.0, 0.0)
    ).astype(BF)
    for i in (0, 2, 3):
        loads[i].wait()
    block = feats.shape[0] // types.shape[1]
    for b in range(types.shape[1]):
        pre = mm(feats[b * block : (b + 1) * block, :], type_w[types[0, b]])
        emb[b * block : (b + 1) * block, :] = jnp.tanh(pre).astype(BF)
    sums = mm(table, emb[...])
    for o in range(4):
        part[o] = sums[8 * o : 8 * o + 8, :]
        part_b[o] = sums[8 * o : 8 * o + 8, :].astype(BF)

    def pool_copy(i):
        dh, dy = ((1, 1), (1, 0), (0, 1), (0, 0))[i]
        o = owner_at(dh, dy)
        return copy_to(
            part_b.at[o],
            part_in.at[k * 8 + lax.rem(c - (2 + o) + 8, 8)],
            a_send.at[i],
            a_recv.at[0],
            {"cells": 2 + o, "ctx": xx * 2 + 1},
        )

    pl.semaphore_wait(barrier, 3 + jnp.where(is_owner, 15, 4))
    for i in range(3):
        pool_copy(i).start()

    @pl.when(jnp.logical_not(is_owner))
    def _():
        pool_copy(3).start()

    @pl.when(is_owner)
    def _():
        pl.semaphore_signal(ready, inc=1, device_id=device(0, 0, 1, 0), device_id_type=MESH)

    loads[4].wait()
    loads[5].wait()
    both_all[place, 0:3, :] = pos[:, 0, :]
    both_all[place, 4:8, :] = tgt[...]
    p_copies = []
    quad = ((1, 1), (1, 0), (0, 1))
    for i, (dy, dx) in enumerate(quad):
        mine = both_all.at[place]
        p_copies.append(copy_to(mine, mine, p_send.at[i], p_recv.at[i], device(0, dy, dx, 0)))
        p_copies[i].start()

    for load in loads[6:]:
        load.wait()
    rates = rate_table()

    def embed_block(i):
        cols = pl.ds(pl.multiple_of(i * q_dev, 128), q_dev)
        for d in range(3):
            turns = rates * both_all[i, pl.ds(d, 1), :]
            whole = jnp.floor(turns + 0.5)
            rest = turns - whole
            parity = whole * 0.5
            sign = 1.0 - 4.0 * (parity - jnp.floor(parity))
            square = rest * rest
            spot = (2 * d) * FREQ
            emb_t[spot : spot + FREQ, cols] = (series(SIN_TERMS, square) * rest * sign).astype(BF)
            emb_t[spot + FREQ : spot + 2 * FREQ, cols] = (series(COS_TERMS, square) * sign).astype(BF)

    out_f = out_wt[...].astype(F32)
    out_t = jnp.concatenate([out_f, jnp.zeros_like(out_f)], axis=0).T.astype(BF)
    lane8 = lax.broadcasted_iota(jnp.int32, (8, 256), 1)
    pick = jnp.where(lax.rem(lane8, 4) == lax.broadcasted_iota(jnp.int32, (8, 256), 0), 1.0, 0.0).astype(BF)
    lane_d = lax.broadcasted_iota(jnp.int32, (D, 256), 1)
    inside = lax.rem(lane_d, 16) // 4
    head_of = (lane_d // 64) * heads + inside
    keep = (lax.broadcasted_iota(jnp.int32, (D, 256), 0) // HEAD_DIM == head_of) & (inside < heads)
    keep = keep & (lax.rem(lane_d, 64) < 48)
    w_out[...] = jnp.where(keep, mm(out_t, pick), 0.0).astype(BF)

    by_hops = sorted(others, key=lambda spot: -((0, 1, 2, 1)[spot[0]] * 2 + spot[1] * 2 + spot[2] * 2 + spot[3]))

    def key_copy(i):
        m, dy, dx, dk = by_hops[i]
        group = flip(xx, dx) * 2 + flip(y, dy)
        return copy_to(
            kv_out.at[group],
            kv_in.at[(c - 2) * 2 + xx],
            k_send.at[i],
            k_recv.at[half],
            device(m, dy, dx, dk),
        )

    @pl.when(is_owner)
    def _():
        arrived = part_in.at[pl.ds(0, 15)]
        copy_to(arrived, arrived, a_send.at[0], a_recv.at[0], {"cells": c, "ctx": x}).wait_recv()
        first, second = part_in[0].astype(F32), part[c - 2]
        for s in range(1, 8):
            first = first + part_in[s].astype(F32)
            second = second + part_in[8 + s].astype(F32)
        pooled = jnp.concatenate([first, second], axis=0)
        scaled = (pooled * anchor_g[...]).astype(BF)
        inverse = lax.rsqrt(jnp.mean(pooled * pooled, axis=1, keepdims=True) + EPS)
        key_lin = mm(scaled, key_w[...]) * inverse
        out_lin = mm(scaled, w_out[...]) * inverse
        low = lax.broadcasted_iota(jnp.int32, (16, 128), 1) < HEAD_DIM
        pieces = []
        for j in range(D // 128):
            piece = key_lin[:, 128 * j : 128 * j + 128]
            square = piece * piece
            first = jnp.sum(jnp.where(low, square, 0.0), axis=1, keepdims=True)
            second = jnp.sum(jnp.where(low, 0.0, square), axis=1, keepdims=True)
            pieces.append(piece * lax.rsqrt(jnp.where(low, first, second) * (1.0 / HEAD_DIM) + EPS))
        keys = jnp.concatenate(pieces, axis=1) * key_g[...]
        coarse = out_lin.astype(BF).astype(F32)
        mixed = jnp.where(lax.rem(lax.broadcasted_iota(jnp.int32, (16, 256), 1), 64) // 16 == 1, out_lin - coarse, coarse)
        for g in range(4):
            kv_out[g] = jnp.concatenate(
                [keys[:, width * g : width * g + width], mixed[:, 64 * g : 64 * g + 64]], axis=1
            ).astype(BF)
        pl.semaphore_wait(ready, 1)
        for i in range(len(others)):
            key_copy(i).start()
        kv_in[(c - 2) * 2 + xx] = kv_out[xx * 2 + y]

    embed_block(place)
    qwin_t[...] = qwin[...].T
    gain_t[...] = jnp.broadcast_to(query_g[:, pl.ds(start, pair)], (128, pair)).T

    for i, (dy, dx) in enumerate(quad):
        p_copies[i].wait_recv()
        embed_block(flip(y, dy) * 2 + flip(xx, dx))

    rows_mine = pl.ds(pl.multiple_of(y * width, 64), width)
    qlin[...] = mm(qwin_t[rows_mine, :], emb_t[...])
    gains = gain_t[rows_mine, :][:, 0:1]

    def norm_of(h):
        piece = qlin[h * HEAD_DIM : (h + 1) * HEAD_DIM, :]
        return lax.rsqrt(jnp.mean(piece * piece, axis=0, keepdims=True) + EPS)

    for h in range(heads):
        rows = slice(h * HEAD_DIM, (h + 1) * HEAD_DIM)
        hats[rows, :] = (qlin[rows, :] * norm_of(h) * gains[rows, :]).astype(BF)
    hats[width:, :] = jnp.zeros((256 - width, hats.shape[1]), BF)

    def keys_arrive(part_of, count):
        landed = kv_in.at[pl.ds(0, count)]
        copy_to(landed, landed, k_send.at[0], k_recv.at[part_of], {"cells": c, "ctx": x}).wait_recv()

    scale = HEAD_DIM ** (-0.5)
    lane = lax.broadcasted_iota(jnp.int32, (64, 128), 1)
    queries = qlin.shape[1]

    def attend(part_of, spot):
        found = jnp.concatenate([kv_in[part_of * 4 + s].astype(F32) for s in range(4)], axis=0)
        tile0, tile1 = found[:, :128], found[:, 128:]
        lefts = [
            jnp.where(lane < HEAD_DIM, tile0, 0.0).astype(BF),
            jnp.where(lane >= HEAD_DIM, tile0, 0.0).astype(BF),
            jnp.where(lane < HEAD_DIM, tile1, 0.0).astype(BF),
        ]
        out_cols = tile1.astype(BF).T[64:96, :]
        tops, outs = [], []
        for h in range(heads):
            exponent = jnp.exp2(
                mm(lefts[h], hats[(h // 2) * 128 : (h // 2) * 128 + 128, :]) * (scale * math.log2(math.e))
            )
            probs[h, spot : spot + 64, :] = exponent
            tops.append(jnp.sum(exponent, axis=0, keepdims=True))
            both_outs = mm(out_cols, exponent.astype(BF))
            outs.append(both_outs[:16] + both_outs[16:])
        return found, tops, outs

    @pl.when(is_owner)
    def _():
        keys_arrive(half, 3)

    @pl.when(jnp.logical_not(is_owner))
    def _():
        keys_arrive(half, 4)

    near_f, near_tops, near_outs = attend(half, 0)
    keys_arrive(1 - half, 4)
    far_f, far_tops, far_outs = attend(1 - half, 64)
    out_row = lax.broadcasted_iota(jnp.int32, (16, queries), 0) // 4
    by_head = jnp.zeros((16, queries), F32)
    shares = []
    for h in range(heads):
        shares.append(1.0 / (near_tops[h] + far_tops[h]))
        by_head = jnp.where(out_row == h, (near_outs[h] + far_outs[h]) * shares[h], by_head)
    pred_part[0] = by_head[0:4] + by_head[4:8] + by_head[8:12]
    o_copies = []
    for i, (dy, dx) in enumerate(quad):
        o_copies.append(
            copy_to(pred_part.at[0], pred_part.at[1 + i], o_send.at[i], o_recv.at[i], device(0, dy, dx, 0))
        )
        o_copies[i].start()

    for i in range(3):
        pool_copy(i).wait_send()

    @pl.when(jnp.logical_not(is_owner))
    def _():
        pool_copy(3).wait_send()

    @pl.when(is_owner)
    def _():
        for i in range(len(others)):
            key_copy(i).wait_send()

    for copy in p_copies:
        copy.wait_send()
    for h in range(heads):
        probs[h] = probs[h] * shares[h]
    goals = jnp.concatenate([both_all[i, 4:8, :] for i in range(4)], axis=1)
    both_f = jnp.concatenate([near_f, far_f], axis=0)
    both_t = both_f.astype(BF).T
    tile1 = both_f[:, 128:]
    lane = lax.broadcasted_iota(jnp.int32, tile1.shape, 1)
    backs = [
        jnp.where((lane >= 64) & (lax.rem(lane, 16) // 4 == h), tile1, 0.0).astype(BF) for h in range(heads)
    ]
    for h in range(heads):
        rows = slice(h * HEAD_DIM, (h + 1) * HEAD_DIM)
        inverse = norm_of(h)
        unit_rows = qlin[rows, :] * inverse
        unit[rows, :] = unit_rows
        wide[rows, :] = (gains[rows, :] * scale) * inverse
        lean[rows, :] = (gains[rows, :] * (scale / HEAD_DIM)) * (unit_rows * inverse)
    for copy in o_copies:
        copy.wait_recv()
    predicted = pred_part[0] + pred_part[1] + pred_part[2] + pred_part[3]
    residue = predicted - goals
    coarse = residue.astype(BF).astype(F32)
    rest = residue - coarse
    none = jnp.zeros((64, queries), F32)
    split = jnp.concatenate([none] + [coarse] * 8 + [rest] * 8, axis=0).astype(BF)
    weighed = by_head * jnp.concatenate([residue] * 4, axis=0)
    for h in range(heads):
        rows = slice(h * HEAD_DIM, (h + 1) * HEAD_DIM)
        inner = jnp.sum(weighed[4 * h : 4 * h + 4], axis=0, keepdims=True)
        grad_s = (probs[h] * (mm(backs[h], split) - inner)).astype(BF)
        grad_q = mm(both_t[rows, :], grad_s)
        shared = jnp.sum(grad_q * lean[rows, :], axis=0, keepdims=True)
        glin[rows, :] = (grad_q * wide[rows, :] - unit[rows, :] * shared).astype(BF)

    deep = D // 8
    tall = deep // 2
    middle = (z == 1) | (z == 2)
    steps_of = ((1, 2, 3), (2, 1, 2), (3, 3, 1))
    places = [jnp.where(z == 1, a, jnp.where(z == 2, b, e)) for a, b, e in steps_of]
    layers = [jnp.where(z == 1, far_z(a), jnp.where(z == 2, far_z(b), far_z(e))) for a, b, e in steps_of] + [z]

    def blocks(side, steps):
        slabs = [emb_t[pl.ds(pl.multiple_of((layers[j] * 2 + side) * deep, 16), deep), :] for j in steps]
        full = lax.dot_general(
            jnp.concatenate(slabs, axis=0), glin[...], (((1,), (1,)), ((), ())), preferred_element_type=F32
        )
        packed = {}
        for i, j in enumerate(steps):
            pieces = []
            for h in range(heads):
                piece = full[deep * i : deep * i + deep, HEAD_DIM * h : HEAD_DIM * h + HEAD_DIM]
                pieces.append(jnp.concatenate([piece[:tall], piece[tall:]], axis=1))
            packed[j] = jnp.concatenate(pieces, axis=0)
        return packed

    sent_blocks = blocks(1 - k, (0, 1, 2, 3))
    for j in range(4):
        y_send[j] = sent_blocks[j].astype(BF)
    to_mate = copy_to(y_send, y_in, g_send.at[4], g_recv.at[4], device(0, 0, 0, 1))
    to_mate.start()

    def along(j):
        slot = 0 if j == 3 else places[j]
        peer = {"cells": layers[j] * 2 + k, "ctx": xx * 2 + y}
        return copy_to(z_send.at[j], z_in.at[slot], g_send.at[j], g_recv.at[slot], peer)

    kept = blocks(k, (0, 1))
    to_mate.wait_recv()
    for j in (0, 1):
        z_send[j] = (kept[j] + y_in[j].astype(F32)).astype(BF)
        along(j).start()
    kept = blocks(k, (2, 3))
    for j in (2,):
        z_send[j] = (kept[j] + y_in[j].astype(F32)).astype(BF)
        along(j).start()
    near = kept[3] + y_in[3].astype(F32)
    total[...] = near

    @pl.when(y != k)
    def _():
        z_send[3] = near.astype(BF)
        along(3).start()

    cols = pl.ds(pl.multiple_of(place * q_dev, 128), q_dev)
    for copy in o_copies:
        copy.wait_send()
    pred_part[0] = predicted
    pred_out[...] = pred_part[0, :, cols]
    to_mate.wait_send()
    for j in range(3):
        along(j).wait_send()

    @pl.when(y != k)
    def _():
        along(3).wait_send()


    def arrived(slot):
        return copy_to(z_send.at[0], z_in.at[slot], g_send.at[0], g_recv.at[slot], device(0, 0, 0, 1))

    @pl.when(y != k)
    def _():
        arrived(0).wait_recv()
        total[...] = z_in[0].astype(F32)

    summed = total[...]
    for slot in (1, 2, 3):
        arrived(slot).wait_recv()
        summed = summed + z_in[slot].astype(F32)
    for h in range(heads):
        spot = slice(h * HEAD_DIM, (h + 1) * HEAD_DIM)
        grad_out[:tall, spot] = summed[tall * h : tall * h + tall, :HEAD_DIM]
        grad_out[tall:, spot] = summed[tall * h : tall * h + tall, HEAD_DIM:]

def finish(pred_in, grad_in, pred_o, grad_o):
    pred_o[...] = pred_in[...]
    grad_o[...] = grad_in[...]

def fused_device(
    cell_feats,
    cell_types,
    cell_routes,
    positions,
    targets,
    type_weight,
    query_weight,
    key_weight,
    out_weight,
    anchor_gain,
    query_gain,
    key_gain,
):
    width = D // 4
    cells = cell_feats.shape[1]
    q_dev = positions.shape[2]
    queries = 4 * q_dev
    outs = targets.shape[1]
    deep = D // 8
    vmem = pl.BlockSpec(memory_space=pltpu.VMEM)
    dma = pltpu.SemaphoreType.DMA
    predicted, grad = pl.pallas_call(
        fused_kernel,
        out_shape=(
            pltpu.VMEM((outs, q_dev), F32),
            pltpu.VMEM((deep, width), F32),
        ),
        in_specs=[pl.BlockSpec(memory_space=pltpu.HBM)] * 12,
        out_specs=(vmem, vmem),
        scratch_shapes=[
            pltpu.VMEM((cells, cell_feats.shape[2]), BF),
            pltpu.SMEM(cell_types.shape, jnp.int32),
            pltpu.VMEM((cell_routes.shape[2], cells), jnp.int32),
            pltpu.VMEM((3, 1, q_dev), F32),
            pltpu.VMEM((outs, q_dev), F32),
            pltpu.VMEM(type_weight.shape, BF),
            pltpu.VMEM((outs, D), BF),
            pltpu.VMEM((1, D), F32),
            pltpu.VMEM((1, D), F32),
            pltpu.VMEM((1, D), F32),
            pltpu.VMEM((D, D), BF),
            pltpu.VMEM((D, 2 * width), BF),
            pltpu.VMEM((2 * width, D), BF),
            pltpu.VMEM((2 * width, 128), F32),
            pltpu.VMEM((cells, D), BF),
            pltpu.VMEM((4, 8, D), F32),
            pltpu.VMEM((4, 8, D), BF),
            pltpu.VMEM((16, 8, D), BF),
            pltpu.VMEM((D, 256), BF),
            pltpu.VMEM((4, 16, 256), BF),
            pltpu.VMEM((8, 16, 256), BF),
            pltpu.VMEM((4, 8, q_dev), F32),
            pltpu.VMEM((4, outs, queries), F32),
            pltpu.VMEM((D, queries), BF),
            pltpu.VMEM((width, queries), F32),
            pltpu.VMEM((256, queries), BF),
            pltpu.VMEM((width, queries), F32),
            pltpu.VMEM((width, queries), F32),
            pltpu.VMEM((width, queries), F32),
            pltpu.VMEM((width // HEAD_DIM, 128, queries), F32),
            pltpu.VMEM((width, queries), BF),
            pltpu.VMEM((4, 3 * deep // 2, 128), BF),
            pltpu.VMEM((4, 3 * deep // 2, 128), BF),
            pltpu.VMEM((4, 3 * deep // 2, 128), BF),
            pltpu.VMEM((4, 3 * deep // 2, 128), BF),
            pltpu.VMEM((3 * deep // 2, 128), F32),
            dma((12,)),
            dma((4,)),
            dma((1,)),
            dma((3,)),
            dma((3,)),
            dma((31,)),
            dma((2,)),
            dma((3,)),
            dma((3,)),
            dma((5,)),
            dma((5,)),
            pltpu.SemaphoreType.REGULAR,
        ],
        compiler_params=pltpu.CompilerParams(
            collective_id=0, has_side_effects=True, vmem_limit_bytes=64 * 1024 * 1024 - 256 * 1024
        ),
    )(
        cell_feats[0],
        cell_types,
        cell_routes[0].T,
        positions[0].reshape(3, 1, q_dev),
        targets[0],
        type_weight,
        query_weight,
        key_weight,
        out_weight.T,
        anchor_gain,
        query_gain,
        key_gain,
    )
    predicted, grad = pl.pallas_call(
        finish,
        out_shape=(jax.ShapeDtypeStruct((outs, q_dev), F32), jax.ShapeDtypeStruct((deep, width), F32)),
        in_specs=[vmem, vmem],
        out_specs=(vmem, vmem),
        compiler_params=pltpu.CompilerParams(vmem_limit_bytes=1024 * 1024),
    )(predicted, grad)
    return (predicted[None], grad)


def solution(mesh):
    in_specs = (
        P(("groups", "dp"), ("cells", "ctx"), None),
        P(("groups", "dp"), ("cells", "ctx")),
        P(("groups", "dp"), ("cells", "ctx"), None),
        P(("groups", "dp"), None, ("cells", "ctx")),
        P(("groups", "dp"), None, ("cells", "ctx")),
        P(),
        P(),
        P(),
        P(),
        P(),
        P(),
        P(),
    )
    out_specs = (P(("groups", "dp"), None, ("cells", "ctx")), P(("groups", "cells"), ("ctx", "dp")))
    sizes = mesh.shape
    fits = sizes["groups"] == 1 and sizes["dp"] == 1 and sizes["ctx"] == 4 and sizes["cells"] == 8
    body = fused_device if fits else general_device
    return jax.shard_map(
        body, mesh=mesh, in_specs=in_specs, out_specs=out_specs, check_vma=False
    )
```
